32 devices in a mesh: shard: 4 (over z), ctx: 4 (over x, core), tp: 2 (over y).
Axes of the slice: x: 2, y: 2, z: 4, core: 2. Of those that a mesh axis runs over, the one named last changes fastest.
Arguments:
- inputs: bfloat16 [8192, 2048], P(('shard', 'ctx')), may hold values from -6 to 6
- segments: int32 [8192], P(('shard', 'ctx')), may hold values from 0 to 11, as said below
- routes: int32 [8192, 6], P(('shard', 'ctx')), may hold values from 0 to 15, all different within a row; in each aligned block of 512 rows (0 to 511, 512 to 1023, ...) at most 288 rows name the same one
- gate_share: float32 [8192, 6], P(('shard', 'ctx')), may hold values from 0.16 to 0.64
- cotangent: bfloat16 [8192, 2048], P(('shard', 'ctx')), may hold values from -6 to 6
- attn_gain: bfloat16 [2048], P(('shard', 'ctx')), may hold values from 0.5 to 1.5
- kv_gain: bfloat16 [512], P(('shard', 'ctx')), may hold values from 0.5 to 1.5
- ffn_gain: bfloat16 [2048], P(('shard', 'ctx')), may hold values from 0.5 to 1.5
- w_query: bfloat16 [2048, 3072], P(('shard', 'ctx'), 'tp'), may hold values from -0.125 to 0.125
- w_latent: bfloat16 [2048, 576], P(('shard', 'ctx')), may hold values from -0.125 to 0.125
- w_expand: bfloat16 [512, 4096], P(('shard', 'ctx'), 'tp'), may hold values from -0.25 to 0.25
- w_output: bfloat16 [2048, 2048], P('tp', ('shard', 'ctx')), may hold values from -1.5 to 1.5
- w_shared_gate: bfloat16 [2048, 2816], P(('shard', 'ctx'), 'tp'), may hold values from -0.125 to 0.125
- w_shared_up: bfloat16 [2048, 2816], P(('shard', 'ctx'), 'tp'), may hold values from -0.125 to 0.125
- w_shared_down: bfloat16 [2816, 2048], P('tp', ('shard', 'ctx')), may hold values from -0.109375 to 0.109375
- expert_gate: bfloat16 [16, 2048, 1408], P(('shard', 'ctx'), None, 'tp'), may hold values from -0.125 to 0.125
- expert_up: bfloat16 [16, 2048, 1408], P(('shard', 'ctx'), None, 'tp'), may hold values from -0.125 to 0.125
- expert_down: bfloat16 [16, 1408, 2048], P(('shard', 'ctx'), 'tp'), may hold values from -0.625 to 0.625
Outputs:
- result: bfloat16 [8192, 2048], P(('shard', 'ctx'))
- grad_inputs: float32 [8192, 2048], P(('shard', 'ctx'))
- grad_attn_gain: float32 [2048], P(('shard', 'ctx'))
- grad_kv_gain: float32 [512], P(('shard', 'ctx'))
- grad_ffn_gain: float32 [2048], P(('shard', 'ctx'))
- grad_w_query: float32 [2048, 3072], P(('shard', 'ctx'), 'tp')
- grad_w_latent: float32 [2048, 576], P(('shard', 'ctx'))
- grad_w_expand: float32 [512, 4096], P(('shard', 'ctx'), 'tp')
- grad_w_output: float32 [2048, 2048], P('tp', ('shard', 'ctx'))
- grad_w_shared_gate: float32 [2048, 2816], P(('shard', 'ctx'), 'tp')
- grad_w_shared_up: float32 [2048, 2816], P(('shard', 'ctx'), 'tp')
- grad_w_shared_down: float32 [2816, 2048], P('tp', ('shard', 'ctx'))
- grad_expert_gate: float32 [16, 2048, 1408], P(('shard', 'ctx'), None, 'tp')
- grad_expert_up: float32 [16, 2048, 1408], P(('shard', 'ctx'), None, 'tp')
- grad_expert_down: float32 [16, 1408, 2048], P(('shard', 'ctx'), 'tp')
The draws below stay inside these ranges and needn't reach their ends.
Inputs may be any that keep to these rules, and one draw needn't show every extreme that they name: `segments`: never falling along the tokens; tokens of different sequences (runs of 2048) have different numbers. `routes`: in each aligned block of 512 rows (the tokens of one index of shard and ctx) no expert is named by more than 288 rows, a bound that some block reaches; the 6 experts of a row differ.
All inputs are finite; a program needn't handle non-finite values.
Results may differ from the reference program's by a relative error of at most 0.019.
Values may be sent and summed in bfloat16 or wider, within the bound.
A program may use at most 448 MiB of HBM per device.

```python
import math
from functools import partial
import jax
import jax.numpy as jnp
import numpy as np
from jax import lax

D = 2048
H = 16
NOPE = 128
ROPE = 64
V = 128
R = 512
FF = 1408
SF = 2816
TOP = 6
TOK_DEV = 512
EXPERTS = 16
LENGTH = 2048
TOKENS = 8192
CAP = 288
N_TP = 2


def draw_segments(key, part):
    key = jax.random.fold_in(key, 7)
    sequences = TOKENS // LENGTH
    first_key, last_key = jax.random.split(key)
    first_cut = jax.random.randint(first_key, (sequences, 1), 1, TOK_DEV // 2 + 1)
    last_cut = LENGTH - jax.random.randint(last_key, (sequences, 1), 1, TOK_DEV // 2 + 1)
    places = jnp.arange(LENGTH, dtype=jnp.int32)[None, :]
    numbers = 3 * jnp.arange(sequences, dtype=jnp.int32)[:, None] + (places >= first_cut).astype(jnp.int32) + (places >= last_cut).astype(jnp.int32)
    return numbers.reshape(-1).astype(jnp.int32)


def steps_of(key, shape, pieces, smallest, largest):
    def one(axis_at, shards_of):
        heights = jax.random.uniform(jax.random.fold_in(jax.random.fold_in(key, 6), axis_at), (shards_of,), jnp.float32, smallest / len(pieces), largest / len(pieces))
        return jnp.repeat(jnp.exp(heights), shape[axis_at] // shards_of).reshape((-1,) + (1,) * (len(shape) - axis_at - 1))

    factor_of = one(*pieces[0])
    for cut in pieces[1:]:
        factor_of = factor_of * one(*cut)
    return factor_of


def routed_block(own_key, own, number, rows, count, top, most, lean):
    order = jax.random.permutation(own_key, count)
    crowded, ordinary = load_shares(count, rows * top, most, lean, True), load_shares(count, rows * top, most, lean, False)
    places = jnp.arange(count)

    def named(tallies, turn):
        used = int((tallies > 0).sum())
        fixed = max(1, used // 4)
        moved = fixed + (places - fixed + turn * (used - fixed)) % max(1, count - fixed)
        return jnp.zeros((count,), jnp.int32).at[order[jnp.where(places < fixed, places, moved)]].set(jnp.asarray(tallies, jnp.int32))

    tallies = jnp.where(number % 4 == 0, named(crowded, number // 4), named(ordinary, number - number // 4 - 1))
    mixed = jax.random.permutation(jax.random.fold_in(own, 3), count)
    donor, receiver = mixed[0:count // 2 * 2:2], mixed[1:count // 2 * 2:2]
    margin = jnp.minimum(tallies[donor] - 1, most - tallies[receiver]) // 2
    margin = jnp.where((donor == order[0]) | (receiver == order[0]) | (tallies[receiver] == 0), 0, jnp.maximum(margin, 0))
    moved = jax.random.randint(jax.random.fold_in(own, 4), (count // 2,), 0, 1 << 20) % (margin + 1)
    tallies = tallies.at[donor].add(-moved).at[receiver].add(moved)
    labels = jnp.searchsorted(jnp.cumsum(tallies), jnp.arange(rows * top), side="right").astype(jnp.int32)
    table = labels.reshape(top, rows).T
    table = table[jax.random.permutation(jax.random.fold_in(own, 1), rows)]
    turn = jax.random.randint(jax.random.fold_in(own, 2), (rows, 1), 0, top)
    return jnp.take_along_axis(table, (jnp.arange(top)[None, :] + turn) % top, axis=1)


def load_shares(number_of, total, reach, lean, full):
    loads = [(1 << 20) // math.isqrt(rank ** lean) + 1 for rank in range(1, number_of + 1)]
    largest = reach if full else min(reach, max(-(-total // number_of), total * loads[0] // sum(loads)))
    least = 1 if total - largest >= number_of - 1 else 0
    holding, surplus = [largest] + [least] * (number_of - 1), total - largest - least * (number_of - 1)
    while surplus > 0:
        movable = [i for i in range(1, number_of) if holding[i] < largest] or [i for i in range(1, number_of) if holding[i] < reach]
        mass, left = sum([loads[i] for i in movable]), surplus
        for i in movable:
            extra = min(reach - holding[i], max(1, left * loads[i] // mass), surplus)
            holding[i] = holding[i] + extra
            surplus = surplus - extra
    return np.array(holding)


def gaussian(key, dims, width, most, cuts=(), kind=jnp.bfloat16):
    level = steps_of(key, dims, cuts, -0.22, 0.18) if cuts else 1.0
    entries = jax.random.normal(key, dims, jnp.float32) * width * level
    return jnp.minimum(jnp.maximum(entries, -most), most).astype(kind)


def setup_inputs(seed: int = 0) -> dict:
    arg_keys = jax.random.split(jax.random.key(seed), 19)
    inputs = gaussian(arg_keys[0], (TOKENS, D), 1.0, 6.0, ((0, 16),))
    segments = draw_segments(jax.random.fold_in(arg_keys[18], 71), 0)
    routes_keys = jax.random.split(jax.random.fold_in(arg_keys[2], 1), TOKENS // TOK_DEV)
    routes_turns = jax.random.permutation(jax.random.fold_in(arg_keys[2], 3), TOKENS // TOK_DEV)
    routes = jax.vmap(lambda own, number: routed_block(jax.random.fold_in(arg_keys[2], 2), own, number, TOK_DEV, EXPERTS, TOP, CAP, 1))(routes_keys, routes_turns).reshape((TOKENS, TOP))
    gate_share = jnp.clip(jnp.exp(math.log(0.64) - 1.3862944 * jax.random.uniform(arg_keys[3], (TOKENS, TOP), jnp.float32) ** steps_of(arg_keys[3], (TOKENS, TOP), ((0, 16),), -0.2, 0.2)), 0.16, 0.64)
    cotangent = gaussian(arg_keys[4], (TOKENS, D), 1.0, 6.0, ((0, 16),))
    attn_gain = jnp.clip(1.0 + 0.1 * jax.random.normal(arg_keys[5], (D,), jnp.float32), 0.5, 1.5).astype(jnp.bfloat16)
    kv_gain = jnp.clip(1.0 + 0.1 * jax.random.normal(arg_keys[6], (R,), jnp.float32), 0.5, 1.5).astype(jnp.bfloat16)
    ffn_gain = jnp.clip(1.0 + 0.1 * jax.random.normal(arg_keys[7], (D,), jnp.float32), 0.5, 1.5).astype(jnp.bfloat16)
    w_query = gaussian(arg_keys[8], (D, H * (NOPE + ROPE)), D ** -0.5, 0.125, ((0, 16), (1, 2)))
    w_latent = gaussian(arg_keys[9], (D, R + ROPE), D ** -0.5, 0.125, ((0, 16),))
    w_expand = gaussian(arg_keys[10], (R, H * (NOPE + V)), R ** -0.5, 0.25, ((0, 16), (1, 2)))
    w_output = gaussian(arg_keys[11], (H * V, D), (H * V // 128) ** -0.5, 1.5, ((0, 2), (1, 16)))
    w_shared_gate = gaussian(arg_keys[12], (D, SF), D ** -0.5, 0.125, ((0, 16), (1, 2)))
    w_shared_up = gaussian(arg_keys[13], (D, SF), D ** -0.5, 0.125, ((0, 16), (1, 2)))
    w_shared_down = gaussian(arg_keys[14], (SF, D), SF ** -0.5, 0.109375, ((0, 2), (1, 16)))
    expert_gate = gaussian(arg_keys[15], (EXPERTS, D, FF), D ** -0.5, 0.125, ((0, 16), (2, 2)))
    expert_up = gaussian(arg_keys[16], (EXPERTS, D, FF), D ** -0.5, 0.125, ((0, 16), (2, 2)))
    expert_down = gaussian(arg_keys[17], (EXPERTS, FF, D), (FF // 16) ** -0.5, 0.625, ((0, 16), (1, 2)))
    return {"inputs": inputs, "segments": segments, "routes": routes, "gate_share": gate_share, "cotangent": cotangent, "attn_gain": attn_gain, "kv_gain": kv_gain, "ffn_gain": ffn_gain, "w_query": w_query, "w_latent": w_latent, "w_expand": w_expand, "w_output": w_output, "w_shared_gate": w_shared_gate, "w_shared_up": w_shared_up, "w_shared_down": w_shared_down, "expert_gate": expert_gate, "expert_up": expert_up, "expert_down": expert_down}


EPS = 1e-06
HIGH = lax.Precision.HIGHEST

@jax.custom_vjp
def low(v):
    return lax.optimization_barrier(v.astype(jnp.bfloat16)).astype(jnp.float32)

@jax.custom_vjp
def low_back(v):
    return v

def low_keep(v):
    return (low(v), None)

def low_pass(kept, grad):
    return (grad,)

def back_keep(v):
    return (v, None)

def back_low(kept, grad):
    return (low(grad),)
low.defvjp(low_keep, low_pass)
low_back.defvjp(back_keep, back_low)

def matmul(left, right):
    return jnp.dot(left, right, precision=HIGH, preferred_element_type=jnp.float32)

def rms_norm(values, gain):
    return values * lax.rsqrt(lax.optimization_barrier(jnp.mean(values * values, -1, keepdims=True)) + EPS) * gain

def rotate(values, sines, cosines):
    half_width = values.shape[-1] // 2
    first = values[..., :half_width]
    second = values[..., half_width:]
    return jnp.concatenate([first * cosines - second * sines, second * cosines + first * sines], -1)

def angles(positions):
    half_width = ROPE // 2
    freq_table = 10000.0 ** (-jnp.arange(half_width, dtype=jnp.float32) / half_width)
    turned = positions.astype(jnp.float32)[:, None] * freq_table[None, :]
    return (jnp.sin(turned), jnp.cos(turned))

def attend(query_seq, kv_seq, rope_seq, segment_seq):
    scale = (NOPE + ROPE) ** (-0.5)
    kv_heads = kv_seq.reshape(LENGTH, H, NOPE + V)
    key_nope = kv_heads[..., :NOPE]
    values = kv_heads[..., NOPE:]
    raw = jnp.einsum('qhd,khd->hqk', query_seq[..., :NOPE], key_nope, precision=HIGH)
    raw = raw + jnp.einsum('qhd,kd->hqk', query_seq[..., NOPE:], rope_seq, precision=HIGH)
    scores = low_back(scale * raw)
    places = jnp.arange(LENGTH, dtype=jnp.int32)
    visible = (segment_seq[None, :] == segment_seq[:, None]) & (places[None, :] <= places[:, None])
    masked = jnp.where(visible[None], scores, -1e+30)
    row_peak = lax.optimization_barrier(jnp.max(masked, -1, keepdims=True))
    exponent = jnp.exp(masked - row_peak)
    attention_probs = exponent / lax.optimization_barrier(jnp.sum(exponent, -1, keepdims=True))
    probs_low = low(attention_probs)
    attended = jnp.einsum('hqk,khd->qhd', probs_low, values, precision=HIGH)
    return low(low_back(attended)).reshape(LENGTH, H * V)

def forward_pass(segments, slot_index, token_rows, shares, hidden_in, attn_gain, kv_gain, ffn_gain, w_query, w_latent, w_expand, w_output, w_shared_gate, w_shared_up, w_shared_down, expert_gate, expert_up, expert_down):
    normed_one = rms_norm(hidden_in, attn_gain)
    attn_low = low(normed_one)
    query_raw = low_back(matmul(attn_low, w_query)).reshape(TOKENS, H, NOPE + ROPE)
    positions = jnp.arange(TOKENS, dtype=jnp.int32) % LENGTH
    sines, cosines = angles(positions)
    query_rot = jnp.concatenate([query_raw[..., :NOPE], rotate(query_raw[..., NOPE:], sines[:, None, :], cosines[:, None, :])], -1)
    query_low = low(query_rot)
    latent = low_back(matmul(attn_low, w_latent))
    compressed = latent[:, :R]
    key_rope = latent[:, R:]
    compressed_low = low(rms_norm(compressed, kv_gain))
    key_rope_low = low(rotate(key_rope, sines, cosines))
    keys_values = low(low_back(matmul(compressed_low, w_expand)))
    sequences = TOKENS // LENGTH
    core = jax.checkpoint(attend)

    def per_sequence(carry, item):
        return (carry, core(item[0], item[1], item[2], item[3]))
    items = (query_low.reshape(sequences, LENGTH, H, NOPE + ROPE), keys_values.reshape(sequences, LENGTH, H * (NOPE + V)), key_rope_low.reshape(sequences, LENGTH, ROPE), segments.reshape(sequences, LENGTH))
    _, attended = lax.scan(per_sequence, jnp.zeros((), jnp.float32), items)
    attended = attended.reshape(TOKENS, H * V)
    middle = hidden_in + low_back(matmul(attended, w_output))
    ffn_low = low(rms_norm(middle, ffn_gain))
    shared_gate = low_back(matmul(ffn_low, w_shared_gate))
    shared_up = low_back(matmul(ffn_low, w_shared_up))
    shared_hidden = low(jax.nn.silu(shared_gate) * shared_up)
    shared_out = matmul(shared_hidden, w_shared_down)
    padded = jnp.concatenate([ffn_low, jnp.zeros((1, D), jnp.float32)], 0)
    group_width = FF // N_TP

    def expert_rows(item):
        gate_weight, up_weight, down_weight, rows_index = item
        rows = padded[rows_index]
        total = jnp.zeros((rows.shape[0], D), jnp.float32)
        for group_index in range(N_TP):
            lower = group_index * group_width
            upper = lower + group_width
            rows_grad = low_back(rows)
            gate_pre = low_back(matmul(rows_grad, gate_weight[:, lower:upper]))
            up_pre = low_back(matmul(rows_grad, up_weight[:, lower:upper]))
            hidden_low = low(jax.nn.silu(gate_pre) * up_pre)
            total = total + low(low_back(matmul(hidden_low, down_weight[lower:upper])))
        return total
    expert_out = lax.map(jax.checkpoint(expert_rows), (expert_gate, expert_up, expert_down, token_rows))
    picked = expert_out.reshape(-1, D)[slot_index].reshape(TOKENS, TOP, D)
    combined = lax.optimization_barrier(jnp.sum(shares[:, :, None] * picked, 1))
    return middle + shared_out + combined

def reference(inputs, segments, routes, gate_share, cotangent, attn_gain, kv_gain, ffn_gain, w_query, w_latent, w_expand, w_output, w_shared_gate, w_shared_up, w_shared_down, expert_gate, expert_up, expert_down):
    flat_routes = routes.reshape(-1).astype(jnp.int32)
    total_slots = CAP * (TOKENS // TOK_DEV)
    onehot_rows = (flat_routes[:, None] == jnp.arange(EXPERTS, dtype=jnp.int32)[None, :]).astype(jnp.int32)
    ranks = lax.optimization_barrier(jnp.sum(jnp.cumsum(onehot_rows, 0) * onehot_rows, 1)) - 1
    slot_index = (flat_routes * total_slots + ranks).astype(jnp.int32)
    token_ids = jnp.arange(TOKENS * TOP, dtype=jnp.int32) // TOP
    token_rows = jnp.full((EXPERTS * total_slots,), TOKENS, jnp.int32).at[slot_index].set(token_ids).reshape(EXPERTS, total_slots)
    shares = gate_share.astype(jnp.float32)
    floats = tuple((item.astype(jnp.float32) for item in (inputs, attn_gain, kv_gain, ffn_gain, w_query, w_latent, w_expand, w_output, w_shared_gate, w_shared_up, w_shared_down, expert_gate, expert_up, expert_down)))
    output, backward = jax.vjp(partial(forward_pass, segments, slot_index, token_rows, shares), *floats)
    grads = backward(cotangent.astype(jnp.float32))
    return (output.astype(jnp.bfloat16), grads[0], grads[1], grads[2], grads[3], grads[4], grads[5], grads[6], grads[7], grads[8], grads[9], grads[10], grads[11], grads[12], grads[13])
```

```python
import functools

import jax
import jax.numpy as jnp
from jax import lax
from jax.experimental import pallas as pl
from jax.experimental.pallas import tpu as pltpu
from jax.sharding import PartitionSpec as P

NOPE = 128
ROPE = 64
V = 128
R = 512
HEAD = 256
EPS = 1e-06
GROUP = ("shard", "ctx")
MESH = pl.DeviceIdType.MESH
BF = jnp.bfloat16
F32 = jnp.float32
MIB = 1 << 20


def norm_forward(values, gain):
    inverse = lax.rsqrt(jnp.mean(values * values, -1, keepdims=True) + EPS)
    return (values * inverse * gain, inverse)


def norm_backward(values, inverse, gain, upstream):
    scaled = upstream * gain
    gain_grad = jnp.sum(upstream * values * inverse, 0)
    value_grad = inverse * scaled - values * inverse**3 * jnp.mean(
        scaled * values, -1, keepdims=True
    )
    return (value_grad, gain_grad)


def rotate(values, sines, cosines):
    half_width = values.shape[-1] // 2
    first = values[..., :half_width]
    second = values[..., half_width:]
    return jnp.concatenate([first * cosines - second * sines, second * cosines + first * sines], -1)


def angles(positions):
    half_width = ROPE // 2
    freq_table = 10000.0 ** (-jnp.arange(half_width, dtype=F32) / half_width)
    turned = positions.astype(F32)[:, None] * freq_table[None, :]
    return (jnp.sin(turned), jnp.cos(turned))


def mm(a, b):
    return jnp.dot(a, b, preferred_element_type=F32)


def mm_nt(a, b):
    return lax.dot_general(a, b, (((1,), (1,)), ((), ())), preferred_element_type=F32)


def mm_tn(a, b):
    return lax.dot_general(a, b, (((0,), (0,)), ((), ())), preferred_element_type=F32)


def ring_place(nz):
    z = lax.axis_index("shard")
    c = lax.axis_index("ctx")
    x, core = c // 2, c % 2
    return jnp.where(x == 0, z, 2 * nz - 1 - z), x, core


def ring_at(nz, p):
    p = lax.rem(p + 4 * nz, 2 * nz)
    return jnp.where(p < nz, p, 2 * nz - 1 - p), p // nz


def ring_lanes(shapes, pieces):
    lanes = []
    for index, (rows, _) in enumerate(shapes):
        first = -(-rows // 32) * 16
        ways = []
        for towards, start, size in ((1, 0, first), (-1, first, rows - first)):
            units = size // 16
            parts = min(pieces, units)
            way, at = [], start
            for part in range(parts):
                here = 16 * (units // parts + (1 if part < units % parts else 0))
                way.append((index, towards, at, here))
                at += here
            ways.append(way)
        for part in range(pieces):
            lanes += [way[part] for way in ways if part < len(way)]
    return lanes


def greet(devices):
    barrier = pltpu.get_barrier_semaphore()
    for device in devices:
        pl.semaphore_signal(barrier, inc=1, device_id=device, device_id_type=MESH)
    pl.semaphore_wait(barrier, len(devices))


def ring_neighbours(nz):
    me, x, core = ring_place(nz)
    zr, xr = ring_at(nz, me + 1)
    zl, xl = ring_at(nz, me - 1)
    right = {"shard": zr, "ctx": xr * 2 + core}
    left = {"shard": zl, "ctx": xl * 2 + core}
    sibling = {"ctx": x * 2 + 1 - core}
    return me, core, right, left, sibling


def link_cost(size, rate):
    return pl.CostEstimate(flops=int(size / rate * 9e14), bytes_accessed=2 * size, transcendentals=0)


def remote(src, dst, send, recv, device):
    return pltpu.make_async_remote_copy(
        src_ref=src, dst_ref=dst, send_sem=send, recv_sem=recv, device_id=device, device_id_type=MESH
    )


def ring_semaphores(nz, count, lanes):
    return (
        [pltpu.SemaphoreType.DMA((count,))]
        + [pltpu.SemaphoreType.DMA((len(lanes), 2 * nz - 1))] * 2
        + [pltpu.SemaphoreType.DMA((len(lanes), 2 * nz))] * 2
    )


def ring_steps(nz, lanes, ins, outs, me, core, right, left, sibling, own_sem, send, recv, sib_send, sib_recv):
    steps = 2 * nz

    def block(place, which):
        z, x = ring_at(nz, place)
        return z * 4 + x * 2 + which

    own = block(me, core)
    local = [pltpu.make_async_copy(a, b.at[own], own_sem.at[i]) for i, (a, b) in enumerate(zip(ins, outs))]
    flying = []
    last = {}
    for step in range(steps):
        for lane, (i, towards, row, rows) in enumerate(lanes):
            here = block(me - towards * step, core)
            piece = pl.ds(row, rows)
            if step > 0:
                last[lane].wait_recv()
            src = ins[i].at[piece] if step == 0 else outs[i].at[here, piece]
            dst = outs[i].at[here, piece]
            if step < steps - 1:
                copy = remote(
                    src, dst, send.at[lane, step], recv.at[lane, step], right if towards > 0 else left
                )
                copy.start()
                last[lane] = copy
                flying.append((copy, False))
            copy = remote(src, dst, sib_send.at[lane, step], sib_recv.at[lane, step], sibling)
            copy.start()
            flying.append((copy, True))
        if step == 0:
            for copy in local:
                copy.start()
        yield
    for copy in local:
        copy.wait()
    for copy, both in flying:
        copy.wait_send()
        if both:
            copy.wait_recv()


def trade_copies(nz, x_ref, o_ref, own_sem, send, recv):
    devices = 4 * nz
    me = lax.axis_index("shard") * 4 + lax.axis_index("ctx")
    local = pltpu.make_async_copy(x_ref.at[me], o_ref.at[me], own_sem)
    copies = []
    for shift in range(1, devices):
        there = lax.rem(me + shift, devices)
        device = {"shard": there // 4, "ctx": lax.rem(there, 4)}
        copies.append(remote(x_ref.at[there], o_ref.at[me], send.at[shift - 1], recv.at[shift - 1], device))
    return local, copies


def trade_partners(nz):
    devices = 4 * nz
    me = lax.axis_index("shard") * 4 + lax.axis_index("ctx")
    there = [lax.rem(me + shift, devices) for shift in range(1, devices)]
    return tuple({"shard": t // 4, "ctx": lax.rem(t, 4)} for t in there)


def trade_semaphores(nz):
    return [pltpu.SemaphoreType.DMA] + [pltpu.SemaphoreType.DMA((4 * nz - 1,))] * 2


def gather_kernel(nz, count, swaps, lanes, *refs):
    total = count + swaps
    ins, outs = refs[:total], refs[total : 2 * total]
    *ring, swap_send, swap_recv = refs[2 * total :]
    me, core, right, left, sibling = ring_neighbours(nz)
    across = {"tp": 1 - lax.axis_index("tp")}
    greet((right, left, sibling) + ((across,) if swaps else ()))
    swapped = [
        remote(ins[count + i], outs[count + i], swap_send.at[i], swap_recv.at[i], across) for i in range(swaps)
    ]
    for step, _ in enumerate(ring_steps(nz, lanes, ins[:count], outs[:count], me, core, right, left, sibling, *ring)):
        if step == 0:
            for copy in swapped:
                copy.start()
    for copy in swapped:
        copy.wait()


def ring_gather(arrays, collective_id, pieces=2, swaps=()):
    nz = lax.axis_size("shard")
    lanes = ring_lanes([a.shape for a in arrays], pieces)
    given = [*arrays, *swaps]
    count, total = len(arrays), len(given)
    return pl.pallas_call(
        functools.partial(gather_kernel, nz, count, len(swaps), lanes),
        out_shape=[jax.ShapeDtypeStruct((4 * nz,) + a.shape, a.dtype) for a in arrays]
        + [jax.ShapeDtypeStruct(a.shape, a.dtype) for a in swaps],
        in_specs=[pl.BlockSpec(memory_space=pl.ANY)] * total,
        out_specs=[pl.BlockSpec(memory_space=pl.ANY)] * total,
        scratch_shapes=ring_semaphores(nz, count, lanes)
        + [pltpu.SemaphoreType.DMA((max(len(swaps), 1),))] * 2,
        compiler_params=pltpu.CompilerParams(collective_id=collective_id, has_side_effects=True),
        cost_estimate=link_cost(4 * nz * sum(a.size * a.dtype.itemsize for a in arrays), 190e9),
        name="ring_gather",
    )(*given)


def gather_shared_kernel(
    nz, swaps, lanes, row_ref, cot_ref, gate_ref, up_ref, down_ref, *refs
):
    swap_in, refs = refs[:swaps], refs[swaps:]
    all_ref, out_ref, gin_ref, dg_ref, du_ref, dd_ref, *refs = refs
    swap_out, refs = refs[:swaps], refs[swaps:]
    xs, cs, outs, gins, own_sem, send, recv, sib_send, sib_recv, loads, stores, swap_sem = refs
    me, core, right, left, sibling = ring_neighbours(nz)
    across = {"tp": 1 - lax.axis_index("tp")}
    greet((right, left, sibling) + ((across,) if swaps else ()))
    steps = 2 * nz
    first = sum(rows for _, towards, _, rows in lanes if towards > 0)
    total = row_ref.shape[0]
    halves = ((1, 0, first), (-1, first, total - first))

    def block(place, which):
        z, x = ring_at(nz, place)
        return z * 4 + x * 2 + which

    def ring_copy(lane, step):
        _, towards, row, rows = lanes[lane]
        ref = all_ref.at[block(me - towards * step, core), pl.ds(row, rows)]
        return remote(ref, ref, send.at[lane, step], recv.at[lane, step], right if towards > 0 else left)

    def sibling_copy(lane, step, which):
        _, towards, row, rows = lanes[lane]
        ref = all_ref.at[block(me - towards * step, which), pl.ds(row, rows)]
        return remote(ref, ref, sib_send.at[lane, step], sib_recv.at[lane, step], sibling)

    def pieces_of(slot, step):
        which = core if slot == 0 else 1 - core
        return [(k, block(me - towards * step, which), pl.ds(row, rows)) for k, (towards, row, rows) in enumerate(halves)]

    def taken(slot, step):
        return [
            pltpu.make_async_copy(src.at[here, piece], dst.at[slot, piece], loads.at[slot, k, j])
            for k, here, piece in pieces_of(slot, step)
            for j, (src, dst) in enumerate(((all_ref, xs), (cot_ref, cs)))
        ]

    def given(slot, step):
        return [
            pltpu.make_async_copy(src.at[slot, piece], dst.at[here, piece], stores.at[slot, k, j])
            for k, here, piece in pieces_of(slot, step)
            for j, (src, dst) in enumerate(((outs, out_ref), (gins, gin_ref)))
        ]

    def work(slot, step, first_time):
        for copy in taken(slot, step):
            copy.wait()

        @pl.when(jnp.logical_not(first_time))
        def _():
            for copy in given(slot, jnp.maximum(step - 1, 0)):
                copy.wait()

        x, c = xs[slot], cs[slot]
        a = mm_nt(x, gate_ref[...])
        b = mm_nt(x, up_ref[...])
        sig = jax.nn.sigmoid(a)
        act = a * sig
        hidden = (act * b).astype(BF)
        grad_hidden = mm_nt(c, down_ref[...])
        grad_gate = (grad_hidden * b * (sig * (1.0 + a * (1.0 - sig)))).astype(BF)
        grad_up = (grad_hidden * act).astype(BF)
        outs[slot] = mm(hidden, down_ref[...]).astype(BF)
        gins[slot] = (mm(grad_gate, gate_ref[...]) + mm(grad_up, up_ref[...])).astype(BF)
        dg_ref[...] += mm_tn(grad_gate, x)
        du_ref[...] += mm_tn(grad_up, x)
        dd_ref[...] += mm_tn(hidden, c)
        for copy in given(slot, step):
            copy.start()

    local = pltpu.make_async_copy(row_ref, all_ref.at[block(me, core)], own_sem)
    local.start()
    swapped = [
        remote(swap_in[i], swap_out[i], swap_sem.at[0, i], swap_sem.at[1, i], across) for i in range(swaps)
    ]
    for copy in swapped:
        copy.start()
    dg_ref[...] = jnp.zeros_like(dg_ref)
    du_ref[...] = jnp.zeros_like(du_ref)
    dd_ref[...] = jnp.zeros_like(dd_ref)
    local.wait()

    def one_step(step, carry):
        for lane in range(len(lanes)):

            @pl.when(jnp.logical_and(step > 0, step < steps))
            def _(lane=lane):
                ring_copy(lane, jnp.maximum(step - 1, 0)).wait_recv()

            @pl.when(step < steps - 1)
            def _(lane=lane):
                ring_copy(lane, step).start()

            @pl.when(step < steps)
            def _(lane=lane):
                sibling_copy(lane, step, core).start()

        @pl.when(step < steps)
        def _():
            for copy in taken(0, step):
                copy.start()

        @pl.when(step > 0)
        def _():
            for lane in range(len(lanes)):
                sibling_copy(lane, step - 1, 1 - core).wait_recv()
            for copy in taken(1, step - 1):
                copy.start()

        @pl.when(step < steps)
        def _():
            work(0, step, step == 0)

        @pl.when(step > 0)
        def _():
            work(1, step - 1, step == 1)

        return carry

    lax.fori_loop(0, steps + 1, one_step, 0)
    for slot in range(2):
        for copy in given(slot, steps - 1):
            copy.wait()
    for lane in range(len(lanes)):
        for step in range(steps):
            if step < steps - 1:
                ring_copy(lane, step).wait_send()
            sibling_copy(lane, step, core).wait_send()
    for copy in swapped:
        copy.wait()


def gather_shared(rows, cot, shared, collective_id, swaps=(), pieces=2):
    nz = lax.axis_size("shard")
    lanes = ring_lanes([rows.shape], pieces)
    tokens, width = rows.shape
    hidden = shared[0].shape[0]
    blocks = jax.ShapeDtypeStruct((4 * nz, tokens, width), BF)
    anywhere, vmem = pl.BlockSpec(memory_space=pl.ANY), pl.BlockSpec(memory_space=pltpu.VMEM)
    return pl.pallas_call(
        functools.partial(gather_shared_kernel, nz, len(swaps), lanes),
        out_shape=[blocks] * 3
        + [jax.ShapeDtypeStruct((hidden, width), F32)] * 3
        + [jax.ShapeDtypeStruct(a.shape, a.dtype) for a in swaps],
        in_specs=[anywhere] * 2 + [vmem] * 3 + [anywhere] * len(swaps),
        out_specs=[anywhere] * 3 + [vmem] * 3 + [anywhere] * len(swaps),
        scratch_shapes=[pltpu.VMEM((2, tokens, width), BF)] * 4
        + [pltpu.SemaphoreType.DMA]
        + [pltpu.SemaphoreType.DMA((len(lanes), 2 * nz - 1))] * 2
        + [pltpu.SemaphoreType.DMA((len(lanes), 2 * nz))] * 2
        + [pltpu.SemaphoreType.DMA((2, 2, 2))] * 2
        + [pltpu.SemaphoreType.DMA((2, max(len(swaps), 1)))],
        compiler_params=pltpu.CompilerParams(
            collective_id=collective_id, has_side_effects=True, vmem_limit_bytes=56 * MIB
        ),
        cost_estimate=link_cost(4 * nz * rows.size * 2, 190e9),
        name="gather_shared",
    )(rows, cot, *shared, *swaps)


def ctx_neighbours():
    c = lax.axis_index("ctx")
    x, core = c // 2, c % 2
    return c, x, core, {"ctx": (1 - x) * 2 + core}, {"ctx": x * 2 + 1 - core}


def ctx_gather_kernel(nz, pieces, x_ref, t_ref, o_ref, u_ref, own_sem, send, recv, sib_send, sib_recv, *trade):
    c, x, core, across, sibling = ctx_neighbours()
    greet(trade_partners(nz))
    size = x_ref.shape[0] // pieces
    far = (1 - x) * 2 + core
    local = pltpu.make_async_copy(x_ref, o_ref.at[c], own_sem)
    first, beside = [], []
    for k in range(pieces):
        piece = pl.ds(k * size, size)
        copy = remote(x_ref.at[piece], o_ref.at[c, piece], send.at[k], recv.at[k], across)
        copy.start()
        first.append(copy)
    copy = remote(x_ref, o_ref.at[c], sib_send.at[pieces], sib_recv.at[pieces], sibling)
    copy.start()
    beside.append(copy)
    local.start()
    kept, traded = trade_copies(nz, t_ref, u_ref, *trade)
    for copy in [kept] + traded:
        copy.start()
    for k in range(pieces):
        piece = pl.ds(k * size, size)
        first[k].wait_recv()
        copy = remote(o_ref.at[far, piece], o_ref.at[far, piece], sib_send.at[k], sib_recv.at[k], sibling)
        copy.start()
        beside.append(copy)
    local.wait()
    for copy in first:
        copy.wait_send()
    for copy in beside + [kept] + traded:
        copy.wait()


def ctx_gather(array, trade, collective_id, pieces=4):
    nz = lax.axis_size("shard")
    return pl.pallas_call(
        functools.partial(ctx_gather_kernel, nz, pieces),
        out_shape=[
            jax.ShapeDtypeStruct((4,) + array.shape, array.dtype),
            jax.ShapeDtypeStruct(trade.shape, trade.dtype),
        ],
        in_specs=[pl.BlockSpec(memory_space=pl.ANY)] * 2,
        out_specs=[pl.BlockSpec(memory_space=pl.ANY)] * 2,
        scratch_shapes=[pltpu.SemaphoreType.DMA]
        + [pltpu.SemaphoreType.DMA((pieces,))] * 2
        + [pltpu.SemaphoreType.DMA((pieces + 1,))] * 2
        + trade_semaphores(nz),
        compiler_params=pltpu.CompilerParams(collective_id=collective_id, has_side_effects=True),
        cost_estimate=link_cost(array.size * array.dtype.itemsize, 30e9),
        name="ctx_gather",
    )(array, trade)


def ctx_scatter_kernel(
    nz, pieces, x_ref, t_ref, o_ref, u_ref, mine, theirs, came, own_sem, sib_send, sib_recv, send, recv, *trade
):
    c, x, core, across, sibling = ctx_neighbours()
    greet(trade_partners(nz))
    size = x_ref.shape[1] // pieces
    loads, shares, flying = {}, {}, []
    for turn in range(2):
        place = (1 - x if turn == 0 else x) * 2
        for k in range(pieces):
            piece = pl.ds(k * size, size)
            loads[turn, k] = pltpu.make_async_copy(
                x_ref.at[place + core, piece], mine.at[turn, piece], own_sem.at[turn, k]
            )
            shares[turn, k] = remote(
                x_ref.at[place + 1 - core, piece],
                theirs.at[turn, piece],
                sib_send.at[turn, k],
                sib_recv.at[turn, k],
                sibling,
            )
            loads[turn, k].start()
            shares[turn, k].start()
    kept, traded = trade_copies(nz, t_ref, u_ref, *trade)
    for copy in [kept] + traded:
        copy.start()
    for turn in range(2):
        for k in range(pieces):
            loads[turn, k].wait()
            shares[turn, k].wait_recv()
            if turn == 1:
                flying[k].wait_recv()

            @pl.loop(0, size // 16)
            def _(step, turn=turn, k=k):
                at = pl.ds(pl.multiple_of(k * size + step * 16, 16), 16)
                total = mine[turn, at, :].astype(F32) + theirs[turn, at, :].astype(F32)
                if turn == 0:
                    mine[turn, at, :] = total.astype(BF)
                else:
                    o_ref[at, :] = total + came[at, :].astype(F32)

            if turn == 0:
                piece = pl.ds(k * size, size)
                copy = remote(mine.at[0, piece], came.at[piece], send.at[k], recv.at[k], across)
                copy.start()
                flying.append(copy)
    for copy in flying:
        copy.wait_send()
    for copy in shares.values():
        copy.wait_send()
    for copy in [kept] + traded:
        copy.wait()


def ctx_scatter(array, trade, collective_id, pieces=4):
    nz = lax.axis_size("shard")
    rows, width = array.shape[1:]
    return pl.pallas_call(
        functools.partial(ctx_scatter_kernel, nz, pieces),
        out_shape=[jax.ShapeDtypeStruct((rows, width), F32), jax.ShapeDtypeStruct(trade.shape, trade.dtype)],
        in_specs=[pl.BlockSpec(memory_space=pl.ANY)] * 2,
        out_specs=[pl.BlockSpec(memory_space=pltpu.VMEM), pl.BlockSpec(memory_space=pl.ANY)],
        scratch_shapes=[
            pltpu.VMEM((2, rows, width), BF),
            pltpu.VMEM((2, rows, width), BF),
            pltpu.VMEM((rows, width), BF),
        ]
        + [pltpu.SemaphoreType.DMA((2, pieces))] * 3
        + [pltpu.SemaphoreType.DMA((pieces,))] * 2
        + trade_semaphores(nz),
        compiler_params=pltpu.CompilerParams(
            collective_id=collective_id, has_side_effects=True, vmem_limit_bytes=32 * MIB
        ),
        cost_estimate=link_cost(array.size * array.dtype.itemsize, 120e9),
        name="ctx_scatter",
    )(array, trade)


def scatter_kernel(nz, count, lanes, *refs):
    ins, outs = refs[:count], refs[count : 2 * count]
    mine, theirs, came = (refs[(2 + k) * count : (3 + k) * count] for k in range(3))
    own_sem, sib_send, sib_recv, send, recv = refs[5 * count :]
    me, core, right, left, sibling = ring_neighbours(nz)
    greet((right, left, sibling))
    steps = 2 * nz

    def block(place, which):
        z, x = ring_at(nz, place)
        return z * 4 + x * 2 + which

    loads, shares = {}, {}
    for step in range(steps):
        for lane, (i, towards, row, rows) in enumerate(lanes):
            place = me - towards * (1 + step)
            piece = pl.ds(row, rows)
            load = pltpu.make_async_copy(
                ins[i].at[block(place, core), piece], mine[i].at[step, piece], own_sem.at[lane, step]
            )
            load.start()
            loads[lane, step] = load
            share = remote(
                ins[i].at[block(place, 1 - core), piece],
                theirs[i].at[step, piece],
                sib_send.at[lane, step],
                sib_recv.at[lane, step],
                sibling,
            )
            share.start()
            shares[lane, step] = share
    flying = {}
    for step in range(steps):
        for lane, (i, towards, row, rows) in enumerate(lanes):
            loads[lane, step].wait()
            shares[lane, step].wait_recv()
            if step > 0:
                flying[lane, step - 1].wait_recv()

            @pl.loop(0, rows // 16)
            def _(turn, i=i, row=row, step=step):
                at = pl.ds(pl.multiple_of(row + turn * 16, 16), 16)
                total = mine[i][step, at, :].astype(F32) + theirs[i][step, at, :].astype(F32)
                if step > 0:
                    total = total + came[i][step - 1, at, :].astype(F32)
                if step < steps - 1:
                    mine[i][step, at, :] = total.astype(BF)
                else:
                    outs[i][at, :] = total

            if step < steps - 1:
                piece = pl.ds(row, rows)
                copy = remote(
                    mine[i].at[step, piece],
                    came[i].at[step, piece],
                    send.at[lane, step],
                    recv.at[lane, step],
                    right if towards > 0 else left,
                )
                copy.start()
                flying[lane, step] = copy
    for copy in flying.values():
        copy.wait_send()
    for copy in shares.values():
        copy.wait_send()


def ring_scatter(arrays, collective_id, pieces=2):
    nz = lax.axis_size("shard")
    shapes = [a.shape[1:] for a in arrays]
    lanes = ring_lanes(shapes, pieces)
    count, steps = len(arrays), 2 * nz
    buffers = [
        pltpu.VMEM((size,) + shape, BF) for size in (steps, steps, steps - 1) for shape in shapes
    ]
    return pl.pallas_call(
        functools.partial(scatter_kernel, nz, count, lanes),
        out_shape=[jax.ShapeDtypeStruct(shape, F32) for shape in shapes],
        in_specs=[pl.BlockSpec(memory_space=pl.ANY)] * count,
        out_specs=[pl.BlockSpec(memory_space=pltpu.VMEM)] * count,
        scratch_shapes=buffers
        + [pltpu.SemaphoreType.DMA((len(lanes), steps))] * 3
        + [pltpu.SemaphoreType.DMA((len(lanes), steps - 1))] * 2,
        compiler_params=pltpu.CompilerParams(
            collective_id=collective_id, has_side_effects=True, vmem_limit_bytes=56 * MIB
        ),
        cost_estimate=link_cost(sum(a.size * a.dtype.itemsize for a in arrays), 190e9),
        name="ring_scatter",
    )(*arrays)


def turn(values, tables):
    cosine, first, second = tables
    return values * cosine + pltpu.roll(values, 96, 1) * first + pltpu.roll(values, 32, 1) * second


def turn_tables(positions):
    sines, cosines = angles(positions)
    nothing = jnp.zeros_like(sines)
    return (
        jnp.concatenate([cosines] * 4, 1),
        jnp.concatenate([-sines, nothing] * 2, 1),
        jnp.concatenate([nothing, sines] * 2, 1),
    )


def turn_back(values, tables):
    cosines, sines = tables[0][:, : ROPE // 2], tables[2][:, ROPE // 2 : ROPE]
    return rotate(values, -sines, cosines)


def project_kernel(heads, x_ref, gain, kv_gain, w_ref, cosine, first, second, *outs):
    low_ref, q_ref, latent_ref, compressed_ref, one_ref, kv_ref = outs
    x = x_ref[...].astype(F32)
    inverse = lax.rsqrt(jnp.mean(x * x, -1, keepdims=True) + EPS)
    low = (x * inverse * gain[...]).astype(BF)
    low_ref[...] = low
    one_ref[...] = inverse
    tables = cosine[...], first[...], second[...]
    nope, rope = heads * NOPE, heads * ROPE
    q_ref[:, :nope] = mm(low, w_ref[:, :nope]).astype(BF)
    raw = mm(low, w_ref[:, nope : nope + rope])
    for k in range(rope // 128):
        q_ref[:, nope + k * 128 : nope + (k + 1) * 128] = turn(raw[:, k * 128 : (k + 1) * 128], tables).astype(BF)
    raw = mm(low, w_ref[:, nope + rope :])
    compressed = raw[:, :R]
    inverse = lax.rsqrt(jnp.mean(compressed * compressed, -1, keepdims=True) + EPS)
    compressed_ref[...] = compressed
    kv_ref[...] = inverse
    latent_ref[:, :R] = (compressed * inverse * kv_gain[...]).astype(BF)
    latent_ref[:, R:] = turn(raw[:, R:], tables).astype(BF)


def project(x, gain, kv_gain, weights, tables, heads):
    rows, width = x.shape
    tile = 128
    columns = heads * (NOPE + ROPE)
    by_row = lambda n: pl.BlockSpec((tile, n), lambda i: (i, 0))
    whole = lambda a: pl.BlockSpec(a.shape, lambda i: (0, 0))
    return pl.pallas_call(
        functools.partial(project_kernel, heads),
        out_shape=(
            jax.ShapeDtypeStruct((rows, width), BF),
            jax.ShapeDtypeStruct((rows, columns), BF),
            jax.ShapeDtypeStruct((rows, R + 128), BF),
            jax.ShapeDtypeStruct((rows, R), F32),
            jax.ShapeDtypeStruct((rows, 1), F32),
            jax.ShapeDtypeStruct((rows, 1), F32),
        ),
        grid=(rows // tile,),
        in_specs=[by_row(width), whole(gain), whole(kv_gain), whole(weights)] + [by_row(128)] * 3,
        out_specs=[by_row(width), by_row(columns), by_row(R + 128), by_row(R), by_row(1), by_row(1)],
        compiler_params=pltpu.CompilerParams(vmem_limit_bytes=48 * MIB),
        cost_estimate=pl.CostEstimate(
            flops=2 * rows * width * weights.shape[1], bytes_accessed=20 * MIB, transcendentals=0
        ),
        name="project",
    )(x, gain, kv_gain, weights, *tables)


def head_key(kv_ref, rope_ref, k):
    rope = rope_ref[...]
    if k:
        rope = pltpu.roll(rope.astype(F32), ROPE, 1).astype(BF)
    return jnp.concatenate([kv_ref[:, k * HEAD : k * HEAD + NOPE], rope], 1)


def attend_kernel(scale, start, qn_ref, qr_ref, kv_ref, rope_ref, seg_q, seg_k, o_ref, l_ref):
    rows, keys = qn_ref.shape[0], kv_ref.shape[0]
    at_q = start[0] + lax.broadcasted_iota(jnp.int32, (rows, keys), 0)
    at_k = lax.broadcasted_iota(jnp.int32, (rows, keys), 1)
    visible = (seg_q[...] == seg_k[...]) & (at_k <= at_q)
    for k in range(2):
        query = jnp.concatenate([qn_ref[:, k * NOPE : (k + 1) * NOPE], qr_ref[...]], 1)
        scores = jnp.where(visible, scale * mm_nt(query, head_key(kv_ref, rope_ref, k)), -1e30)
        peak = jnp.max(scores, -1, keepdims=True)
        weights = jnp.exp(scores - peak)
        total = jnp.sum(weights, -1, keepdims=True)
        values = kv_ref[:, k * HEAD + NOPE : (k + 1) * HEAD]
        o_ref[:, k * V : (k + 1) * V] = (mm(weights.astype(BF), values) * (1.0 / total)).astype(BF)
        l_ref[k] = peak + jnp.log(total)


def attend(query, expanded, rope, seg_q, seg_k, start, scale):
    rows, keys = query.shape[0], expanded.shape[0]
    heads = query.shape[1] // (NOPE + ROPE)
    return pl.pallas_call(
        functools.partial(attend_kernel, scale),
        out_shape=(
            jax.ShapeDtypeStruct((rows, heads * V), BF),
            jax.ShapeDtypeStruct((heads, rows, 1), F32),
        ),
        grid_spec=pltpu.PrefetchScalarGridSpec(
            num_scalar_prefetch=1,
            grid=(heads // 2,),
            in_specs=[
                pl.BlockSpec((rows, 2 * NOPE), lambda h, s: (0, h)),
                pl.BlockSpec((rows, 2 * ROPE), lambda h, s: (0, heads + h)),
                pl.BlockSpec((keys, 2 * HEAD), lambda h, s: (0, h)),
                pl.BlockSpec((keys, 128), lambda h, s: (0, R // 128)),
                pl.BlockSpec((rows, 1), lambda h, s: (0, 0)),
                pl.BlockSpec((1, keys), lambda h, s: (0, 0)),
            ],
            out_specs=[
                pl.BlockSpec((rows, 2 * V), lambda h, s: (0, h)),
                pl.BlockSpec((2, rows, 1), lambda h, s: (h, 0, 0)),
            ],
        ),
        compiler_params=pltpu.CompilerParams(vmem_limit_bytes=60 * MIB),
        cost_estimate=pl.CostEstimate(
            flops=2 * heads * rows * keys * 384, bytes_accessed=12 * MIB, transcendentals=heads * rows * keys
        ),
        name="attend",
    )(start, query, query, expanded, rope, seg_q, seg_k)


def attend_back_kernel(
    scale, start, qn_ref, qr_ref, kv_ref, rope_ref, g_ref, l_ref, seg_q, seg_k, cosine, first, second,
    dqn_ref, dqr_ref, dkv_ref, dr_ref, dr_acc,
):
    rows, keys = qn_ref.shape[0], kv_ref.shape[0]
    at_k = lax.broadcasted_iota(jnp.int32, (keys, rows), 0)
    at_q = start[0] + lax.broadcasted_iota(jnp.int32, (keys, rows), 1)
    visible = (seg_q[...] == seg_k[...]) & (at_k <= at_q)
    grad_ropes, grad_turned = [], None
    for k in range(2):
        key = head_key(kv_ref, rope_ref, k)
        query = jnp.concatenate([qn_ref[:, k * NOPE : (k + 1) * NOPE], qr_ref[...]], 1)
        grad = g_ref[:, k * V : (k + 1) * V]
        scores = scale * mm_nt(key, query)
        probs = jnp.exp(jnp.where(visible, scores, -1e30) - l_ref[k])
        grad_probs = mm_nt(kv_ref[:, k * HEAD + NOPE : (k + 1) * HEAD], grad)
        mean = jnp.sum(probs * grad_probs, 0, keepdims=True)
        grad_scores = (probs * (grad_probs - mean)).astype(BF)
        dkv_ref[:, k * HEAD + NOPE : (k + 1) * HEAD] = mm(probs.astype(BF), grad).astype(BF)
        grad_key = scale * mm(grad_scores, query)
        dkv_ref[:, k * HEAD : k * HEAD + NOPE] = grad_key[:, :NOPE].astype(BF)
        grad_ropes.append(grad_key[:, NOPE:])
        grad_query = scale * mm_tn(grad_scores, key)
        dqn_ref[:, k * NOPE : (k + 1) * NOPE] = grad_query[:, :NOPE].astype(BF)
        grad_turned = grad_query[:, NOPE:] if k == 0 else grad_turned + grad_query[:, NOPE:]
    dqr_ref[...] = turn(grad_turned, (cosine[...], -first[...], -second[...])).astype(BF)
    lane = lax.broadcasted_iota(jnp.int32, (keys, 128), 1)
    grad_rope = jnp.where(lane < ROPE, grad_ropes[0] + pltpu.roll(grad_ropes[1], ROPE, 1), 0.0)

    @pl.when(pl.program_id(0) == 0)
    def _():
        dr_acc[...] = grad_rope

    @pl.when(pl.program_id(0) > 0)
    def _():
        dr_acc[...] += grad_rope

    @pl.when(pl.program_id(0) == pl.num_programs(0) - 1)
    def _():
        dr_ref[...] = dr_acc[...].astype(BF)


def attend_back(query, expanded, rope, grad, logs, seg_q, seg_k, start, tables, scale):
    rows, keys = query.shape[0], expanded.shape[0]
    heads = query.shape[1] // (NOPE + ROPE)
    one = lambda shape: pl.BlockSpec(shape, lambda h, s: (0, 0))
    return pl.pallas_call(
        functools.partial(attend_back_kernel, scale),
        out_shape=(
            jax.ShapeDtypeStruct((rows, heads * NOPE), BF),
            jax.ShapeDtypeStruct((rows, heads * ROPE), BF),
            jax.ShapeDtypeStruct((keys, heads * (NOPE + V)), BF),
            jax.ShapeDtypeStruct((keys, 128), BF),
        ),
        grid_spec=pltpu.PrefetchScalarGridSpec(
            num_scalar_prefetch=1,
            grid=(heads // 2,),
            in_specs=[
                pl.BlockSpec((rows, 2 * NOPE), lambda h, s: (0, h)),
                pl.BlockSpec((rows, 2 * ROPE), lambda h, s: (0, heads + h)),
                pl.BlockSpec((keys, 2 * HEAD), lambda h, s: (0, h)),
                pl.BlockSpec((keys, 128), lambda h, s: (0, R // 128)),
                pl.BlockSpec((rows, 2 * V), lambda h, s: (0, h)),
                pl.BlockSpec((2, 1, rows), lambda h, s: (h, 0, 0)),
                one((1, rows)),
                one((keys, 1)),
            ]
            + [one((rows, 128))] * 3,
            out_specs=[
                pl.BlockSpec((rows, 2 * NOPE), lambda h, s: (0, h)),
                pl.BlockSpec((rows, 2 * ROPE), lambda h, s: (0, h)),
                pl.BlockSpec((keys, 2 * HEAD), lambda h, s: (0, h)),
                one((keys, 128)),
            ],
            scratch_shapes=[pltpu.VMEM((keys, 128), F32)],
        ),
        compiler_params=pltpu.CompilerParams(vmem_limit_bytes=60 * MIB),
        cost_estimate=pl.CostEstimate(
            flops=2 * heads * rows * keys * 1024, bytes_accessed=24 * MIB, transcendentals=heads * rows * keys
        ),
        name="attend_back",
    )(start, query, query, expanded, rope, grad, logs, seg_q, seg_k, *tables)


TILE = 256


def pack_kernel(pair_tile, pair_block, pair_first, pair_on, rank, share, x_ref, o_ref, w_ref, *, weighted):
    i = pl.program_id(0)
    tokens = x_ref.shape[1]

    @pl.when(pair_on[i] == 1)
    def _():
        slot = pair_tile[i] * TILE + lax.broadcasted_iota(jnp.int32, (TILE, tokens), 0)
        chosen = rank[0] == slot
        rows = mm(chosen.astype(F32).astype(BF), x_ref[0])
        weight = jnp.sum(jnp.where(chosen, share[0], 0.0), 1, keepdims=True)
        if weighted:
            rows = rows * weight
        rows = rows.astype(BF)

        @pl.when(pair_first[i] == 1)
        def _():
            o_ref[...] = rows
            w_ref[...] = weight

        @pl.when(pair_first[i] == 0)
        def _():
            o_ref[...] += rows
            w_ref[...] += weight


def pack(pairs, rank, share, x, weighted):
    blocks, tokens, width = x.shape
    slots = blocks * tokens
    return pl.pallas_call(
        functools.partial(pack_kernel, weighted=weighted),
        out_shape=(
            jax.ShapeDtypeStruct((slots, width), BF),
            jax.ShapeDtypeStruct((slots, 1), F32),
        ),
        grid_spec=pltpu.PrefetchScalarGridSpec(
            num_scalar_prefetch=4,
            grid=(pairs["tile"].shape[0],),
            in_specs=[
                pl.BlockSpec((1, 1, tokens), lambda i, t, b, f, a: (b[i], 0, 0)),
                pl.BlockSpec((1, 1, tokens), lambda i, t, b, f, a: (b[i], 0, 0)),
                pl.BlockSpec((1, tokens, width), lambda i, t, b, f, a: (b[i], 0, 0)),
            ],
            out_specs=[
                pl.BlockSpec((TILE, width), lambda i, t, b, f, a: (t[i], 0)),
                pl.BlockSpec((TILE, 1), lambda i, t, b, f, a: (t[i], 0)),
            ],
        ),
        compiler_params=pltpu.CompilerParams(vmem_limit_bytes=40 * MIB),
        cost_estimate=pl.CostEstimate(
            flops=2 * 24 * TILE * tokens * width, bytes_accessed=28 * MIB, transcendentals=0
        ),
        name="pack",
    )(pairs["tile"], pairs["block"], pairs["first_tile"], pairs["on"], rank, share, x)


def expert_kernel(parts, tiles, x_ref, g_ref, w_ref, *refs):
    gates, ups, downs = (refs[k * parts : (k + 1) * parts] for k in range(3))
    out_ref, gin_ref = refs[3 * parts : 3 * parts + 2]
    hids, ggs, gus = (refs[3 * parts + 2 + k * parts : 3 * parts + 2 + (k + 1) * parts] for k in range(3))

    @pl.when(pl.program_id(0) < tiles[0])
    def _():
        x, g = x_ref[...], g_ref[...]
        out = gin = None
        for part in range(parts):
            gate, up, down = gates[part][...], ups[part][...], downs[part][...]
            a = mm_nt(x, gate)
            b = mm_nt(x, up)
            sig = jax.nn.sigmoid(a)
            act = a * sig
            hidden = (act * b).astype(BF)
            hids[part][...] = hidden
            grad_hidden = mm_nt(g, down)
            grad_gate = (grad_hidden * b * (sig * (1.0 + a * (1.0 - sig)))).astype(BF)
            grad_up = (grad_hidden * act).astype(BF)
            ggs[part][...] = grad_gate
            gus[part][...] = grad_up
            o = mm(hidden, down)
            gi = mm(grad_gate, gate) + mm(grad_up, up)
            out = o if out is None else out + o
            gin = gi if gin is None else gin + gi
        out_ref[...] = (out * w_ref[...]).astype(BF)
        gin_ref[...] = gin.astype(BF)


def experts(tiles, x, g, w, gates, ups, downs):
    slots, width = x.shape
    parts, hidden = len(gates), gates[0].shape[0]
    row = lambda i, t: (jnp.minimum(i, t[0] - 1), 0)
    whole = lambda i, t: (0, 0)
    once = pl.Buffered(1)
    results = pl.pallas_call(
        functools.partial(expert_kernel, parts),
        out_shape=(jax.ShapeDtypeStruct((slots, width), BF),) * 2
        + (jax.ShapeDtypeStruct((slots, hidden), BF),) * (3 * parts),
        grid_spec=pltpu.PrefetchScalarGridSpec(
            num_scalar_prefetch=1,
            grid=(slots // TILE,),
            in_specs=[
                pl.BlockSpec((TILE, width), row),
                pl.BlockSpec((TILE, width), row),
                pl.BlockSpec((TILE, 1), row),
            ]
            + [pl.BlockSpec((hidden, width), whole, pipeline_mode=once)] * (3 * parts),
            out_specs=[pl.BlockSpec((TILE, width), row)] * 2
            + [pl.BlockSpec((TILE, hidden), row)] * (3 * parts),
        ),
        compiler_params=pltpu.CompilerParams(vmem_limit_bytes=60 * MIB),
        cost_estimate=pl.CostEstimate(
            flops=12 * 2560 * width * parts * hidden, bytes_accessed=100 * MIB, transcendentals=0
        ),
        name="experts",
    )(tiles, x, g, w, *gates, *ups, *downs)
    kept = [results[2 + k * parts : 2 + (k + 1) * parts] for k in range(3)]
    return results[0], results[1], kept


def expert_sums(tiles, x_ref, g_ref, hid_ref, gg_ref, gu_ref, sums):
    @pl.when(pl.program_id(0) < tiles[0])
    def _():
        x, g = x_ref[...], g_ref[...]
        sums[0][...] += mm_tn(gg_ref[...], x)
        sums[1][...] += mm_tn(gu_ref[...], x)
        sums[2][...] += mm_tn(hid_ref[...], g)


def expert_sums_kernel(tiles, x_ref, g_ref, hid_ref, gg_ref, gu_ref, *refs):
    outs, sums = refs[:3], refs[3:]

    @pl.when(pl.program_id(0) == 0)
    def _():
        for total in sums:
            total[...] = jnp.zeros_like(total)

    expert_sums(tiles, x_ref, g_ref, hid_ref, gg_ref, gu_ref, sums)

    @pl.when(pl.program_id(0) == pl.num_programs(0) - 1)
    def _():
        for out, total in zip(outs, sums):
            out[...] = total[...].astype(out.dtype)


def expert_totals_kernel(tiles, x_ref, g_ref, hid_ref, gg_ref, gu_ref, *refs):
    starts, outs = refs[:3], refs[3:]

    @pl.when(pl.program_id(0) == 0)
    def _():
        for out, start in zip(outs, starts):
            out[...] = start[...].astype(F32)

    expert_sums(tiles, x_ref, g_ref, hid_ref, gg_ref, gu_ref, outs)


def expert_grads(tiles, x, g, hid, gg, gu, starts=None):
    slots, width = x.shape
    hidden = hid.shape[1]
    row = lambda i, t: (jnp.minimum(i, t[0] - 1), 0)
    whole = lambda i, t: (0, 0)
    once = pl.Buffered(1)
    kernel = expert_sums_kernel if starts is None else expert_totals_kernel
    held = [pl.BlockSpec((hidden, width), whole, pipeline_mode=once)] * 3
    return pl.pallas_call(
        kernel,
        out_shape=(jax.ShapeDtypeStruct((hidden, width), BF if starts is None else F32),) * 3,
        grid_spec=pltpu.PrefetchScalarGridSpec(
            num_scalar_prefetch=1,
            grid=(slots // TILE,),
            in_specs=[pl.BlockSpec((TILE, width), row)] * 2
            + [pl.BlockSpec((TILE, hidden), row)] * 3
            + (held if starts is not None else []),
            out_specs=held,
            scratch_shapes=[pltpu.VMEM((hidden, width), F32)] * 3 if starts is None else [],
        ),
        compiler_params=pltpu.CompilerParams(vmem_limit_bytes=60 * MIB),
        cost_estimate=pl.CostEstimate(
            flops=6 * 2560 * width * hidden, bytes_accessed=40 * MIB, transcendentals=0
        ),
        name="expert_grads",
    )(tiles, x, g, hid, gg, gu, *(starts or ()))


def dense_kernel(
    pair_tile, pair_block, pair_first, pair_last, pair_real, rank, x_ref, c_ref, out_ref, gin_ref, total_ref, grad_ref, acc, gacc
):
    i = pl.program_id(0)

    @pl.when(pair_first[i] == 1)
    def _():
        acc[...] = x_ref[0].astype(F32)
        gacc[...] = c_ref[0].astype(F32)

    @pl.when(pair_real[i] == 1)
    def _():
        tokens = rank.shape[1]
        slot = pair_tile[i] * TILE + lax.broadcasted_iota(jnp.int32, (tokens, TILE), 1)
        chosen = (rank[0] == slot).astype(F32).astype(BF)
        acc[...] += mm(chosen, out_ref[...])
        gacc[...] += mm(chosen, gin_ref[...])

    @pl.when(pair_last[i] == 1)
    def _():
        total_ref[0] = acc[...].astype(BF)
        grad_ref[0] = gacc[...].astype(BF)


def dense(pairs, rank_column, shared_out, shared_gin, out, gin):
    blocks, tokens, width = shared_out.shape
    by_block = lambda i, t, b, f, l, r: (b[i], 0, 0)
    by_tile = lambda i, t, b, f, l, r: (t[i], 0)
    return pl.pallas_call(
        dense_kernel,
        out_shape=(jax.ShapeDtypeStruct((blocks, tokens, width), BF),) * 2,
        grid_spec=pltpu.PrefetchScalarGridSpec(
            num_scalar_prefetch=5,
            grid=(pairs["tile"].shape[0],),
            in_specs=[
                pl.BlockSpec((1, tokens, 1), by_block),
                pl.BlockSpec((1, tokens, width), by_block),
                pl.BlockSpec((1, tokens, width), by_block),
                pl.BlockSpec((TILE, width), by_tile),
                pl.BlockSpec((TILE, width), by_tile),
            ],
            out_specs=[pl.BlockSpec((1, tokens, width), by_block)] * 2,
            scratch_shapes=[pltpu.VMEM((tokens, width), F32)] * 2,
        ),
        compiler_params=pltpu.CompilerParams(vmem_limit_bytes=60 * MIB),
        cost_estimate=pl.CostEstimate(
            flops=4 * 26 * TILE * tokens * width, bytes_accessed=90 * MIB, transcendentals=0
        ),
        name="dense",
    )(
        pairs["tile"], pairs["block"], pairs["first_block"], pairs["last_block"], pairs["real"],
        rank_column, shared_out, shared_gin, out, gin,
    )


def routing(share):
    blocks, tokens = share.shape
    used = (share > 0).astype(F32)
    upper = (jnp.arange(tokens)[:, None] <= jnp.arange(tokens)[None, :]).astype(BF)
    inside = mm(used.astype(BF), upper).astype(jnp.int32)
    counts = inside[:, -1]
    lower = jnp.arange(blocks)[:, None] > jnp.arange(blocks)[None, :]
    start = jnp.sum(jnp.where(lower, counts[None, :], 0), 1)
    end = start + counts
    rank = jnp.where(share > 0, start[:, None] + inside - 1, -1)
    last_tile = blocks * tokens // TILE - 1
    first = jnp.minimum(start // TILE, last_tile)
    last = jnp.where(counts > 0, (end - 1) // TILE, first)
    spans = last - first + 1
    after = jnp.sum(jnp.where(lower | jnp.eye(blocks, dtype=bool), spans[None, :], 0), 1)
    size = 2 * blocks
    turn = jnp.arange(size)
    all_pairs = after[-1]
    on = turn < all_pairs
    place = jnp.minimum(turn, all_pairs - 1)
    block = jnp.sum((after[None, :] <= place[:, None]).astype(jnp.int32), 1)
    pick = block[:, None] == jnp.arange(blocks)[None, :]
    take = lambda v: jnp.sum(jnp.where(pick, v[None, :], 0), 1)
    tile = take(first) + place - take(after - spans)
    shifted = lambda v: jnp.concatenate([jnp.full((1,), -1, v.dtype), v[:-1]])
    as_int = lambda v: v.astype(jnp.int32)
    pairs = {
        "tile": as_int(tile),
        "block": as_int(block),
        "on": as_int(on),
        "real": as_int(on & (take(counts) > 0)),
        "first_tile": as_int(on & (shifted(tile) != tile)),
        "first_block": as_int(on & (shifted(block) != block)),
        "last_block": as_int(on & (place == take(after) - 1)),
    }
    tiles = as_int(jnp.maximum((end[-1] + TILE - 1) // TILE, 1))[None]
    return rank.astype(jnp.int32), pairs, tiles


def other_half_sum(rows, product):
    parts, me = lax.axis_size("tp"), lax.axis_index("tp")
    size = rows.shape[0] // parts
    if parts != 2:
        return lax.psum_scatter(product(rows).astype(BF), "tp", scatter_dimension=0, tiled=True).astype(F32)
    sent = product(lax.dynamic_slice_in_dim(rows, (1 - me) * size, size)).astype(BF)
    came = lax.ppermute(sent, "tp", [(0, 1), (1, 0)])
    return product(lax.dynamic_slice_in_dim(rows, me * size, size)) + came.astype(F32)


def swap_tp(v):
    return lax.ppermute(v, "tp", [(0, 1), (1, 0)])


def join_tp(v):
    if lax.axis_size("tp") != 2:
        return lax.all_gather(v, "tp", axis=0, tiled=True)
    came = swap_tp(v)
    return jnp.where(lax.axis_index("tp") == 0, jnp.stack([v, came]), jnp.stack([came, v])).reshape(
        (2 * v.shape[0],) + v.shape[1:]
    )


def on_device(
    inputs,
    segments,
    routes,
    gate_share,
    cotangent,
    attn_gain,
    kv_gain,
    ffn_gain,
    w_query,
    w_latent,
    w_expand,
    w_output,
    w_shared_gate,
    w_shared_up,
    w_shared_down,
    expert_gate,
    expert_up,
    expert_down,
):
    tokens, width = inputs.shape
    parts, part = lax.axis_size("tp"), lax.axis_index("tp")
    half = tokens // parts
    group = lax.axis_size(GROUP)
    me = lax.axis_index(GROUP)
    ctx = lax.axis_size("ctx")
    query_width = w_query.shape[1]
    heads = query_width // (NOPE + ROPE)
    scale = (NOPE + ROPE) ** (-0.5)
    own_half = lambda v: lax.dynamic_slice_in_dim(v, part * half, half)

    gain_row = jnp.concatenate([attn_gain, kv_gain, ffn_gain])
    n_attn, n_kv = attn_gain.shape[0], kv_gain.shape[0]
    gain_rows = jnp.zeros((16, 384), BF).at[0, : gain_row.shape[0]].set(gain_row)
    by_head = w_query.reshape(-1, heads, NOPE + ROPE)
    first_weights = jnp.concatenate(
        [
            by_head[..., :NOPE].reshape(-1, heads * NOPE),
            by_head[..., NOPE:].reshape(-1, heads * ROPE),
            w_latent,
            jnp.zeros((w_latent.shape[0], 128 - ROPE), BF),
        ],
        1,
    )
    expert_ids = jnp.arange(group, dtype=jnp.int32)
    shares = jnp.sum(
        jnp.where(own_half(routes).T[None] == expert_ids[:, None, None], own_half(gate_share).T[None], 0.0), 1
    )
    gate, up, down = (jnp.swapaxes(expert_gate[0], 0, 1), jnp.swapaxes(expert_up[0], 0, 1), expert_down[0])
    together = lax.optimization_barrier
    piece = w_shared_gate.shape[1] // group
    depth = w_shared_gate.shape[0]
    cut = lambda v: v.reshape(group, piece, depth)
    shared_sent = jnp.concatenate(
        [cut(jnp.swapaxes(w_shared_gate, 0, 1)), cut(jnp.swapaxes(w_shared_up, 0, 1)), cut(w_shared_down)], 1
    )
    first = ring_gather(
        [
            first_weights,
            jnp.swapaxes(w_output, 0, 1),
            w_expand,
            gain_rows,
            shares,
            jnp.broadcast_to(segments[None], (16, tokens)),
        ],
        1,
        swaps=[gate] if parts == 2 else [],
    )
    first_full, output_full, expand_full, gains, share, all_segments = first[:6]
    expand_full = expand_full.reshape(R, -1)
    output_full = output_full.reshape(width, -1)
    attn_scale = gains[:, 0, :n_attn].reshape(-1).astype(F32)
    kv_scale = gains[:, 0, n_attn : n_attn + n_kv].reshape(-1).astype(F32)
    ffn_scale = gains[:, 0, n_attn + n_kv : gain_row.shape[0]].reshape(-1).astype(F32)
    first_full = first_full.reshape(width, -1)
    all_segments = lax.dynamic_slice_in_dim(
        all_segments[:, 0], lax.axis_index("shard") * ctx, ctx
    ).reshape(-1)
    share = lax.dynamic_index_in_dim(share, me, 1, keepdims=False)
    rank, pairs, tiles = routing(share)

    cot_all = lax.all_gather(together((own_half(cotangent), gains))[0], GROUP, axis=0, tiled=False)
    if parts == 2:
        up_other = swap_tp(together((up, gains))[0])

    residual = inputs.astype(F32)
    start = lax.axis_index("ctx") * tokens
    tables = turn_tables(start + jnp.arange(tokens, dtype=jnp.int32))
    attn_low, query_low, latent_low, compressed, inverse_one, inverse_kv = project(
        inputs, attn_scale[None], kv_scale[None], first_full, tables, heads
    )
    all_latent, shared_own = ctx_gather(latent_low, shared_sent, 5)
    all_latent = all_latent.reshape(ctx * tokens, -1)
    shared_own = jnp.swapaxes(shared_own, 0, 1).reshape(3 * piece, width)
    expanded = mm(all_latent[:, :R], expand_full).astype(BF)
    begin = start.astype(jnp.int32)[None]
    if parts == 2:
        expanded, shared_own, up_other = together((expanded, shared_own, up_other))
        shared_parts = [shared_own, swap_tp(shared_own)]
    else:
        shared_parts = list(lax.all_gather(shared_own, "tp", axis=0, tiled=False))
    attended, logs = attend(
        query_low, expanded, all_latent, segments[:, None], all_segments[None, :], begin, scale
    )
    attended, shared_parts = together((attended, shared_parts))
    shared = [
        jnp.concatenate([v[k * piece : (k + 1) * piece] for v in shared_parts], 0) for k in range(3)
    ]
    middle = own_half(residual) + other_half_sum(attended, lambda rows: mm_nt(rows, output_full))
    normed_two, inverse_two = norm_forward(middle, ffn_scale)
    ffn_low = normed_two.astype(BF)

    rank_row, share_row = rank[:, None, :], share[:, None, :]
    grad_rows, weights = pack(pairs, rank_row, share_row, cot_all, True)
    if parts == 2:
        ffn_low, grad_rows = together((ffn_low, grad_rows))
        rows_all, shared_out, shared_gin, *shared_grads, down_other = gather_shared(
            ffn_low, cot_all, shared, 2, swaps=[down]
        )
        gates, ups, downs = [gate, first[6]], [up, up_other], [down, down_other]
    else:
        rows_all, shared_out, shared_gin, *shared_grads = gather_shared(ffn_low, cot_all, shared, 2)
        gates, ups, downs = (list(lax.all_gather(v, "tp", axis=0, tiled=False)) for v in (gate, up, down))
    rows_in, _ = pack(pairs, rank_row, share_row, rows_all, False)
    expert_out, expert_gin, kept = experts(tiles, rows_in, grad_rows, weights, gates, ups, downs)

    grads_of = lambda which, *starts: expert_grads(
        tiles, rows_in, grad_rows, *(k[which] for k in kept), *starts
    )
    if parts == 2:
        expert_out, sent = together((expert_out, grads_of(1)))
        came = [swap_tp(v) for v in sent]
    moe_part, grad_part = dense(pairs, rank[:, :, None], shared_out, shared_gin, expert_out, expert_gin)
    (grad_normed_two,) = ring_scatter([grad_part], 3)
    if parts == 2:
        grad_normed_two, came = together((grad_normed_two, came))
        own_grads = grads_of(0, tuple(came))
    else:
        sent = [grads_of(k) for k in range(parts)]
        own_grads = [
            lax.psum_scatter(jnp.stack(v), "tp", scatter_dimension=0, tiled=False).astype(F32) for v in zip(*sent)
        ]

    grad_out = own_half(cotangent).astype(F32)
    grad_mid_norm, ffn_gain_grad = norm_backward(middle, inverse_two, ffn_scale, grad_normed_two)
    grad_middle = grad_out + grad_mid_norm
    grad_middle_low = join_tp(grad_middle.astype(BF))
    grad_middle_low, own_grads = together((grad_middle_low, own_grads))
    gate_grad, up_grad, down_grad = (
        jnp.swapaxes(own_grads[0], 0, 1)[None], jnp.swapaxes(own_grads[1], 0, 1)[None], own_grads[2][None]
    )
    shared_back = [
        jnp.concatenate([v[k * piece : (k + 1) * piece] for v in shared_grads], 0) for k in range(parts)
    ]
    shared_back, grad_middle_low = together((shared_back, grad_middle_low))
    if parts == 2:
        shared_back = (shared_back[0], swap_tp(shared_back[1].astype(BF)))
    else:
        shared_back = lax.psum_scatter(jnp.stack(shared_back).astype(BF), "tp", scatter_dimension=0, tiled=False)

    moe_part = lax.optimization_barrier((moe_part, grad_normed_two))[0]
    moe_total = lax.psum_scatter(
        moe_part.reshape(group * half, width), GROUP, scatter_dimension=0, tiled=True
    )

    grad_attended = mm(grad_middle_low, output_full).astype(BF)
    grad_nope, grad_turned, grad_kv, grad_rope = attend_back(
        query_low, expanded, all_latent, grad_attended, jnp.swapaxes(logs, 1, 2),
        segments[None, :], all_segments[:, None], begin, tables, scale,
    )
    shared_back, grad_kv = together((shared_back, grad_kv))
    if parts == 2:
        shared_back = shared_back[0] + shared_back[1].astype(F32)
    shared_back = jnp.swapaxes(shared_back.astype(BF).reshape(3 * piece, group, depth), 0, 1)
    output_grad = mm_tn(grad_middle_low, attended).astype(BF)
    grad_query = jnp.concatenate([grad_nope, grad_turned], 1)
    grad_comp = mm_nt(grad_kv, expand_full)
    grad_comp = jnp.concatenate([grad_comp.astype(BF), grad_rope], 1)
    grad_comp, shared_back = ctx_scatter(grad_comp.reshape(ctx, tokens, -1), shared_back, 6)
    expand_grad = mm_tn(all_latent[:, :R], grad_kv).astype(BF)
    query_grad = mm_tn(attn_low, grad_query).astype(BF)
    grad_compressed, kv_gain_grad = norm_backward(compressed, inverse_kv, kv_scale, grad_comp[:, :R])
    grad_latent = jnp.concatenate(
        [grad_compressed, turn_back(grad_comp[:, R : R + ROPE], tables)], -1
    ).astype(BF)
    latent_grad = mm_tn(attn_low, grad_latent).astype(BF)
    grad_first = jnp.concatenate([grad_query, grad_latent, jnp.zeros((tokens, 128 - ROPE), BF)], 1)
    grad_normed_one = other_half_sum(grad_first, lambda rows: mm_nt(rows, first_full))
    grad_in_norm, attn_gain_grad = norm_backward(
        own_half(residual), own_half(inverse_one), attn_scale, grad_normed_one
    )
    grad_inputs = join_tp((grad_middle + grad_in_norm).astype(BF))

    moe_total, attn_gain_grad = together((moe_total, attn_gain_grad))
    result = join_tp((middle + moe_total.astype(F32)).astype(BF))

    gain_grads = jnp.concatenate(
        [v.reshape(group, -1) for v in (attn_gain_grad, kv_gain_grad, ffn_gain_grad)], 1
    ).astype(BF)
    tail = jnp.zeros((group, 16, 384), BF).at[:, 0, : gain_grads.shape[1]].set(gain_grads)
    output_own, expand_own, query_own, latent_own, gains_own = ring_scatter(
        [
            output_grad.reshape(group, -1, output_grad.shape[1]),
            expand_grad.reshape(group, -1, expand_grad.shape[1]),
            query_grad.reshape(group, -1, query_width),
            latent_grad.reshape(group, -1, latent_grad.shape[1]),
            tail,
        ],
        4,
        pieces=1,
    )
    output_own = jnp.swapaxes(output_own, 0, 1)
    back = [shared_back[:, k * piece : (k + 1) * piece].reshape(-1, depth).astype(F32) for k in range(3)]
    sgate_grad, sup_grad, sdown_grad = jnp.swapaxes(back[0], 0, 1), jnp.swapaxes(back[1], 0, 1), back[2]
    nopes = query_own[:, : heads * NOPE].reshape(-1, heads, NOPE)
    query_own = jnp.concatenate([nopes, query_own[:, heads * NOPE :].reshape(-1, heads, ROPE)], -1)
    query_own = query_own.reshape(-1, query_width)
    if parts == 2:
        small = jnp.concatenate([latent_own.reshape(-1, 128), gains_own[:8].reshape(-1, 128)], 0)
        small = small + swap_tp(small)
        latent_own = small[: -gains_own[:8].size // 128].reshape(latent_own.shape)
        gains_own = small[-gains_own[:8].size // 128 :].reshape(8, -1)[0]
    else:
        latent_own, gains_own = lax.psum((latent_own, gains_own[0]), "tp")
    return (
        result,
        grad_inputs.astype(F32),
        gains_own[:n_attn],
        gains_own[n_attn : n_attn + n_kv],
        gains_own[n_attn + n_kv : gain_row.shape[0]],
        query_own,
        latent_own,
        expand_own,
        output_own,
        sgate_grad,
        sup_grad,
        sdown_grad,
        gate_grad,
        up_grad,
        down_grad,
    )


def solution(mesh):
    group = P(GROUP)
    rows = P(GROUP, None)
    both = P(GROUP, "tp")
    turned = P("tp", GROUP)
    return jax.shard_map(
        on_device,
        mesh=mesh,
        in_specs=(
            rows, group, rows, rows, rows, group, group, group,
            both, rows, both, turned, both, both, turned,
            P(GROUP, None, "tp"), P(GROUP, None, "tp"), P(GROUP, "tp", None),
        ),
        out_specs=(
            rows, rows, group, group, group,
            both, rows, both, turned, both, both, turned,
            P(GROUP, None, "tp"), P(GROUP, None, "tp"), P(GROUP, "tp", None),
        ),
        check_vma=False,
    )
```

```python
import functools

import jax
import jax.numpy as jnp
from jax import lax
from jax.experimental import pallas as pl
from jax.experimental.pallas import tpu as pltpu
from jax.sharding import PartitionSpec as P

NOPE = 128
ROPE = 64
V = 128
R = 512
HEAD = 256
EPS = 1e-06
GROUP = ("shard", "ctx")
MESH = pl.DeviceIdType.MESH
BF = jnp.bfloat16
F32 = jnp.float32
MIB = 1 << 20


def norm_forward(values, gain):
    inverse = lax.rsqrt(jnp.mean(values * values, -1, keepdims=True) + EPS)
    return (values * inverse * gain, inverse)


def norm_backward(values, inverse, gain, upstream):
    scaled = upstream * gain
    gain_grad = jnp.sum(upstream * values * inverse, 0)
    value_grad = inverse * scaled - values * inverse**3 * jnp.mean(
        scaled * values, -1, keepdims=True
    )
    return (value_grad, gain_grad)


def angles(positions):
    half_width = ROPE // 2
    freq_table = 10000.0 ** (-jnp.arange(half_width, dtype=F32) / half_width)
    turned = positions.astype(F32)[:, None] * freq_table[None, :]
    return (jnp.sin(turned), jnp.cos(turned))


def mm(a, b):
    return jnp.dot(a, b, preferred_element_type=F32)


def mm_nt(a, b):
    return lax.dot_general(a, b, (((1,), (1,)), ((), ())), preferred_element_type=F32)


def mm_tn(a, b):
    return lax.dot_general(a, b, (((0,), (0,)), ((), ())), preferred_element_type=F32)


def ring_place(nz):
    z = lax.axis_index("shard")
    c = lax.axis_index("ctx")
    x, core = c // 2, c % 2
    return jnp.where(x == 0, z, 2 * nz - 1 - z), x, core


def ring_at(nz, p):
    p = lax.rem(p + 4 * nz, 2 * nz)
    return jnp.where(p < nz, p, 2 * nz - 1 - p), p // nz


def ring_lanes(shapes, pieces):
    lanes = []
    for index, (rows, _) in enumerate(shapes):
        first = -(-rows // 32) * 16
        ways = []
        for towards, start, size in ((1, 0, first), (-1, first, rows - first)):
            units = size // 16
            parts = min(pieces, units)
            way, at = [], start
            for part in range(parts):
                here = 16 * (units // parts + (1 if part < units % parts else 0))
                way.append((index, towards, at, here))
                at += here
            ways.append(way)
        for part in range(pieces):
            lanes += [way[part] for way in ways if part < len(way)]
    return lanes


def greet(devices):
    barrier = pltpu.get_barrier_semaphore()
    for device in devices:
        pl.semaphore_signal(barrier, inc=1, device_id=device, device_id_type=MESH)
    pl.semaphore_wait(barrier, len(devices))


def ring_neighbours(nz):
    me, x, core = ring_place(nz)
    zr, xr = ring_at(nz, me + 1)
    zl, xl = ring_at(nz, me - 1)
    right = {"shard": zr, "ctx": xr * 2 + core}
    left = {"shard": zl, "ctx": xl * 2 + core}
    sibling = {"ctx": x * 2 + 1 - core}
    return me, core, right, left, sibling


def link_cost(size, rate):
    return pl.CostEstimate(flops=int(size / rate * 9e14), bytes_accessed=2 * size, transcendentals=0)


def remote(src, dst, send, recv, device):
    return pltpu.make_async_remote_copy(
        src_ref=src, dst_ref=dst, send_sem=send, recv_sem=recv, device_id=device, device_id_type=MESH
    )


def ring_semaphores(nz, count, lanes):
    return (
        [pltpu.SemaphoreType.DMA((count,))]
        + [pltpu.SemaphoreType.DMA((len(lanes), 2 * nz - 1))] * 2
        + [pltpu.SemaphoreType.DMA((len(lanes), 2 * nz))] * 2
    )


def ring_steps(nz, lanes, ins, outs, me, core, right, left, sibling, own_sem, send, recv, sib_send, sib_recv):
    steps = 2 * nz

    def block(place, which):
        z, x = ring_at(nz, place)
        return z * 4 + x * 2 + which

    own = block(me, core)
    local = [pltpu.make_async_copy(a, b.at[own], own_sem.at[i]) for i, (a, b) in enumerate(zip(ins, outs))]
    flying = []
    last = {}
    for step in range(steps):
        for lane, (i, towards, row, rows) in enumerate(lanes):
            here = block(me - towards * step, core)
            piece = pl.ds(row, rows)
            if step > 0:
                last[lane].wait_recv()
            src = ins[i].at[piece] if step == 0 else outs[i].at[here, piece]
            dst = outs[i].at[here, piece]
            if step < steps - 1:
                copy = remote(
                    src, dst, send.at[lane, step], recv.at[lane, step], right if towards > 0 else left
                )
                copy.start()
                last[lane] = copy
                flying.append((copy, False))
            copy = remote(src, dst, sib_send.at[lane, step], sib_recv.at[lane, step], sibling)
            copy.start()
            flying.append((copy, True))
        if step == 0:
            for copy in local:
                copy.start()
        yield
    for copy in local:
        copy.wait()
    for copy, both in flying:
        copy.wait_send()
        if both:
            copy.wait_recv()


def trade_copies(nz, x_ref, o_ref, own_sem, send, recv):
    devices = 4 * nz
    me = lax.axis_index("shard") * 4 + lax.axis_index("ctx")
    local = pltpu.make_async_copy(x_ref.at[me], o_ref.at[me], own_sem)
    copies = []
    for shift in range(1, devices):
        there = lax.rem(me + shift, devices)
        device = {"shard": there // 4, "ctx": lax.rem(there, 4)}
        copies.append(remote(x_ref.at[there], o_ref.at[me], send.at[shift - 1], recv.at[shift - 1], device))
    return local, copies


def trade_partners(nz):
    devices = 4 * nz
    me = lax.axis_index("shard") * 4 + lax.axis_index("ctx")
    there = [lax.rem(me + shift, devices) for shift in range(1, devices)]
    return tuple({"shard": t // 4, "ctx": lax.rem(t, 4)} for t in there)


def trade_semaphores(nz):
    return [pltpu.SemaphoreType.DMA] + [pltpu.SemaphoreType.DMA((4 * nz - 1,))] * 2


def gather_kernel(nz, count, swaps, lanes, *refs):
    total = count + swaps
    ins, outs = refs[:total], refs[total : 2 * total]
    *ring, swap_send, swap_recv = refs[2 * total :]
    me, core, right, left, sibling = ring_neighbours(nz)
    across = {"tp": 1 - lax.axis_index("tp")}
    greet((right, left, sibling) + ((across,) if swaps else ()))
    swapped = [
        remote(ins[count + i], outs[count + i], swap_send.at[i], swap_recv.at[i], across) for i in range(swaps)
    ]
    for step, _ in enumerate(ring_steps(nz, lanes, ins[:count], outs[:count], me, core, right, left, sibling, *ring)):
        if step == 0:
            for copy in swapped:
                copy.start()
    for copy in swapped:
        copy.wait()


def ring_gather(arrays, collective_id, pieces=2, swaps=()):
    nz = lax.axis_size("shard")
    lanes = ring_lanes([a.shape for a in arrays], pieces)
    given = [*arrays, *swaps]
    count, total = len(arrays), len(given)
    return pl.pallas_call(
        functools.partial(gather_kernel, nz, count, len(swaps), lanes),
        out_shape=[jax.ShapeDtypeStruct((4 * nz,) + a.shape, a.dtype) for a in arrays]
        + [jax.ShapeDtypeStruct(a.shape, a.dtype) for a in swaps],
        in_specs=[pl.BlockSpec(memory_space=pl.ANY)] * total,
        out_specs=[pl.BlockSpec(memory_space=pl.ANY)] * total,
        scratch_shapes=ring_semaphores(nz, count, lanes)
        + [pltpu.SemaphoreType.DMA((max(len(swaps), 1),))] * 2,
        compiler_params=pltpu.CompilerParams(collective_id=collective_id, has_side_effects=True),
        cost_estimate=link_cost(4 * nz * sum(a.size * a.dtype.itemsize for a in arrays), 190e9),
        name="ring_gather",
    )(*given)


def gather_shared_kernel(
    nz, swaps, lanes, row_ref, cot_ref, gate_ref, up_ref, down_ref, *refs
):
    swap_in, refs = refs[:swaps], refs[swaps:]
    all_ref, out_ref, gin_ref, dg_ref, du_ref, dd_ref, *refs = refs
    swap_out, refs = refs[:swaps], refs[swaps:]
    xs, cs, outs, gins, own_sem, send, recv, sib_send, sib_recv, loads, stores, swap_sem = refs
    me, core, right, left, sibling = ring_neighbours(nz)
    across = {"tp": 1 - lax.axis_index("tp")}
    greet((right, left, sibling) + ((across,) if swaps else ()))
    steps = 2 * nz
    first = sum(rows for _, towards, _, rows in lanes if towards > 0)
    total = row_ref.shape[0]
    halves = ((1, 0, first), (-1, first, total - first))

    def block(place, which):
        z, x = ring_at(nz, place)
        return z * 4 + x * 2 + which

    def ring_copy(lane, step, src=None):
        _, towards, row, rows = lanes[lane]
        ref = all_ref.at[block(me - towards * step, core), pl.ds(row, rows)]
        src = ref if src is None else src.at[pl.ds(row, rows)]
        return remote(src, ref, send.at[lane, step], recv.at[lane, step], right if towards > 0 else left)

    def sibling_copy(lane, step, which, src=None):
        _, towards, row, rows = lanes[lane]
        ref = all_ref.at[block(me - towards * step, which), pl.ds(row, rows)]
        src = ref if src is None else src.at[pl.ds(row, rows)]
        return remote(src, ref, sib_send.at[lane, step], sib_recv.at[lane, step], sibling)

    def pieces_of(beside, step):
        which = 1 - core if beside else core
        return [(k, block(me - towards * step, which), pl.ds(row, rows)) for k, (towards, row, rows) in enumerate(halves)]

    def taken(beside, step):
        slot = 2 * beside + lax.rem(step, 2)
        return [
            pltpu.make_async_copy(src.at[here, piece], dst.at[slot, piece], loads.at[slot, k, j])
            for k, here, piece in pieces_of(beside, step)
            for j, (src, dst) in enumerate(((all_ref, xs), (cot_ref, cs)))
        ]

    def given(beside, step):
        slot = 2 * beside + lax.rem(step, 2)
        return [
            pltpu.make_async_copy(src.at[slot, piece], dst.at[here, piece], stores.at[slot, k, j])
            for k, here, piece in pieces_of(beside, step)
            for j, (src, dst) in enumerate(((outs, out_ref), (gins, gin_ref)))
        ]

    def work(beside, step):
        slot = 2 * beside + lax.rem(step, 2)
        for copy in taken(beside, step):
            copy.wait()

        @pl.when(step > 1)
        def _():
            for copy in given(beside, step - 2):
                copy.wait()

        x, c = xs[slot], cs[slot]
        a = mm_nt(x, gate_ref[...])
        b = mm_nt(x, up_ref[...])
        sig = jax.nn.sigmoid(a)
        act = a * sig
        hidden = (act * b).astype(BF)
        grad_hidden = mm_nt(c, down_ref[...])
        grad_gate = (grad_hidden * b * (sig * (1.0 + a * (1.0 - sig)))).astype(BF)
        grad_up = (grad_hidden * act).astype(BF)
        outs[slot] = mm(hidden, down_ref[...]).astype(BF)
        gins[slot] = (mm(grad_gate, gate_ref[...]) + mm(grad_up, up_ref[...])).astype(BF)
        dg_ref[...] += mm_tn(grad_gate, x)
        du_ref[...] += mm_tn(grad_up, x)
        dd_ref[...] += mm_tn(hidden, c)
        for copy in given(beside, step):
            copy.start()

    local = pltpu.make_async_copy(row_ref, xs.at[3], own_sem)
    local.start()
    for lane in range(len(lanes)):
        ring_copy(lane, 0, row_ref).start()
    for lane in range(len(lanes)):
        sibling_copy(lane, 0, core, row_ref).start()
    swapped = [
        remote(swap_in[i], swap_out[i], swap_sem.at[0, i], swap_sem.at[1, i], across) for i in range(swaps)
    ]
    for copy in swapped:
        copy.start()
    dg_ref[...] = jnp.zeros_like(dg_ref)
    du_ref[...] = jnp.zeros_like(du_ref)
    dd_ref[...] = jnp.zeros_like(dd_ref)
    local.wait()
    local = pltpu.make_async_copy(xs.at[3], all_ref.at[block(me, core)], own_sem)
    local.start()
    local.wait()

    def pass_on(step, some):
        for lane in some:

            @pl.when(jnp.logical_and(step > 0, step < steps))
            def _(lane=lane):
                ring_copy(lane, step - 1).wait_recv()

            @pl.when(jnp.logical_and(step > 0, step < steps - 1))
            def _(lane=lane):
                ring_copy(lane, step).start()

            @pl.when(jnp.logical_and(step > 0, step < steps))
            def _(lane=lane):
                sibling_copy(lane, step, core).start()

    def one_step(step, carry):
        middle = len(lanes) // 2
        pass_on(step, range(middle))

        @pl.when(jnp.logical_and(step > 0, step <= steps))
        def _():
            work(0, step - 1)

        pass_on(step, range(middle, len(lanes)))

        @pl.when(step < steps)
        def _():
            for copy in taken(0, step):
                copy.start()

        @pl.when(jnp.logical_and(step > 0, step <= steps))
        def _():
            for lane in range(len(lanes)):
                sibling_copy(lane, step - 1, 1 - core).wait_recv()
            for copy in taken(1, step - 1):
                copy.start()

        @pl.when(step > 1)
        def _():
            work(1, step - 2)

        return carry

    lax.fori_loop(0, steps + 2, one_step, 0)
    for beside in range(2):
        for step in (steps - 2, steps - 1):
            for copy in given(beside, step):
                copy.wait()
    for lane in range(len(lanes)):
        for step in range(steps):
            if step < steps - 1:
                ring_copy(lane, step).wait_send()
            sibling_copy(lane, step, core).wait_send()
    for copy in swapped:
        copy.wait()


def gather_shared(rows, cot, shared, collective_id, swaps=(), pieces=2):
    nz = lax.axis_size("shard")
    lanes = ring_lanes([rows.shape], pieces)
    tokens, width = rows.shape
    hidden = shared[0].shape[0]
    blocks = jax.ShapeDtypeStruct((4 * nz, tokens, width), BF)
    anywhere, vmem = pl.BlockSpec(memory_space=pl.ANY), pl.BlockSpec(memory_space=pltpu.VMEM)
    return pl.pallas_call(
        functools.partial(gather_shared_kernel, nz, len(swaps), lanes),
        out_shape=[blocks] * 3
        + [jax.ShapeDtypeStruct((hidden, width), F32)] * 3
        + [jax.ShapeDtypeStruct(a.shape, a.dtype) for a in swaps],
        in_specs=[anywhere] * 2 + [vmem] * 3 + [anywhere] * len(swaps),
        out_specs=[anywhere] * 3 + [vmem] * 3 + [anywhere] * len(swaps),
        scratch_shapes=[pltpu.VMEM((4, tokens, width), BF)] * 4
        + [pltpu.SemaphoreType.DMA]
        + [pltpu.SemaphoreType.DMA((len(lanes), 2 * nz - 1))] * 2
        + [pltpu.SemaphoreType.DMA((len(lanes), 2 * nz))] * 2
        + [pltpu.SemaphoreType.DMA((4, 2, 2))] * 2
        + [pltpu.SemaphoreType.DMA((2, max(len(swaps), 1)))],
        compiler_params=pltpu.CompilerParams(
            collective_id=collective_id, has_side_effects=True, vmem_limit_bytes=56 * MIB
        ),
        cost_estimate=link_cost(4 * nz * rows.size * 2, 190e9),
        name="gather_shared",
    )(rows, cot, *shared, *swaps)


def ctx_neighbours():
    c = lax.axis_index("ctx")
    x, core = c // 2, c % 2
    return c, x, core, {"ctx": (1 - x) * 2 + core}, {"ctx": x * 2 + 1 - core}


def ctx_gather_kernel(nz, pieces, x_ref, t_ref, o_ref, u_ref, held, own_sem, send, recv, sib_send, sib_recv, *trade):
    c, x, core, across, sibling = ctx_neighbours()
    greet(trade_partners(nz))
    size = x_ref.shape[0] // pieces
    far = (1 - x) * 2 + core
    local = pltpu.make_async_copy(x_ref, held, own_sem)
    first, beside = [], []
    for k in range(pieces):
        piece = pl.ds(k * size, size)
        copy = remote(x_ref.at[piece], o_ref.at[c, piece], send.at[k], recv.at[k], across)
        copy.start()
        first.append(copy)
    copy = remote(x_ref, o_ref.at[c], sib_send.at[pieces], sib_recv.at[pieces], sibling)
    copy.start()
    beside.append(copy)
    local.start()
    kept, traded = trade_copies(nz, t_ref, u_ref, *trade)
    for copy in [kept] + traded:
        copy.start()
    local.wait()
    local = pltpu.make_async_copy(held, o_ref.at[c], own_sem)
    local.start()
    for k in range(pieces):
        piece = pl.ds(k * size, size)
        first[k].wait_recv()
        copy = remote(o_ref.at[far, piece], o_ref.at[far, piece], sib_send.at[k], sib_recv.at[k], sibling)
        copy.start()
        beside.append(copy)
    local.wait()
    for copy in first:
        copy.wait_send()
    for copy in beside + [kept] + traded:
        copy.wait()


def ctx_gather(array, trade, collective_id, pieces=4):
    nz = lax.axis_size("shard")
    return pl.pallas_call(
        functools.partial(ctx_gather_kernel, nz, pieces),
        out_shape=[
            jax.ShapeDtypeStruct((4,) + array.shape, array.dtype),
            jax.ShapeDtypeStruct(trade.shape, trade.dtype),
        ],
        in_specs=[pl.BlockSpec(memory_space=pl.ANY)] * 2,
        out_specs=[pl.BlockSpec(memory_space=pl.ANY)] * 2,
        scratch_shapes=[pltpu.VMEM(array.shape, array.dtype), pltpu.SemaphoreType.DMA]
        + [pltpu.SemaphoreType.DMA((pieces,))] * 2
        + [pltpu.SemaphoreType.DMA((pieces + 1,))] * 2
        + trade_semaphores(nz),
        compiler_params=pltpu.CompilerParams(collective_id=collective_id, has_side_effects=True),
        cost_estimate=link_cost(array.size * array.dtype.itemsize, 30e9),
        name="ctx_gather",
    )(array, trade)


def ctx_scatter_kernel(pieces, x_ref, o_ref, mine, theirs, came, own_sem, sib_send, sib_recv, send, recv):
    c, x, core, across, sibling = ctx_neighbours()
    greet((across, sibling))
    size = x_ref.shape[1] // pieces
    loads, shares, flying = {}, {}, []
    for turn in range(2):
        place = (1 - x if turn == 0 else x) * 2
        for k in range(pieces):
            piece = pl.ds(k * size, size)
            loads[turn, k] = pltpu.make_async_copy(
                x_ref.at[place + core, piece], mine.at[turn, piece], own_sem.at[turn, k]
            )
            shares[turn, k] = remote(
                x_ref.at[place + 1 - core, piece],
                theirs.at[turn, piece],
                sib_send.at[turn, k],
                sib_recv.at[turn, k],
                sibling,
            )
            loads[turn, k].start()
            shares[turn, k].start()
    for turn in range(2):
        for k in range(pieces):
            loads[turn, k].wait()
            shares[turn, k].wait_recv()
            if turn == 1:
                flying[k].wait_recv()

            @pl.loop(0, size // 16)
            def _(step, turn=turn, k=k):
                at = pl.ds(pl.multiple_of(k * size + step * 16, 16), 16)
                total = mine[turn, at, :].astype(F32) + theirs[turn, at, :].astype(F32)
                if turn == 0:
                    mine[turn, at, :] = total.astype(BF)
                else:
                    o_ref[at, :] = total + came[at, :].astype(F32)

            if turn == 0:
                piece = pl.ds(k * size, size)
                copy = remote(mine.at[0, piece], came.at[piece], send.at[k], recv.at[k], across)
                copy.start()
                flying.append(copy)
    for copy in flying:
        copy.wait_send()
    for copy in shares.values():
        copy.wait_send()


def ctx_scatter(array, collective_id, pieces=4):
    rows, width = array.shape[1:]
    return pl.pallas_call(
        functools.partial(ctx_scatter_kernel, pieces),
        out_shape=jax.ShapeDtypeStruct((rows, width), F32),
        in_specs=[pl.BlockSpec(memory_space=pl.ANY)],
        out_specs=pl.BlockSpec(memory_space=pltpu.VMEM),
        scratch_shapes=[
            pltpu.VMEM((2, rows, width), BF),
            pltpu.VMEM((2, rows, width), BF),
            pltpu.VMEM((rows, width), BF),
        ]
        + [pltpu.SemaphoreType.DMA((2, pieces))] * 3
        + [pltpu.SemaphoreType.DMA((pieces,))] * 2,
        compiler_params=pltpu.CompilerParams(
            collective_id=collective_id, has_side_effects=True, vmem_limit_bytes=32 * MIB
        ),
        cost_estimate=link_cost(array.size * array.dtype.itemsize, 120e9),
        name="ctx_scatter",
    )(array)


def scatter_kernel(nz, count, swaps, lanes, *refs):
    swap_in, swap_out = refs[count : count + swaps], refs[2 * count + swaps : 2 * (count + swaps)]
    swap_send, swap_recv = refs[-2:]
    refs = refs[:count] + refs[count + swaps : 2 * count + swaps] + refs[2 * (count + swaps) : -2]
    ins, outs = refs[:count], refs[count : 2 * count]
    mine, theirs, came = (refs[(2 + k) * count : (3 + k) * count] for k in range(3))
    own_sem, sib_send, sib_recv, send, recv = refs[5 * count :]
    me, core, right, left, sibling = ring_neighbours(nz)
    across = {"tp": 1 - lax.axis_index("tp")}
    greet((right, left, sibling) + ((across,) if swaps else ()))
    swapped = [remote(swap_in[i], swap_out[i], swap_send.at[i], swap_recv.at[i], across) for i in range(swaps)]
    steps = 2 * nz

    def block(place, which):
        z, x = ring_at(nz, place)
        return z * 4 + x * 2 + which

    loads, shares = {}, {}
    for step in range(steps):
        for lane, (i, towards, row, rows) in enumerate(lanes):
            place = me - towards * (1 + step)
            piece = pl.ds(row, rows)
            load = pltpu.make_async_copy(
                ins[i].at[block(place, core), piece], mine[i].at[step, piece], own_sem.at[lane, step]
            )
            load.start()
            loads[lane, step] = load
            share = remote(
                ins[i].at[block(place, 1 - core), piece],
                theirs[i].at[step, piece],
                sib_send.at[lane, step],
                sib_recv.at[lane, step],
                sibling,
            )
            share.start()
            shares[lane, step] = share
    for copy in swapped:
        copy.start()
    flying = {}
    for step in range(steps):
        for lane, (i, towards, row, rows) in enumerate(lanes):
            loads[lane, step].wait()
            shares[lane, step].wait_recv()
            if step > 0:
                flying[lane, step - 1].wait_recv()

            @pl.loop(0, rows // 16)
            def _(turn, i=i, row=row, step=step):
                at = pl.ds(pl.multiple_of(row + turn * 16, 16), 16)
                total = mine[i][step, at, :].astype(F32) + theirs[i][step, at, :].astype(F32)
                if step > 0:
                    total = total + came[i][step - 1, at, :].astype(F32)
                if step < steps - 1:
                    mine[i][step, at, :] = total.astype(BF)
                else:
                    outs[i][at, :] = total

            if step < steps - 1:
                piece = pl.ds(row, rows)
                copy = remote(
                    mine[i].at[step, piece],
                    came[i].at[step, piece],
                    send.at[lane, step],
                    recv.at[lane, step],
                    right if towards > 0 else left,
                )
                copy.start()
                flying[lane, step] = copy
    for copy in flying.values():
        copy.wait_send()
    for copy in shares.values():
        copy.wait_send()
    for copy in swapped:
        copy.wait()


def ring_scatter(arrays, collective_id, pieces=2, swaps=(), rate=190e9):
    nz = lax.axis_size("shard")
    shapes = [a.shape[1:] for a in arrays]
    lanes = ring_lanes(shapes, pieces)
    count, steps = len(arrays), 2 * nz
    buffers = [
        pltpu.VMEM((size,) + shape, BF) for size in (steps, steps, steps - 1) for shape in shapes
    ]
    return pl.pallas_call(
        functools.partial(scatter_kernel, nz, count, len(swaps), lanes),
        out_shape=[jax.ShapeDtypeStruct(shape, F32) for shape in shapes]
        + [jax.ShapeDtypeStruct(a.shape, a.dtype) for a in swaps],
        in_specs=[pl.BlockSpec(memory_space=pl.ANY)] * (count + len(swaps)),
        out_specs=[pl.BlockSpec(memory_space=pltpu.VMEM)] * count
        + [pl.BlockSpec(memory_space=pl.ANY)] * len(swaps),
        scratch_shapes=buffers
        + [pltpu.SemaphoreType.DMA((len(lanes), steps))] * 3
        + [pltpu.SemaphoreType.DMA((len(lanes), steps - 1))] * 2
        + [pltpu.SemaphoreType.DMA((max(len(swaps), 1),))] * 2,
        compiler_params=pltpu.CompilerParams(
            collective_id=collective_id, has_side_effects=True, vmem_limit_bytes=56 * MIB
        ),
        cost_estimate=link_cost(sum(a.size * a.dtype.itemsize for a in arrays), rate),
        name="ring_scatter",
    )(*arrays, *swaps)


def turn(values, tables):
    cosine, first, second = tables
    return values * cosine + pltpu.roll(values, 96, 1) * first + pltpu.roll(values, 32, 1) * second


def turn_tables(positions):
    sines, cosines = angles(positions)
    nothing = jnp.zeros_like(sines)
    return (
        jnp.concatenate([cosines] * 4, 1),
        jnp.concatenate([-sines, nothing] * 2, 1),
        jnp.concatenate([nothing, sines] * 2, 1),
    )


def project_kernel(heads, x_ref, gain, kv_gain, w_ref, cosine, first, second, *outs):
    low_ref, q_ref, latent_ref, compressed_ref, one_ref, kv_ref = outs
    x = x_ref[...].astype(F32)
    inverse = lax.rsqrt(jnp.mean(x * x, -1, keepdims=True) + EPS)
    low = (x * inverse * gain[...]).astype(BF)
    low_ref[...] = low
    one_ref[...] = inverse
    tables = cosine[...], first[...], second[...]
    nope, rope = heads * NOPE, heads * ROPE
    q_ref[:, :nope] = mm(low, w_ref[:, :nope]).astype(BF)
    raw = mm(low, w_ref[:, nope : nope + rope])
    for k in range(rope // 128):
        q_ref[:, nope + k * 128 : nope + (k + 1) * 128] = turn(raw[:, k * 128 : (k + 1) * 128], tables).astype(BF)
    raw = mm(low, w_ref[:, nope + rope :])
    compressed = raw[:, :R]
    inverse = lax.rsqrt(jnp.mean(compressed * compressed, -1, keepdims=True) + EPS)
    compressed_ref[...] = compressed
    kv_ref[...] = inverse
    latent_ref[:, :R] = (compressed * inverse * kv_gain[...]).astype(BF)
    latent_ref[:, R:] = turn(raw[:, R:], tables).astype(BF)


def project(x, gain, kv_gain, weights, tables, heads):
    rows, width = x.shape
    tile = 128
    columns = heads * (NOPE + ROPE)
    by_row = lambda n: pl.BlockSpec((tile, n), lambda i: (i, 0))
    whole = lambda a: pl.BlockSpec(a.shape, lambda i: (0, 0))
    return pl.pallas_call(
        functools.partial(project_kernel, heads),
        out_shape=(
            jax.ShapeDtypeStruct((rows, width), BF),
            jax.ShapeDtypeStruct((rows, columns), BF),
            jax.ShapeDtypeStruct((rows, R + 128), BF),
            jax.ShapeDtypeStruct((rows, R), F32),
            jax.ShapeDtypeStruct((rows, 1), F32),
            jax.ShapeDtypeStruct((rows, 1), F32),
        ),
        grid=(rows // tile,),
        in_specs=[by_row(width), whole(gain), whole(kv_gain), whole(weights)] + [by_row(128)] * 3,
        out_specs=[by_row(width), by_row(columns), by_row(R + 128), by_row(R), by_row(1), by_row(1)],
        compiler_params=pltpu.CompilerParams(vmem_limit_bytes=48 * MIB),
        cost_estimate=pl.CostEstimate(
            flops=2 * rows * width * weights.shape[1], bytes_accessed=20 * MIB, transcendentals=0
        ),
        name="project",
    )(x, gain, kv_gain, weights, *tables)


def head_key(kv_ref, rope_ref, k):
    rope = rope_ref[...]
    if k:
        rope = pltpu.roll(rope.astype(F32), ROPE, 1).astype(BF)
    return jnp.concatenate([kv_ref[:, k * HEAD : k * HEAD + NOPE], rope], 1)


def attend_kernel(scale, qn_ref, qr_ref, kv_ref, rope_ref, seg_q, seg_k, o_ref, l_ref):
    rows, keys = qn_ref.shape[0], kv_ref.shape[0]
    at_q = lax.axis_index("ctx") * rows + lax.broadcasted_iota(jnp.int32, (rows, keys), 0)
    at_k = lax.broadcasted_iota(jnp.int32, (rows, keys), 1)
    visible = (seg_q[...] == seg_k[...]) & (at_k <= at_q)
    for k in range(2):
        query = jnp.concatenate([qn_ref[:, k * NOPE : (k + 1) * NOPE], qr_ref[...]], 1)
        scores = jnp.where(visible, scale * mm_nt(query, head_key(kv_ref, rope_ref, k)), -1e30)
        peak = jnp.max(scores, -1, keepdims=True)
        weights = jnp.exp(scores - peak)
        total = jnp.sum(weights, -1, keepdims=True)
        values = kv_ref[:, k * HEAD + NOPE : (k + 1) * HEAD]
        o_ref[:, k * V : (k + 1) * V] = (mm(weights.astype(BF), values) * (1.0 / total)).astype(BF)
        l_ref[k] = peak + jnp.log(total)


def attend(query, expanded, rope, seg_q, seg_k, scale):
    rows, keys = query.shape[0], expanded.shape[0]
    heads = query.shape[1] // (NOPE + ROPE)
    return pl.pallas_call(
        functools.partial(attend_kernel, scale),
        out_shape=(
            jax.ShapeDtypeStruct((rows, heads * V), BF),
            jax.ShapeDtypeStruct((heads, rows, 1), F32),
        ),
        grid=(heads // 2,),
        in_specs=[
            pl.BlockSpec((rows, 2 * NOPE), lambda h: (0, h)),
            pl.BlockSpec((rows, 2 * ROPE), lambda h: (0, heads + h)),
            pl.BlockSpec((keys, 2 * HEAD), lambda h: (0, h)),
            pl.BlockSpec((keys, 128), lambda h: (0, R // 128)),
            pl.BlockSpec((rows, 1), lambda h: (0, 0)),
            pl.BlockSpec((1, keys), lambda h: (0, 0)),
        ],
        out_specs=[
            pl.BlockSpec((rows, 2 * V), lambda h: (0, h)),
            pl.BlockSpec((2, rows, 1), lambda h: (h, 0, 0)),
        ],
        compiler_params=pltpu.CompilerParams(vmem_limit_bytes=60 * MIB),
        cost_estimate=pl.CostEstimate(
            flops=2 * heads * rows * keys * 384, bytes_accessed=12 * MIB, transcendentals=heads * rows * keys
        ),
        name="attend",
    )(query, query, expanded, rope, seg_q, seg_k)


def attend_back_kernel(
    scale, qn_ref, qr_ref, kv_ref, rope_ref, g_ref, l_ref, seg_q, seg_k, expand_ref, cosine, first, second,
    dqn_ref, dqr_ref, dkv_ref, dl_ref, comp_acc, rope_acc,
):
    pair, last = pl.program_id(0), pl.num_programs(0) - 1
    rows, keys = qn_ref.shape[0], kv_ref.shape[0]
    at_k = lax.broadcasted_iota(jnp.int32, (keys, rows), 0)
    at_q = lax.axis_index("ctx") * rows + lax.broadcasted_iota(jnp.int32, (keys, rows), 1)
    visible = (seg_q[...] == seg_k[...]) & (at_k <= at_q)
    grad_ropes, grad_turned = [], None
    for k in range(2):
        key = head_key(kv_ref, rope_ref, k)
        query = jnp.concatenate([qn_ref[:, k * NOPE : (k + 1) * NOPE], qr_ref[...]], 1)
        grad = g_ref[:, k * V : (k + 1) * V]
        scores = scale * mm_nt(key, query)
        probs = jnp.exp(jnp.where(visible, scores, -1e30) - l_ref[k])
        grad_probs = mm_nt(kv_ref[:, k * HEAD + NOPE : (k + 1) * HEAD], grad)
        mean = jnp.sum(probs * grad_probs, 0, keepdims=True)
        grad_scores = (probs * (grad_probs - mean)).astype(BF)
        dkv_ref[:, k * HEAD + NOPE : (k + 1) * HEAD] = mm(probs.astype(BF), grad).astype(BF)
        grad_key = scale * mm(grad_scores, query)
        dkv_ref[:, k * HEAD : k * HEAD + NOPE] = grad_key[:, :NOPE].astype(BF)
        grad_ropes.append(grad_key[:, NOPE:])
        grad_query = scale * mm_tn(grad_scores, key)
        dqn_ref[:, k * NOPE : (k + 1) * NOPE] = grad_query[:, :NOPE].astype(BF)
        grad_turned = grad_query[:, NOPE:] if k == 0 else grad_turned + grad_query[:, NOPE:]
    dqr_ref[...] = turn(grad_turned, (cosine[...], -first[...], -second[...])).astype(BF)
    lane = lax.broadcasted_iota(jnp.int32, (keys, 128), 1)
    grad_rope = jnp.where(lane < ROPE, grad_ropes[0] + pltpu.roll(grad_ropes[1], ROPE, 1), 0.0)
    grad_comp = mm_nt(dkv_ref[...], expand_ref[...])

    @pl.when(pair == 0)
    def _():
        rope_acc[...] = grad_rope
        comp_acc[...] = grad_comp

    @pl.when(pair > 0)
    def _():
        rope_acc[...] += grad_rope
        comp_acc[...] += grad_comp

    @pl.when(pair == last)
    def _():
        dl_ref[:, :R] = comp_acc[...].astype(BF)
        dl_ref[:, R:] = rope_acc[...].astype(BF)


def attend_back(query, expanded, rope, grad, logs, seg_q, seg_k, expand, tables, scale):
    rows, keys = query.shape[0], expanded.shape[0]
    heads = query.shape[1] // (NOPE + ROPE)
    one = lambda shape: pl.BlockSpec(shape, lambda h: (0, 0))
    return pl.pallas_call(
        functools.partial(attend_back_kernel, scale),
        out_shape=(
            jax.ShapeDtypeStruct((rows, heads * NOPE), BF),
            jax.ShapeDtypeStruct((rows, heads * ROPE), BF),
            jax.ShapeDtypeStruct((keys, heads * (NOPE + V)), BF),
            jax.ShapeDtypeStruct((keys, R + 128), BF),
        ),
        grid=(heads // 2,),
        in_specs=[
            pl.BlockSpec((rows, 2 * NOPE), lambda h: (0, h)),
            pl.BlockSpec((rows, 2 * ROPE), lambda h: (0, heads + h)),
            pl.BlockSpec((keys, 2 * HEAD), lambda h: (0, h)),
            pl.BlockSpec((keys, 128), lambda h: (0, R // 128)),
            pl.BlockSpec((rows, 2 * V), lambda h: (0, h)),
            pl.BlockSpec((2, 1, rows), lambda h: (h, 0, 0)),
            one((1, rows)),
            one((keys, 1)),
            pl.BlockSpec((R, 2 * HEAD), lambda h: (0, h)),
        ]
        + [one((rows, 128))] * 3,
        out_specs=[
            pl.BlockSpec((rows, 2 * NOPE), lambda h: (0, h)),
            pl.BlockSpec((rows, 2 * ROPE), lambda h: (0, h)),
            pl.BlockSpec((keys, 2 * HEAD), lambda h: (0, h)),
            one((keys, R + 128)),
        ],
        scratch_shapes=[pltpu.VMEM((keys, R), F32), pltpu.VMEM((keys, 128), F32)],
        compiler_params=pltpu.CompilerParams(vmem_limit_bytes=60 * MIB),
        cost_estimate=pl.CostEstimate(
            flops=2 * heads * rows * keys * 1536, bytes_accessed=24 * MIB, transcendentals=heads * rows * keys
        ),
        name="attend_back",
    )(query, query, expanded, rope, grad, logs, seg_q, seg_k, expand, *tables)


def project_back_kernel(
    gn_ref, gr_ref, gl_ref, compressed_ref, kv_ref, gain, cosine, first, second, w_ref, sum_ref, grad_ref, gain_ref
):
    upstream = gl_ref[:, :R]
    compressed, inverse = compressed_ref[...], kv_ref[...]
    scaled = upstream * gain[...]
    mean = jnp.mean(scaled * compressed, -1, keepdims=True)
    grad = inverse * scaled - compressed * (inverse * inverse * inverse * mean)
    gains = jnp.sum(upstream * compressed * inverse, 0, keepdims=True)
    nope, rope = gn_ref.shape[1], gr_ref.shape[1]
    start = nope + rope
    grad_ref[:, :nope] = gn_ref[...]
    grad_ref[:, nope:start] = gr_ref[...]
    grad_ref[:, start : start + R] = grad.astype(BF)
    grad_ref[:, start + R :] = turn(gl_ref[:, R:], (cosine[...], -first[...], -second[...])).astype(BF)
    sum_ref[...] = mm_nt(grad_ref[...], w_ref[...]).astype(BF)

    @pl.when(pl.program_id(0) == 0)
    def _():
        gain_ref[...] = gains

    @pl.when(pl.program_id(0) > 0)
    def _():
        gain_ref[...] += gains


def project_back(grad_nope, grad_turned, grad_latent, compressed, inverse_kv, kv_gain, tables, weights):
    rows, columns = grad_nope.shape[0], weights.shape[1]
    width, tile = weights.shape[0], 128
    by_row = lambda n: pl.BlockSpec((tile, n), lambda i: (i, 0))
    whole = lambda a, **mode: pl.BlockSpec(a.shape, lambda i: (0, 0), **mode)
    return pl.pallas_call(
        project_back_kernel,
        out_shape=(
            jax.ShapeDtypeStruct((rows, width), BF),
            jax.ShapeDtypeStruct((rows, columns), BF),
            jax.ShapeDtypeStruct((1, R), F32),
        ),
        grid=(rows // tile,),
        in_specs=[
            by_row(grad_nope.shape[1]),
            by_row(grad_turned.shape[1]),
            by_row(R + 128),
            by_row(R),
            by_row(1),
            whole(kv_gain),
        ]
        + [by_row(128)] * 3
        + [whole(weights, pipeline_mode=pl.Buffered(1))],
        out_specs=[by_row(width), by_row(columns), pl.BlockSpec((1, R), lambda i: (0, 0))],
        compiler_params=pltpu.CompilerParams(vmem_limit_bytes=48 * MIB),
        cost_estimate=pl.CostEstimate(
            flops=2 * rows * width * columns, bytes_accessed=20 * MIB, transcendentals=0
        ),
        name="project_back",
    )(grad_nope, grad_turned, grad_latent, compressed, inverse_kv, kv_gain, *tables, weights)


TILE = 256


def pack_kernel(pair_tile, pair_block, pair_first, pair_on, rank, share, x_ref, o_ref, w_ref, *, weighted):
    i = pl.program_id(0)
    tokens = rank.shape[2]

    @pl.when(pair_on[i] == 1)
    def _():
        slot = pair_tile[i] * TILE + lax.broadcasted_iota(jnp.int32, (TILE, tokens), 0)
        chosen = rank[0] == slot
        rows = mm(chosen.astype(F32).astype(BF), x_ref[0])
        weight = jnp.sum(jnp.where(chosen, share[0], 0.0), 1, keepdims=True)
        if weighted:
            rows = rows * weight
        rows = rows.astype(BF)

        @pl.when(pair_first[i] == 1)
        def _():
            o_ref[...] = rows
            w_ref[...] = weight

        @pl.when(pair_first[i] == 0)
        def _():
            o_ref[...] += rows
            w_ref[...] += weight


def pack(pairs, rank, share, x, weighted):
    (blocks, _, tokens), width = rank.shape, x.shape[2]
    slots = blocks * tokens
    return pl.pallas_call(
        functools.partial(pack_kernel, weighted=weighted),
        out_shape=(
            jax.ShapeDtypeStruct((slots, width), BF),
            jax.ShapeDtypeStruct((slots, 1), F32),
        ),
        grid_spec=pltpu.PrefetchScalarGridSpec(
            num_scalar_prefetch=4,
            grid=(pairs["tile"].shape[0],),
            in_specs=[
                pl.BlockSpec((1, 1, tokens), lambda i, t, b, f, a: (b[i], 0, 0)),
                pl.BlockSpec((1, 1, tokens), lambda i, t, b, f, a: (b[i], 0, 0)),
                pl.BlockSpec((1, tokens, width), lambda i, t, b, f, a: (b[i], 0, 0)),
            ],
            out_specs=[
                pl.BlockSpec((TILE, width), lambda i, t, b, f, a: (t[i], 0)),
                pl.BlockSpec((TILE, 1), lambda i, t, b, f, a: (t[i], 0)),
            ],
        ),
        compiler_params=pltpu.CompilerParams(vmem_limit_bytes=40 * MIB),
        cost_estimate=pl.CostEstimate(
            flops=2 * 24 * TILE * tokens * width, bytes_accessed=28 * MIB, transcendentals=0
        ),
        name="pack",
    )(pairs["tile"], pairs["block"], pairs["first_tile"], pairs["on"], rank, share, x)


def expert_kernel(parts, tiles, x_ref, g_ref, w_ref, *refs):
    given, (out_ref, gin_ref, hid, gg, gu, gate, up, down, sem) = refs[: 3 * parts], refs[3 * parts :]
    size, room = given[0].shape[0], gate.shape[0] // parts

    @pl.when(pl.program_id(0) == 0)
    def _():
        copies = [
            pltpu.make_async_copy(given[k * parts + p], held.at[pl.ds(p * room, size)], sem.at[k, p])
            for k, held in enumerate((gate, up, down))
            for p in range(parts)
        ]
        for copy in copies:
            copy.start()
        if room > size:
            for held in (gate, up, down):
                for p in range(parts):
                    held[pl.ds(p * room + size, room - size), :] = jnp.zeros((room - size, held.shape[1]), BF)
        for copy in copies:
            copy.wait()

    @pl.when(pl.program_id(0) < tiles[0])
    def _():
        x, g = x_ref[...], g_ref[...]
        a = mm_nt(x, gate[...])
        b = mm_nt(x, up[...])
        grad_hidden = mm_nt(g, down[...])
        sig = jax.nn.sigmoid(a)
        act = a * sig
        hidden = (act * b).astype(BF)
        hid[...] = hidden
        out_ref[...] = (mm(hidden, down[...]) * w_ref[...]).astype(BF)
        grad_gate = (grad_hidden * b * (sig * (1.0 + a * (1.0 - sig)))).astype(BF)
        grad_up = (grad_hidden * act).astype(BF)
        gg[...] = grad_gate
        gu[...] = grad_up
        gin_ref[...] = (mm(grad_gate, gate[...]) + mm(grad_up, up[...])).astype(BF)


def experts(tiles, x, g, w, gates, ups, downs):
    slots, width = x.shape
    parts, hidden = len(gates), gates[0].shape[0]
    room = -(-hidden // 128) * 128
    row = lambda i, t: (jnp.minimum(i, t[0] - 1), 0)
    anywhere = pl.BlockSpec(memory_space=pl.ANY)
    return pl.pallas_call(
        functools.partial(expert_kernel, parts),
        out_shape=(jax.ShapeDtypeStruct((slots, width), BF),) * 2
        + (jax.ShapeDtypeStruct((slots, parts * room), BF),) * 3,
        grid_spec=pltpu.PrefetchScalarGridSpec(
            num_scalar_prefetch=1,
            grid=(slots // TILE,),
            in_specs=[
                pl.BlockSpec((TILE, width), row),
                pl.BlockSpec((TILE, width), row),
                pl.BlockSpec((TILE, 1), row),
            ]
            + [anywhere] * (3 * parts),
            out_specs=[pl.BlockSpec((TILE, width), row)] * 2
            + [pl.BlockSpec((TILE, parts * room), row)] * 3,
            scratch_shapes=[pltpu.VMEM((parts * room, width), BF)] * 3 + [pltpu.SemaphoreType.DMA((3, parts))],
        ),
        compiler_params=pltpu.CompilerParams(vmem_limit_bytes=60 * MIB),
        cost_estimate=pl.CostEstimate(
            flops=12 * 2560 * width * parts * hidden, bytes_accessed=100 * MIB, transcendentals=0
        ),
        name="experts",
    )(tiles, x, g, w, *gates, *ups, *downs)


def expert_sums(tiles, x_ref, g_ref, hid_ref, gg_ref, gu_ref, sums):
    @pl.when(pl.program_id(0) < tiles[0])
    def _():
        x, g = x_ref[...], g_ref[...]
        size = sums[0].shape[0]
        sums[0][...] += mm_tn(gg_ref[:, :size], x)
        sums[1][...] += mm_tn(gu_ref[:, :size], x)
        sums[2][...] += mm_tn(hid_ref[:, :size], g)


def expert_sums_kernel(tiles, x_ref, g_ref, hid_ref, gg_ref, gu_ref, *refs):
    outs, sums = refs[:3], refs[3:]

    @pl.when(pl.program_id(0) == 0)
    def _():
        for total in sums:
            total[...] = jnp.zeros_like(total)

    expert_sums(tiles, x_ref, g_ref, hid_ref, gg_ref, gu_ref, sums)

    @pl.when(pl.program_id(0) == pl.num_programs(0) - 1)
    def _():
        for out, total in zip(outs, sums):
            out[...] = total[...].astype(out.dtype)


def expert_totals_kernel(tiles, x_ref, g_ref, hid_ref, gg_ref, gu_ref, *refs):
    starts, outs = refs[:3], refs[3:]

    @pl.when(pl.program_id(0) == 0)
    def _():
        for out, start in zip(outs, starts):
            out[...] = start[...].astype(F32)

    expert_sums(tiles, x_ref, g_ref, hid_ref, gg_ref, gu_ref, outs)


def expert_grads(tiles, x, g, hid, gg, gu, part, hidden, starts=None):
    slots, width = x.shape
    room = -(-hidden // 128) * 128
    row = lambda i, t: (jnp.minimum(i, t[0] - 1), 0)
    column = lambda i, t: (jnp.minimum(i, t[0] - 1), part)
    whole = lambda i, t: (0, 0)
    once = pl.Buffered(1)
    kernel = expert_sums_kernel if starts is None else expert_totals_kernel
    held = [pl.BlockSpec((hidden, width), whole, pipeline_mode=once)] * 3
    return pl.pallas_call(
        kernel,
        out_shape=(jax.ShapeDtypeStruct((hidden, width), BF if starts is None else F32),) * 3,
        grid_spec=pltpu.PrefetchScalarGridSpec(
            num_scalar_prefetch=1,
            grid=(slots // TILE,),
            in_specs=[pl.BlockSpec((TILE, width), row)] * 2
            + [pl.BlockSpec((TILE, room), column)] * 3
            + (held if starts is not None else []),
            out_specs=held,
            scratch_shapes=[pltpu.VMEM((hidden, width), F32)] * 3 if starts is None else [],
        ),
        compiler_params=pltpu.CompilerParams(vmem_limit_bytes=60 * MIB),
        cost_estimate=pl.CostEstimate(
            flops=6 * 2560 * width * hidden, bytes_accessed=40 * MIB, transcendentals=0
        ),
        name="expert_grads",
    )(tiles, x, g, hid, gg, gu, *(starts or ()))


def dense_kernel(
    pair_tile, pair_block, pair_first, pair_last, pair_real, rank, x_ref, c_ref, out_ref, gin_ref, total_ref, grad_ref, acc, gacc
):
    i = pl.program_id(0)

    @pl.when(pair_first[i] == 1)
    def _():
        acc[...] = x_ref[0].astype(F32)
        gacc[...] = c_ref[0].astype(F32)

    @pl.when(pair_real[i] == 1)
    def _():
        tokens = rank.shape[1]
        slot = pair_tile[i] * TILE + lax.broadcasted_iota(jnp.int32, (tokens, TILE), 1)
        chosen = (rank[0] == slot).astype(F32).astype(BF)
        acc[...] += mm(chosen, out_ref[...])
        gacc[...] += mm(chosen, gin_ref[...])

    @pl.when(pair_last[i] == 1)
    def _():
        total_ref[0] = acc[...].astype(BF)
        grad_ref[0] = gacc[...].astype(BF)


def dense(pairs, rank_column, shared_out, shared_gin, out, gin):
    blocks, tokens, width = shared_out.shape
    by_block = lambda i, t, b, f, l, r: (b[i], 0, 0)
    by_tile = lambda i, t, b, f, l, r: (t[i], 0)
    return pl.pallas_call(
        dense_kernel,
        out_shape=(jax.ShapeDtypeStruct((blocks, tokens, width), BF),) * 2,
        grid_spec=pltpu.PrefetchScalarGridSpec(
            num_scalar_prefetch=5,
            grid=(pairs["tile"].shape[0],),
            in_specs=[
                pl.BlockSpec((1, tokens, 1), by_block),
                pl.BlockSpec((1, tokens, width), by_block),
                pl.BlockSpec((1, tokens, width), by_block),
                pl.BlockSpec((TILE, width), by_tile),
                pl.BlockSpec((TILE, width), by_tile),
            ],
            out_specs=[pl.BlockSpec((1, tokens, width), by_block)] * 2,
            scratch_shapes=[pltpu.VMEM((tokens, width), F32)] * 2,
        ),
        compiler_params=pltpu.CompilerParams(vmem_limit_bytes=60 * MIB),
        cost_estimate=pl.CostEstimate(
            flops=4 * 26 * TILE * tokens * width, bytes_accessed=90 * MIB, transcendentals=0
        ),
        name="dense",
    )(
        pairs["tile"], pairs["block"], pairs["first_block"], pairs["last_block"], pairs["real"],
        rank_column, shared_out, shared_gin, out, gin,
    )


def routing(share):
    blocks, tokens = share.shape
    used = (share > 0).astype(F32)
    upper = (jnp.arange(tokens)[:, None] <= jnp.arange(tokens)[None, :]).astype(BF)
    inside = mm(used.astype(BF), upper).astype(jnp.int32)
    counts = inside[:, -1]
    lower = jnp.arange(blocks)[:, None] > jnp.arange(blocks)[None, :]
    start = jnp.sum(jnp.where(lower, counts[None, :], 0), 1)
    end = start + counts
    rank = jnp.where(share > 0, start[:, None] + inside - 1, -1)
    last_tile = blocks * tokens // TILE - 1
    first = jnp.minimum(start // TILE, last_tile)
    last = jnp.where(counts > 0, (end - 1) // TILE, first)
    spans = last - first + 1
    after = jnp.sum(jnp.where(lower | jnp.eye(blocks, dtype=bool), spans[None, :], 0), 1)
    size = blocks + blocks * tokens // TILE
    turn = jnp.arange(size)
    all_pairs = after[-1]
    on = turn < all_pairs
    place = jnp.minimum(turn, all_pairs - 1)
    block = jnp.sum((after[None, :] <= place[:, None]).astype(jnp.int32), 1)
    pick = block[:, None] == jnp.arange(blocks)[None, :]
    take = lambda v: jnp.sum(jnp.where(pick, v[None, :], 0), 1)
    tile = take(first) + place - take(after - spans)
    shifted = lambda v: jnp.concatenate([jnp.full((1,), -1, v.dtype), v[:-1]])
    as_int = lambda v: v.astype(jnp.int32)
    pairs = {
        "tile": as_int(tile),
        "block": as_int(block),
        "on": as_int(on),
        "real": as_int(on & (take(counts) > 0)),
        "first_tile": as_int(on & (shifted(tile) != tile)),
        "first_block": as_int(on & (shifted(block) != block)),
        "last_block": as_int(on & (place == take(after) - 1)),
    }
    tiles = as_int(jnp.maximum((end[-1] + TILE - 1) // TILE, 1))[None]
    return rank.astype(jnp.int32), pairs, tiles


def other_half_sum(rows, product, beside):
    parts, me = lax.axis_size("tp"), lax.axis_index("tp")
    size = rows.shape[0] // parts
    if parts != 2:
        summed = lax.psum_scatter(product(rows).astype(BF), "tp", scatter_dimension=0, tiled=True)
        return summed.astype(F32), beside
    sent = product(lax.dynamic_slice_in_dim(rows, (1 - me) * size, size)).astype(BF)
    came, beside = lax.optimization_barrier((lax.ppermute(sent, "tp", [(0, 1), (1, 0)]), beside))
    return product(lax.dynamic_slice_in_dim(rows, me * size, size)) + came.astype(F32), beside


def swap_tp(v):
    return lax.ppermute(v, "tp", [(0, 1), (1, 0)])


def join_tp(v, came=None):
    if lax.axis_size("tp") != 2:
        return lax.all_gather(v, "tp", axis=0, tiled=True)
    came = swap_tp(v) if came is None else came
    return jnp.where(lax.axis_index("tp") == 0, jnp.stack([v, came]), jnp.stack([came, v])).reshape(
        (2 * v.shape[0],) + v.shape[1:]
    )


def on_device(
    inputs,
    segments,
    routes,
    gate_share,
    cotangent,
    attn_gain,
    kv_gain,
    ffn_gain,
    w_query,
    w_latent,
    w_expand,
    w_output,
    w_shared_gate,
    w_shared_up,
    w_shared_down,
    expert_gate,
    expert_up,
    expert_down,
):
    tokens, width = inputs.shape
    parts, part = lax.axis_size("tp"), lax.axis_index("tp")
    half = tokens // parts
    group = lax.axis_size(GROUP)
    me = lax.axis_index(GROUP)
    ctx = lax.axis_size("ctx")
    query_width = w_query.shape[1]
    heads = query_width // (NOPE + ROPE)
    scale = (NOPE + ROPE) ** (-0.5)
    own_half = lambda v: lax.dynamic_slice_in_dim(v, part * half, half)

    gain_row = jnp.concatenate([attn_gain, kv_gain, ffn_gain])
    n_attn, n_kv = attn_gain.shape[0], kv_gain.shape[0]
    gain_rows = jnp.zeros((16, 384), BF).at[0, : gain_row.shape[0]].set(gain_row)
    by_head = w_query.reshape(-1, heads, NOPE + ROPE)
    first_weights = jnp.concatenate(
        [
            by_head[..., :NOPE].reshape(-1, heads * NOPE),
            by_head[..., NOPE:].reshape(-1, heads * ROPE),
            w_latent,
            jnp.zeros((w_latent.shape[0], 128 - ROPE), BF),
        ],
        1,
    )
    expert_ids = jnp.arange(group, dtype=jnp.int32)
    shares = jnp.sum(
        jnp.where(own_half(routes).T[None] == expert_ids[:, None, None], own_half(gate_share).T[None], 0.0), 1
    )
    gate, up, down = (jnp.swapaxes(expert_gate[0], 0, 1), jnp.swapaxes(expert_up[0], 0, 1), expert_down[0])
    together = lax.optimization_barrier
    piece = w_shared_gate.shape[1] // group
    depth = w_shared_gate.shape[0]
    cut = lambda v: v.reshape(group, piece, depth)
    shared_sent = jnp.concatenate(
        [cut(jnp.swapaxes(w_shared_gate, 0, 1)), cut(jnp.swapaxes(w_shared_up, 0, 1)), cut(w_shared_down)], 1
    )
    first = ring_gather(
        [
            first_weights,
            jnp.swapaxes(w_output, 0, 1),
            w_expand,
            gain_rows,
            shares,
            jnp.broadcast_to(segments[None], (16, tokens)),
        ],
        1,
        swaps=[gate] if parts == 2 else [],
    )
    first_full, output_full, expand_full, gains, share, all_segments = first[:6]
    expand_full = expand_full.reshape(R, -1)
    output_full = output_full.reshape(width, -1)
    attn_scale = gains[:, 0, :n_attn].reshape(-1).astype(F32)
    kv_scale = gains[:, 0, n_attn : n_attn + n_kv].reshape(-1).astype(F32)
    ffn_scale = gains[:, 0, n_attn + n_kv : gain_row.shape[0]].reshape(-1).astype(F32)
    first_full = first_full.reshape(width, -1)
    all_segments = lax.dynamic_slice_in_dim(
        all_segments[:, 0], lax.axis_index("shard") * ctx, ctx
    ).reshape(-1)
    share = lax.dynamic_index_in_dim(share, me, 1, keepdims=False)
    rank, pairs, tiles = routing(share)

    cot_half = jnp.concatenate([own_half(cotangent), jnp.zeros((8, width), BF)], 0)
    cot_all = lax.all_gather(together((cot_half, gains))[0], GROUP, axis=0, tiled=False)
    if parts == 2:
        up_other = swap_tp(together((up, gains))[0])

    residual = inputs.astype(F32)
    start = lax.axis_index("ctx") * tokens
    tables = turn_tables(start + jnp.arange(tokens, dtype=jnp.int32))
    attn_low, query_low, latent_low, compressed, inverse_one, inverse_kv = project(
        inputs, attn_scale[None], kv_scale[None], first_full, tables, heads
    )
    all_latent, shared_own = ctx_gather(latent_low, shared_sent, 5)
    all_latent = all_latent.reshape(ctx * tokens, -1)
    shared_own = jnp.swapaxes(shared_own, 0, 1).reshape(3 * piece, width)
    expanded = mm(all_latent[:, :R], expand_full).astype(BF)
    if parts == 2:
        expanded, shared_own, up_other = together((expanded, shared_own, up_other))
        shared_parts = [shared_own, swap_tp(shared_own)]
    else:
        shared_parts = list(lax.all_gather(shared_own, "tp", axis=0, tiled=False))
    attended, logs = attend(query_low, expanded, all_latent, segments[:, None], all_segments[None, :], scale)
    attended, shared_parts = together((attended, shared_parts))
    shared = [
        jnp.concatenate([v[k * piece : (k + 1) * piece] for v in shared_parts], 0) for k in range(3)
    ]
    rank_row, share_row = rank[:, None, :], share[:, None, :]
    packed_grads = pack(pairs, rank_row, share_row, cot_all, True)
    attended_sum, (grad_rows, weights) = other_half_sum(
        attended, lambda rows: mm_nt(rows, output_full), packed_grads
    )
    middle = own_half(residual) + attended_sum
    normed_two, inverse_two = norm_forward(middle, ffn_scale)
    ffn_low = normed_two.astype(BF)

    if parts == 2:
        rows_all, shared_out, shared_gin, *shared_grads, down_other = gather_shared(
            ffn_low, cot_all, shared, 2, swaps=[down]
        )
        gates, ups, downs = [gate, first[6]], [up, up_other], [down, down_other]
    else:
        rows_all, shared_out, shared_gin, *shared_grads = gather_shared(ffn_low, cot_all, shared, 2)
        gates, ups, downs = (list(lax.all_gather(v, "tp", axis=0, tiled=False)) for v in (gate, up, down))
    rows_in, _ = pack(pairs, rank_row, share_row, rows_all, False)

    shared_back = [
        jnp.concatenate([v[k * piece : (k + 1) * piece] for v in shared_grads], 0) for k in range(parts)
    ]
    if parts == 2:
        shared_came = swap_tp(shared_back[1].astype(BF))
        rows_in, shared_came = together((rows_in, shared_came))
        shared_back = shared_back[0] + shared_came.astype(F32)
    else:
        shared_back = lax.psum_scatter(jnp.stack(shared_back).astype(BF), "tp", scatter_dimension=0, tiled=False)
    shared_back = lax.all_gather(shared_back.astype(BF), GROUP, axis=0, tiled=False)
    expert_out, expert_gin, *kept = experts(tiles, rows_in, grad_rows, weights, gates, ups, downs)

    grads_of = lambda which, *starts: expert_grads(
        tiles, rows_in, grad_rows, *kept, which, gate.shape[0], *starts
    )
    if parts == 2:
        expert_out, sent = together((expert_out, grads_of(1)))
        came = [swap_tp(v) for v in sent]
    moe_part, grad_part = dense(
        pairs, rank[:, :, None], shared_out, shared_gin, expert_out, expert_gin
    )
    grad_part, shared_back = together((grad_part, shared_back))
    shared_back = lax.dynamic_slice_in_dim(shared_back, me * depth, depth, 2)
    (grad_normed_two,) = ring_scatter([grad_part], 3)
    if parts == 2:
        grad_normed_two, came = together((grad_normed_two, came))
    if parts != 2:
        sent = [grads_of(k) for k in range(parts)]
        own_grads = [
            lax.psum_scatter(jnp.stack(v), "tp", scatter_dimension=0, tiled=False).astype(F32) for v in zip(*sent)
        ]

    grad_out = own_half(cotangent).astype(F32)
    grad_mid_norm, ffn_gain_grad = norm_backward(middle, inverse_two, ffn_scale, grad_normed_two)
    grad_middle = grad_out + grad_mid_norm
    grad_middle_low = join_tp(grad_middle.astype(BF))
    moe_part = lax.optimization_barrier((moe_part, grad_normed_two))[0]
    moe_total = lax.psum_scatter(
        moe_part, GROUP, scatter_dimension=0, tiled=False
    )

    grad_attended = mm(grad_middle_low, output_full).astype(BF)
    grad_nope, grad_turned, grad_kv, grad_latent = attend_back(
        query_low, expanded, all_latent, grad_attended, jnp.swapaxes(logs, 1, 2),
        segments[None, :], all_segments[:, None], expand_full, tables, scale,
    )
    grad_latent = ctx_scatter(grad_latent.reshape(ctx, tokens, -1), 6)
    grad_normed_one, grad_first, kv_gain_grad = project_back(
        grad_nope, grad_turned, grad_latent, compressed, inverse_kv, kv_scale[None], tables, first_full
    )
    if parts == 2:
        grad_normed_came = swap_tp(lax.dynamic_slice_in_dim(grad_normed_one, (1 - part) * half, half))
        (grad_middle_low, attended, all_latent, grad_kv, came), grad_normed_one = together(
            ((grad_middle_low, attended, all_latent, grad_kv, came), grad_normed_one)
        )
        own_grads, grad_normed_came = together((grads_of(0, tuple(came)), grad_normed_came))
        grad_normed_one = own_half(grad_normed_one).astype(F32) + grad_normed_came.astype(F32)
    else:
        grad_normed_one = lax.psum_scatter(grad_normed_one, "tp", scatter_dimension=0, tiled=True).astype(F32)
    gate_grad, up_grad, down_grad = (
        jnp.swapaxes(own_grads[0], 0, 1)[None], jnp.swapaxes(own_grads[1], 0, 1)[None], own_grads[2][None]
    )
    first_grad = mm_tn(attn_low, grad_first).astype(BF)
    output_grad = mm_tn(grad_middle_low, attended).astype(BF)
    expand_grad = mm_tn(all_latent[:, :R], grad_kv).astype(BF)
    grad_in_norm, attn_gain_grad = norm_backward(
        own_half(residual), own_half(inverse_one), attn_scale, grad_normed_one
    )
    grad_inputs = (grad_middle + grad_in_norm).astype(BF)

    gain_grads = jnp.concatenate(
        [v.reshape(group, -1) for v in (attn_gain_grad, kv_gain_grad[0], ffn_gain_grad)], 1
    ).astype(BF)
    tail = jnp.zeros((group, 16, 384), BF).at[:, 0, : gain_grads.shape[1]].set(gain_grads)
    moe_total, tail = together((moe_total, tail))
    result = (middle + moe_total.astype(F32)).astype(BF)
    first_own, output_own, expand_own, gains_own, *came = ring_scatter(
        [
            first_grad.reshape(group, -1, first_grad.shape[1]),
            output_grad.reshape(group, -1, output_grad.shape[1]),
            expand_grad.reshape(group, -1, expand_grad.shape[1]),
            tail,
        ],
        4,
        pieces=1,
        swaps=[grad_inputs, result] if parts == 2 else [],
    )
    grad_inputs, result = join_tp(grad_inputs, *came[:1]), join_tp(result, *came[1:])
    output_own = jnp.swapaxes(output_own, 0, 1)
    back = [shared_back[:, k * piece : (k + 1) * piece].reshape(-1, depth).astype(F32) for k in range(3)]
    sgate_grad, sup_grad, sdown_grad = jnp.swapaxes(back[0], 0, 1), jnp.swapaxes(back[1], 0, 1), back[2]
    nopes = first_own[:, : heads * NOPE].reshape(-1, heads, NOPE)
    query_own = jnp.concatenate([nopes, first_own[:, heads * NOPE : query_width].reshape(-1, heads, ROPE)], -1)
    query_own = query_own.reshape(-1, query_width)
    latent_own = first_own[:, query_width : query_width + R + ROPE]
    if parts == 2:
        small = jnp.concatenate([latent_own.reshape(-1, 128), gains_own[:8].reshape(-1, 128)], 0)
        small = small + swap_tp(small)
        latent_own = small[: -gains_own[:8].size // 128].reshape(latent_own.shape)
        gains_own = small[-gains_own[:8].size // 128 :].reshape(8, -1)[0]
    else:
        latent_own, gains_own = lax.psum((latent_own, gains_own[0]), "tp")
    return (
        result,
        grad_inputs.astype(F32),
        gains_own[:n_attn],
        gains_own[n_attn : n_attn + n_kv],
        gains_own[n_attn + n_kv : gain_row.shape[0]],
        query_own,
        latent_own,
        expand_own,
        output_own,
        sgate_grad,
        sup_grad,
        sdown_grad,
        gate_grad,
        up_grad,
        down_grad,
    )


def solution(mesh):
    group = P(GROUP)
    rows = P(GROUP, None)
    both = P(GROUP, "tp")
    turned = P("tp", GROUP)
    return jax.shard_map(
        on_device,
        mesh=mesh,
        in_specs=(
            rows, group, rows, rows, rows, group, group, group,
            both, rows, both, turned, both, both, turned,
            P(GROUP, None, "tp"), P(GROUP, None, "tp"), P(GROUP, "tp", None),
        ),
        out_specs=(
            rows, rows, group, group, group,
            both, rows, both, turned, both, both, turned,
            P(GROUP, None, "tp"), P(GROUP, None, "tp"), P(GROUP, "tp", None),
        ),
        check_vma=False,
    )
```

```python
import functools

import jax
import jax.numpy as jnp
from jax import lax
from jax.experimental import pallas as pl
from jax.experimental.pallas import tpu as pltpu
from jax.sharding import PartitionSpec as P

NOPE = 128
ROPE = 64
V = 128
R = 512
HEAD = 256
EPS = 1e-06
GROUP = ("shard", "ctx")
MESH = pl.DeviceIdType.MESH
BF = jnp.bfloat16
F32 = jnp.float32
MIB = 1 << 20


def norm_forward(values, gain):
    inverse = lax.rsqrt(jnp.mean(values * values, -1, keepdims=True) + EPS)
    return (values * inverse * gain, inverse)


def norm_backward(values, inverse, gain, upstream):
    scaled = upstream * gain
    gain_grad = jnp.sum(upstream * values * inverse, 0)
    value_grad = inverse * scaled - values * inverse**3 * jnp.mean(
        scaled * values, -1, keepdims=True
    )
    return (value_grad, gain_grad)


def angles(positions):
    half_width = ROPE // 2
    freq_table = 10000.0 ** (-jnp.arange(half_width, dtype=F32) / half_width)
    turned = positions.astype(F32)[:, None] * freq_table[None, :]
    return (jnp.sin(turned), jnp.cos(turned))


def mm(a, b):
    return jnp.dot(a, b, preferred_element_type=F32)


def mm_nt(a, b):
    return lax.dot_general(a, b, (((1,), (1,)), ((), ())), preferred_element_type=F32)


def mm_tn(a, b):
    return lax.dot_general(a, b, (((0,), (0,)), ((), ())), preferred_element_type=F32)


def ring_place(nz):
    z = lax.axis_index("shard")
    c = lax.axis_index("ctx")
    x, core = c // 2, c % 2
    return jnp.where(x == 0, z, 2 * nz - 1 - z), x, core


def ring_at(nz, p):
    p = lax.rem(p + 4 * nz, 2 * nz)
    return jnp.where(p < nz, p, 2 * nz - 1 - p), p // nz


def ring_lanes(shapes, pieces):
    lanes = []
    for index, (rows, _) in enumerate(shapes):
        first = -(-rows // 32) * 16
        ways = []
        for towards, start, size in ((1, 0, first), (-1, first, rows - first)):
            units = size // 16
            parts = min(pieces, units)
            way, at = [], start
            for part in range(parts):
                here = 16 * (units // parts + (1 if part < units % parts else 0))
                way.append((index, towards, at, here))
                at += here
            ways.append(way)
        for part in range(pieces):
            lanes += [way[part] for way in ways if part < len(way)]
    return lanes


def greet(devices):
    barrier = pltpu.get_barrier_semaphore()
    for device in devices:
        pl.semaphore_signal(barrier, inc=1, device_id=device, device_id_type=MESH)
    pl.semaphore_wait(barrier, len(devices))


def ring_neighbours(nz):
    me, x, core = ring_place(nz)
    zr, xr = ring_at(nz, me + 1)
    zl, xl = ring_at(nz, me - 1)
    right = {"shard": zr, "ctx": xr * 2 + core}
    left = {"shard": zl, "ctx": xl * 2 + core}
    sibling = {"ctx": x * 2 + 1 - core}
    return me, core, right, left, sibling


def link_cost(size, rate):
    return pl.CostEstimate(flops=int(size / rate * 9e14), bytes_accessed=2 * size, transcendentals=0)


def remote(src, dst, send, recv, device):
    return pltpu.make_async_remote_copy(
        src_ref=src, dst_ref=dst, send_sem=send, recv_sem=recv, device_id=device, device_id_type=MESH
    )


def ring_semaphores(nz, count, lanes):
    return (
        [pltpu.SemaphoreType.DMA((count,))]
        + [pltpu.SemaphoreType.DMA((len(lanes), 2 * nz - 1))] * 2
        + [pltpu.SemaphoreType.DMA((len(lanes), 2 * nz))] * 2
    )


def ring_steps(nz, lanes, ins, outs, me, core, right, left, sibling, own_sem, send, recv, sib_send, sib_recv):
    steps = 2 * nz

    def block(place, which):
        z, x = ring_at(nz, place)
        return z * 4 + x * 2 + which

    own = block(me, core)
    local = [pltpu.make_async_copy(a, b.at[own], own_sem.at[i]) for i, (a, b) in enumerate(zip(ins, outs))]
    flying = []
    last = {}
    for step in range(steps):
        for lane, (i, towards, row, rows) in enumerate(lanes):
            here = block(me - towards * step, core)
            piece = pl.ds(row, rows)
            if step > 0:
                last[lane].wait_recv()
            src = ins[i].at[piece] if step == 0 else outs[i].at[here, piece]
            dst = outs[i].at[here, piece]
            if step < steps - 1:
                copy = remote(
                    src, dst, send.at[lane, step], recv.at[lane, step], right if towards > 0 else left
                )
                copy.start()
                last[lane] = copy
                flying.append((copy, False))
            copy = remote(src, dst, sib_send.at[lane, step], sib_recv.at[lane, step], sibling)
            copy.start()
            flying.append((copy, True))
        if step == 0:
            for copy in local:
                copy.start()
        yield
    for copy in local:
        copy.wait()
    for copy, both in flying:
        copy.wait_send()
        if both:
            copy.wait_recv()


def trade_copies(nz, x_ref, o_ref, own_sem, send, recv):
    devices = 4 * nz
    me = lax.axis_index("shard") * 4 + lax.axis_index("ctx")
    local = pltpu.make_async_copy(x_ref.at[me], o_ref.at[me], own_sem)
    copies = []
    for shift in range(1, devices):
        there = lax.rem(me + shift, devices)
        device = {"shard": there // 4, "ctx": lax.rem(there, 4)}
        copies.append(remote(x_ref.at[there], o_ref.at[me], send.at[shift - 1], recv.at[shift - 1], device))
    return local, copies


def trade_partners(nz):
    devices = 4 * nz
    me = lax.axis_index("shard") * 4 + lax.axis_index("ctx")
    there = [lax.rem(me + shift, devices) for shift in range(1, devices)]
    return tuple({"shard": t // 4, "ctx": lax.rem(t, 4)} for t in there)


def trade_semaphores(nz):
    return [pltpu.SemaphoreType.DMA] + [pltpu.SemaphoreType.DMA((4 * nz - 1,))] * 2


def gather_kernel(nz, count, swaps, lanes, *refs):
    total = count + swaps
    ins, outs = refs[:total], refs[total : 2 * total]
    *ring, swap_send, swap_recv = refs[2 * total :]
    me, core, right, left, sibling = ring_neighbours(nz)
    across = {"tp": 1 - lax.axis_index("tp")}
    greet((right, left, sibling) + ((across,) if swaps else ()))
    swapped = [
        remote(ins[count + i], outs[count + i], swap_send.at[i], swap_recv.at[i], across) for i in range(swaps)
    ]
    for step, _ in enumerate(ring_steps(nz, lanes, ins[:count], outs[:count], me, core, right, left, sibling, *ring)):
        if step == 0:
            for copy in swapped:
                copy.start()
    for copy in swapped:
        copy.wait()


def ring_gather(arrays, collective_id, pieces=2, swaps=()):
    nz = lax.axis_size("shard")
    lanes = ring_lanes([a.shape for a in arrays], pieces)
    given = [*arrays, *swaps]
    count, total = len(arrays), len(given)
    return pl.pallas_call(
        functools.partial(gather_kernel, nz, count, len(swaps), lanes),
        out_shape=[jax.ShapeDtypeStruct((4 * nz,) + a.shape, a.dtype) for a in arrays]
        + [jax.ShapeDtypeStruct(a.shape, a.dtype) for a in swaps],
        in_specs=[pl.BlockSpec(memory_space=pl.ANY)] * total,
        out_specs=[pl.BlockSpec(memory_space=pl.ANY)] * total,
        scratch_shapes=ring_semaphores(nz, count, lanes)
        + [pltpu.SemaphoreType.DMA((max(len(swaps), 1),))] * 2,
        compiler_params=pltpu.CompilerParams(collective_id=collective_id, has_side_effects=True),
        cost_estimate=link_cost(4 * nz * sum(a.size * a.dtype.itemsize for a in arrays), 190e9),
        name="ring_gather",
    )(*given)


def gather_shared_kernel(
    nz, swaps, lanes, row_ref, cot_ref, gate_ref, up_ref, down_ref, *refs
):
    swap_in, refs = refs[:swaps], refs[swaps:]
    all_ref, out_ref, gin_ref, dg_ref, du_ref, dd_ref, *refs = refs
    swap_out, refs = refs[:swaps], refs[swaps:]
    xs, cs, outs, gins, own_sem, send, recv, sib_send, sib_recv, loads, stores, swap_sem = refs
    me, core, right, left, sibling = ring_neighbours(nz)
    across = {"tp": 1 - lax.axis_index("tp")}
    greet((right, left, sibling) + ((across,) if swaps else ()))
    steps = 2 * nz
    first = sum(rows for _, towards, _, rows in lanes if towards > 0)
    total = row_ref.shape[0]
    halves = ((1, 0, first), (-1, first, total - first))

    def block(place, which):
        z, x = ring_at(nz, place)
        return z * 4 + x * 2 + which

    def ring_copy(lane, step, src=None):
        _, towards, row, rows = lanes[lane]
        ref = all_ref.at[block(me - towards * step, core), pl.ds(row, rows)]
        src = ref if src is None else src.at[pl.ds(row, rows)]
        return remote(src, ref, send.at[lane, step], recv.at[lane, step], right if towards > 0 else left)

    def sibling_copy(lane, step, which, src=None):
        _, towards, row, rows = lanes[lane]
        ref = all_ref.at[block(me - towards * step, which), pl.ds(row, rows)]
        src = ref if src is None else src.at[pl.ds(row, rows)]
        return remote(src, ref, sib_send.at[lane, step], sib_recv.at[lane, step], sibling)

    def pieces_of(beside, step):
        which = 1 - core if beside else core
        return [(k, block(me - towards * step, which), pl.ds(row, rows)) for k, (towards, row, rows) in enumerate(halves)]

    def taken(beside, step):
        slot = 2 * beside + lax.rem(step, 2)
        return [
            pltpu.make_async_copy(src.at[here, piece], dst.at[slot, piece], loads.at[slot, k, j])
            for k, here, piece in pieces_of(beside, step)
            for j, (src, dst) in enumerate(((all_ref, xs), (cot_ref, cs)))
        ]

    def given(beside, step):
        slot = 2 * beside + lax.rem(step, 2)
        return [
            pltpu.make_async_copy(src.at[slot, piece], dst.at[here, piece], stores.at[slot, k, j])
            for k, here, piece in pieces_of(beside, step)
            for j, (src, dst) in enumerate(((outs, out_ref), (gins, gin_ref)))
        ]

    def work(beside, step):
        slot = 2 * beside + lax.rem(step, 2)
        for copy in taken(beside, step):
            copy.wait()

        @pl.when(step > 1)
        def _():
            for copy in given(beside, step - 2):
                copy.wait()

        x, c = xs[slot], cs[slot]
        a = mm_nt(x, gate_ref[...])
        b = mm_nt(x, up_ref[...])
        sig = jax.nn.sigmoid(a)
        act = a * sig
        hidden = (act * b).astype(BF)
        grad_hidden = mm_nt(c, down_ref[...])
        grad_gate = (grad_hidden * b * (sig * (1.0 + a * (1.0 - sig)))).astype(BF)
        grad_up = (grad_hidden * act).astype(BF)
        outs[slot] = mm(hidden, down_ref[...]).astype(BF)
        gins[slot] = (mm(grad_gate, gate_ref[...]) + mm(grad_up, up_ref[...])).astype(BF)
        dg_ref[...] += mm_tn(grad_gate, x)
        du_ref[...] += mm_tn(grad_up, x)
        dd_ref[...] += mm_tn(hidden, c)
        for copy in given(beside, step):
            copy.start()

    local = pltpu.make_async_copy(row_ref, xs.at[3], own_sem)
    local.start()
    for lane in range(len(lanes)):
        ring_copy(lane, 0, row_ref).start()
    for lane in range(len(lanes)):
        sibling_copy(lane, 0, core, row_ref).start()
    swapped = [
        remote(swap_in[i], swap_out[i], swap_sem.at[0, i], swap_sem.at[1, i], across) for i in range(swaps)
    ]
    for copy in swapped:
        copy.start()
    dg_ref[...] = jnp.zeros_like(dg_ref)
    du_ref[...] = jnp.zeros_like(du_ref)
    dd_ref[...] = jnp.zeros_like(dd_ref)
    local.wait()
    local = pltpu.make_async_copy(xs.at[3], all_ref.at[block(me, core)], own_sem)
    local.start()
    local.wait()

    def pass_on(step, some):
        for lane in some:

            @pl.when(jnp.logical_and(step > 0, step < steps))
            def _(lane=lane):
                ring_copy(lane, step - 1).wait_recv()

            @pl.when(jnp.logical_and(step > 0, step < steps - 1))
            def _(lane=lane):
                ring_copy(lane, step).start()

            @pl.when(jnp.logical_and(step > 0, step < steps))
            def _(lane=lane):
                sibling_copy(lane, step, core).start()

    def one_step(step, carry):
        middle = len(lanes) // 2
        pass_on(step, range(middle))

        @pl.when(jnp.logical_and(step > 0, step <= steps))
        def _():
            work(0, step - 1)

        pass_on(step, range(middle, len(lanes)))

        @pl.when(step < steps)
        def _():
            for copy in taken(0, step):
                copy.start()

        @pl.when(jnp.logical_and(step > 0, step <= steps))
        def _():
            for lane in range(len(lanes)):
                sibling_copy(lane, step - 1, 1 - core).wait_recv()
            for copy in taken(1, step - 1):
                copy.start()

        @pl.when(step > 1)
        def _():
            work(1, step - 2)

        return carry

    lax.fori_loop(0, steps + 2, one_step, 0)
    for beside in range(2):
        for step in (steps - 2, steps - 1):
            for copy in given(beside, step):
                copy.wait()
    for lane in range(len(lanes)):
        for step in range(steps):
            if step < steps - 1:
                ring_copy(lane, step).wait_send()
            sibling_copy(lane, step, core).wait_send()
    for copy in swapped:
        copy.wait()


def gather_shared(rows, cot, shared, collective_id, swaps=(), pieces=2):
    nz = lax.axis_size("shard")
    lanes = ring_lanes([rows.shape], pieces)
    tokens, width = rows.shape
    hidden = shared[0].shape[0]
    blocks = jax.ShapeDtypeStruct((4 * nz, tokens, width), BF)
    anywhere, vmem = pl.BlockSpec(memory_space=pl.ANY), pl.BlockSpec(memory_space=pltpu.VMEM)
    return pl.pallas_call(
        functools.partial(gather_shared_kernel, nz, len(swaps), lanes),
        out_shape=[blocks] * 3
        + [jax.ShapeDtypeStruct((hidden, width), F32)] * 3
        + [jax.ShapeDtypeStruct(a.shape, a.dtype) for a in swaps],
        in_specs=[anywhere] * 2 + [vmem] * 3 + [anywhere] * len(swaps),
        out_specs=[anywhere] * 3 + [vmem] * 3 + [anywhere] * len(swaps),
        scratch_shapes=[pltpu.VMEM((4, tokens, width), BF)] * 4
        + [pltpu.SemaphoreType.DMA]
        + [pltpu.SemaphoreType.DMA((len(lanes), 2 * nz - 1))] * 2
        + [pltpu.SemaphoreType.DMA((len(lanes), 2 * nz))] * 2
        + [pltpu.SemaphoreType.DMA((4, 2, 2))] * 2
        + [pltpu.SemaphoreType.DMA((2, max(len(swaps), 1)))],
        compiler_params=pltpu.CompilerParams(
            collective_id=collective_id, has_side_effects=True, vmem_limit_bytes=56 * MIB
        ),
        cost_estimate=link_cost(4 * nz * rows.size * 2, 190e9),
        name="gather_shared",
    )(rows, cot, *shared, *swaps)


def ctx_neighbours():
    c = lax.axis_index("ctx")
    x, core = c // 2, c % 2
    return c, x, core, {"ctx": (1 - x) * 2 + core}, {"ctx": x * 2 + 1 - core}


def ctx_gather_kernel(nz, pieces, x_ref, t_ref, o_ref, u_ref, held, own_sem, send, recv, sib_send, sib_recv, *trade):
    c, x, core, across, sibling = ctx_neighbours()
    greet(trade_partners(nz))
    size = x_ref.shape[0] // pieces
    far = (1 - x) * 2 + core
    local = pltpu.make_async_copy(x_ref, held, own_sem)
    first, beside = [], []
    for k in range(pieces):
        piece = pl.ds(k * size, size)
        copy = remote(x_ref.at[piece], o_ref.at[c, piece], send.at[k], recv.at[k], across)
        copy.start()
        first.append(copy)
    copy = remote(x_ref, o_ref.at[c], sib_send.at[pieces], sib_recv.at[pieces], sibling)
    copy.start()
    beside.append(copy)
    local.start()
    kept, traded = trade_copies(nz, t_ref, u_ref, *trade)
    for copy in [kept] + traded:
        copy.start()
    local.wait()
    local = pltpu.make_async_copy(held, o_ref.at[c], own_sem)
    local.start()
    for k in range(pieces):
        piece = pl.ds(k * size, size)
        first[k].wait_recv()
        copy = remote(o_ref.at[far, piece], o_ref.at[far, piece], sib_send.at[k], sib_recv.at[k], sibling)
        copy.start()
        beside.append(copy)
    local.wait()
    for copy in first:
        copy.wait_send()
    for copy in beside + [kept] + traded:
        copy.wait()


def ctx_gather(array, trade, collective_id, pieces=4):
    nz = lax.axis_size("shard")
    return pl.pallas_call(
        functools.partial(ctx_gather_kernel, nz, pieces),
        out_shape=[
            jax.ShapeDtypeStruct((4,) + array.shape, array.dtype),
            jax.ShapeDtypeStruct(trade.shape, trade.dtype),
        ],
        in_specs=[pl.BlockSpec(memory_space=pl.ANY)] * 2,
        out_specs=[pl.BlockSpec(memory_space=pl.ANY)] * 2,
        scratch_shapes=[pltpu.VMEM(array.shape, array.dtype), pltpu.SemaphoreType.DMA]
        + [pltpu.SemaphoreType.DMA((pieces,))] * 2
        + [pltpu.SemaphoreType.DMA((pieces + 1,))] * 2
        + trade_semaphores(nz),
        compiler_params=pltpu.CompilerParams(collective_id=collective_id, has_side_effects=True),
        cost_estimate=link_cost(array.size * array.dtype.itemsize, 30e9),
        name="ctx_gather",
    )(array, trade)


def ctx_scatter_kernel(pieces, x_ref, o_ref, mine, theirs, came, own_sem, sib_send, sib_recv, send, recv):
    c, x, core, across, sibling = ctx_neighbours()
    greet((across, sibling))
    size = x_ref.shape[1] // pieces
    loads, shares, flying = {}, {}, []
    for turn in range(2):
        place = (1 - x if turn == 0 else x) * 2
        for k in range(pieces):
            piece = pl.ds(k * size, size)
            loads[turn, k] = pltpu.make_async_copy(
                x_ref.at[place + core, piece], mine.at[turn, piece], own_sem.at[turn, k]
            )
            shares[turn, k] = remote(
                x_ref.at[place + 1 - core, piece],
                theirs.at[turn, piece],
                sib_send.at[turn, k],
                sib_recv.at[turn, k],
                sibling,
            )
            loads[turn, k].start()
            shares[turn, k].start()
    for turn in range(2):
        for k in range(pieces):
            loads[turn, k].wait()
            shares[turn, k].wait_recv()
            if turn == 1:
                flying[k].wait_recv()

            @pl.loop(0, size // 16)
            def _(step, turn=turn, k=k):
                at = pl.ds(pl.multiple_of(k * size + step * 16, 16), 16)
                total = mine[turn, at, :].astype(F32) + theirs[turn, at, :].astype(F32)
                if turn == 0:
                    mine[turn, at, :] = total.astype(BF)
                else:
                    o_ref[at, :] = total + came[at, :].astype(F32)

            if turn == 0:
                piece = pl.ds(k * size, size)
                copy = remote(mine.at[0, piece], came.at[piece], send.at[k], recv.at[k], across)
                copy.start()
                flying.append(copy)
    for copy in flying:
        copy.wait_send()
    for copy in shares.values():
        copy.wait_send()


def ctx_scatter(array, collective_id, pieces=4):
    rows, width = array.shape[1:]
    return pl.pallas_call(
        functools.partial(ctx_scatter_kernel, pieces),
        out_shape=jax.ShapeDtypeStruct((rows, width), F32),
        in_specs=[pl.BlockSpec(memory_space=pl.ANY)],
        out_specs=pl.BlockSpec(memory_space=pltpu.VMEM),
        scratch_shapes=[
            pltpu.VMEM((2, rows, width), BF),
            pltpu.VMEM((2, rows, width), BF),
            pltpu.VMEM((rows, width), BF),
        ]
        + [pltpu.SemaphoreType.DMA((2, pieces))] * 3
        + [pltpu.SemaphoreType.DMA((pieces,))] * 2,
        compiler_params=pltpu.CompilerParams(
            collective_id=collective_id, has_side_effects=True, vmem_limit_bytes=32 * MIB
        ),
        cost_estimate=link_cost(array.size * array.dtype.itemsize, 120e9),
        name="ctx_scatter",
    )(array)


def scatter_kernel(nz, count, swaps, lanes, *refs):
    swap_in, swap_out = refs[count : count + swaps], refs[2 * count + swaps : 2 * (count + swaps)]
    swap_send, swap_recv = refs[-2:]
    refs = refs[:count] + refs[count + swaps : 2 * count + swaps] + refs[2 * (count + swaps) : -2]
    ins, outs = refs[:count], refs[count : 2 * count]
    mine, theirs, came = (refs[(2 + k) * count : (3 + k) * count] for k in range(3))
    own_sem, sib_send, sib_recv, send, recv = refs[5 * count :]
    me, core, right, left, sibling = ring_neighbours(nz)
    across = {"tp": 1 - lax.axis_index("tp")}
    greet((right, left, sibling) + ((across,) if swaps else ()))
    swapped = [remote(swap_in[i], swap_out[i], swap_send.at[i], swap_recv.at[i], across) for i in range(swaps)]
    steps = 2 * nz

    def block(place, which):
        z, x = ring_at(nz, place)
        return z * 4 + x * 2 + which

    loads, shares = {}, {}
    for step in range(steps):
        for lane, (i, towards, row, rows) in enumerate(lanes):
            place = me - towards * (1 + step)
            piece = pl.ds(row, rows)
            load = pltpu.make_async_copy(
                ins[i].at[block(place, core), piece], mine[i].at[step, piece], own_sem.at[lane, step]
            )
            load.start()
            loads[lane, step] = load
            share = remote(
                ins[i].at[block(place, 1 - core), piece],
                theirs[i].at[step, piece],
                sib_send.at[lane, step],
                sib_recv.at[lane, step],
                sibling,
            )
            share.start()
            shares[lane, step] = share
    for copy in swapped:
        copy.start()
    flying = {}
    for step in range(steps):
        for lane, (i, towards, row, rows) in enumerate(lanes):
            loads[lane, step].wait()
            shares[lane, step].wait_recv()
            if step > 0:
                flying[lane, step - 1].wait_recv()

            @pl.loop(0, rows // 16)
            def _(turn, i=i, row=row, step=step):
                at = pl.ds(pl.multiple_of(row + turn * 16, 16), 16)
                total = mine[i][step, at, :].astype(F32) + theirs[i][step, at, :].astype(F32)
                if step > 0:
                    total = total + came[i][step - 1, at, :].astype(F32)
                if step < steps - 1:
                    mine[i][step, at, :] = total.astype(BF)
                else:
                    outs[i][at, :] = total

            if step < steps - 1:
                piece = pl.ds(row, rows)
                copy = remote(
                    mine[i].at[step, piece],
                    came[i].at[step, piece],
                    send.at[lane, step],
                    recv.at[lane, step],
                    right if towards > 0 else left,
                )
                copy.start()
                flying[lane, step] = copy
    for copy in flying.values():
        copy.wait_send()
    for copy in shares.values():
        copy.wait_send()
    for copy in swapped:
        copy.wait()


def ring_scatter(arrays, collective_id, pieces=2, swaps=(), rate=190e9):
    nz = lax.axis_size("shard")
    shapes = [a.shape[1:] for a in arrays]
    lanes = ring_lanes(shapes, pieces)
    count, steps = len(arrays), 2 * nz
    buffers = [
        pltpu.VMEM((size,) + shape, BF) for size in (steps, steps, steps - 1) for shape in shapes
    ]
    return pl.pallas_call(
        functools.partial(scatter_kernel, nz, count, len(swaps), lanes),
        out_shape=[jax.ShapeDtypeStruct(shape, F32) for shape in shapes]
        + [jax.ShapeDtypeStruct(a.shape, a.dtype) for a in swaps],
        in_specs=[pl.BlockSpec(memory_space=pl.ANY)] * (count + len(swaps)),
        out_specs=[pl.BlockSpec(memory_space=pltpu.VMEM)] * count
        + [pl.BlockSpec(memory_space=pl.ANY)] * len(swaps),
        scratch_shapes=buffers
        + [pltpu.SemaphoreType.DMA((len(lanes), steps))] * 3
        + [pltpu.SemaphoreType.DMA((len(lanes), steps - 1))] * 2
        + [pltpu.SemaphoreType.DMA((max(len(swaps), 1),))] * 2,
        compiler_params=pltpu.CompilerParams(
            collective_id=collective_id, has_side_effects=True, vmem_limit_bytes=56 * MIB
        ),
        cost_estimate=link_cost(sum(a.size * a.dtype.itemsize for a in arrays), rate),
        name="ring_scatter",
    )(*arrays, *swaps)


def turn(values, tables):
    cosine, first, second = tables
    return values * cosine + pltpu.roll(values, 96, 1) * first + pltpu.roll(values, 32, 1) * second


def turn_tables(positions):
    sines, cosines = angles(positions)
    nothing = jnp.zeros_like(sines)
    return (
        jnp.concatenate([cosines] * 4, 1),
        jnp.concatenate([-sines, nothing] * 2, 1),
        jnp.concatenate([nothing, sines] * 2, 1),
    )


def project_kernel(heads, x_ref, gain, kv_gain, w_ref, cosine, first, second, *outs):
    low_ref, q_ref, latent_ref, compressed_ref, one_ref, kv_ref = outs
    x = x_ref[...].astype(F32)
    inverse = lax.rsqrt(jnp.mean(x * x, -1, keepdims=True) + EPS)
    low = (x * inverse * gain[...]).astype(BF)
    low_ref[...] = low
    one_ref[...] = inverse
    tables = cosine[...], first[...], second[...]
    nope, rope = heads * NOPE, heads * ROPE
    q_ref[:, :nope] = mm(low, w_ref[:, :nope]).astype(BF)
    raw = mm(low, w_ref[:, nope : nope + rope])
    for k in range(rope // 128):
        q_ref[:, nope + k * 128 : nope + (k + 1) * 128] = turn(raw[:, k * 128 : (k + 1) * 128], tables).astype(BF)
    raw = mm(low, w_ref[:, nope + rope :])
    compressed = raw[:, :R]
    inverse = lax.rsqrt(jnp.mean(compressed * compressed, -1, keepdims=True) + EPS)
    compressed_ref[...] = compressed
    kv_ref[...] = inverse
    latent_ref[:, :R] = (compressed * inverse * kv_gain[...]).astype(BF)
    latent_ref[:, R:] = turn(raw[:, R:], tables).astype(BF)


def project(x, gain, kv_gain, weights, tables, heads):
    rows, width = x.shape
    tile = 128
    columns = heads * (NOPE + ROPE)
    by_row = lambda n: pl.BlockSpec((tile, n), lambda i: (i, 0))
    whole = lambda a: pl.BlockSpec(a.shape, lambda i: (0, 0))
    return pl.pallas_call(
        functools.partial(project_kernel, heads),
        out_shape=(
            jax.ShapeDtypeStruct((rows, width), BF),
            jax.ShapeDtypeStruct((rows, columns), BF),
            jax.ShapeDtypeStruct((rows, R + 128), BF),
            jax.ShapeDtypeStruct((rows, R), F32),
            jax.ShapeDtypeStruct((rows, 1), F32),
            jax.ShapeDtypeStruct((rows, 1), F32),
        ),
        grid=(rows // tile,),
        in_specs=[by_row(width), whole(gain), whole(kv_gain), whole(weights)] + [by_row(128)] * 3,
        out_specs=[by_row(width), by_row(columns), by_row(R + 128), by_row(R), by_row(1), by_row(1)],
        compiler_params=pltpu.CompilerParams(vmem_limit_bytes=48 * MIB),
        cost_estimate=pl.CostEstimate(
            flops=2 * rows * width * weights.shape[1], bytes_accessed=20 * MIB, transcendentals=0
        ),
        name="project",
    )(x, gain, kv_gain, weights, *tables)


def head_key(kv_ref, rope_ref, k):
    rope = rope_ref[...]
    if k:
        rope = pltpu.roll(rope.astype(F32), ROPE, 1).astype(BF)
    return jnp.concatenate([kv_ref[:, k * HEAD : k * HEAD + NOPE], rope], 1)


def attend_kernel(scale, qn_ref, qr_ref, kv_ref, rope_ref, seg_q, seg_k, o_ref, l_ref):
    rows, keys = qn_ref.shape[0], kv_ref.shape[0]
    at_q = lax.axis_index("ctx") * rows + lax.broadcasted_iota(jnp.int32, (rows, keys), 0)
    at_k = lax.broadcasted_iota(jnp.int32, (rows, keys), 1)
    visible = (seg_q[...] == seg_k[...]) & (at_k <= at_q)
    for k in range(2):
        query = jnp.concatenate([qn_ref[:, k * NOPE : (k + 1) * NOPE], qr_ref[...]], 1)
        scores = jnp.where(visible, scale * mm_nt(query, head_key(kv_ref, rope_ref, k)), -1e30)
        peak = jnp.max(scores, -1, keepdims=True)
        weights = jnp.exp(scores - peak)
        total = jnp.sum(weights, -1, keepdims=True)
        values = kv_ref[:, k * HEAD + NOPE : (k + 1) * HEAD]
        o_ref[:, k * V : (k + 1) * V] = (mm(weights.astype(BF), values) * (1.0 / total)).astype(BF)
        l_ref[k] = peak + jnp.log(total)


def attend(query, expanded, rope, seg_q, seg_k, scale):
    rows, keys = query.shape[0], expanded.shape[0]
    heads = query.shape[1] // (NOPE + ROPE)
    return pl.pallas_call(
        functools.partial(attend_kernel, scale),
        out_shape=(
            jax.ShapeDtypeStruct((rows, heads * V), BF),
            jax.ShapeDtypeStruct((heads, rows, 1), F32),
        ),
        grid=(heads // 2,),
        in_specs=[
            pl.BlockSpec((rows, 2 * NOPE), lambda h: (0, h)),
            pl.BlockSpec((rows, 2 * ROPE), lambda h: (0, heads + h)),
            pl.BlockSpec((keys, 2 * HEAD), lambda h: (0, h)),
            pl.BlockSpec((keys, 128), lambda h: (0, R // 128)),
            pl.BlockSpec((rows, 1), lambda h: (0, 0)),
            pl.BlockSpec((1, keys), lambda h: (0, 0)),
        ],
        out_specs=[
            pl.BlockSpec((rows, 2 * V), lambda h: (0, h)),
            pl.BlockSpec((2, rows, 1), lambda h: (h, 0, 0)),
        ],
        compiler_params=pltpu.CompilerParams(vmem_limit_bytes=60 * MIB),
        cost_estimate=pl.CostEstimate(
            flops=2 * heads * rows * keys * 384, bytes_accessed=12 * MIB, transcendentals=heads * rows * keys
        ),
        name="attend",
    )(query, query, expanded, rope, seg_q, seg_k)


def attend_back_kernel(
    scale, qn_ref, qr_ref, kv_ref, rope_ref, g_ref, l_ref, seg_q, seg_k, expand_ref, cosine, first, second,
    dqn_ref, dqr_ref, dkv_ref, dl_ref, comp_acc, rope_acc,
):
    pair, last = pl.program_id(0), pl.num_programs(0) - 1
    rows, keys = qn_ref.shape[0], kv_ref.shape[0]
    at_k = lax.broadcasted_iota(jnp.int32, (keys, rows), 0)
    at_q = lax.axis_index("ctx") * rows + lax.broadcasted_iota(jnp.int32, (keys, rows), 1)
    visible = (seg_q[...] == seg_k[...]) & (at_k <= at_q)
    grad_ropes, grad_turned = [], None
    for k in range(2):
        key = head_key(kv_ref, rope_ref, k)
        query = jnp.concatenate([qn_ref[:, k * NOPE : (k + 1) * NOPE], qr_ref[...]], 1)
        grad = g_ref[:, k * V : (k + 1) * V]
        scores = scale * mm_nt(key, query)
        probs = jnp.exp(jnp.where(visible, scores, -1e30) - l_ref[k])
        grad_probs = mm_nt(kv_ref[:, k * HEAD + NOPE : (k + 1) * HEAD], grad)
        mean = jnp.sum(probs * grad_probs, 0, keepdims=True)
        grad_scores = (probs * (grad_probs - mean)).astype(BF)
        dkv_ref[:, k * HEAD + NOPE : (k + 1) * HEAD] = mm(probs.astype(BF), grad).astype(BF)
        grad_key = scale * mm(grad_scores, query)
        dkv_ref[:, k * HEAD : k * HEAD + NOPE] = grad_key[:, :NOPE].astype(BF)
        grad_ropes.append(grad_key[:, NOPE:])
        grad_query = scale * mm_tn(grad_scores, key)
        dqn_ref[:, k * NOPE : (k + 1) * NOPE] = grad_query[:, :NOPE].astype(BF)
        grad_turned = grad_query[:, NOPE:] if k == 0 else grad_turned + grad_query[:, NOPE:]
    dqr_ref[...] = turn(grad_turned, (cosine[...], -first[...], -second[...])).astype(BF)
    lane = lax.broadcasted_iota(jnp.int32, (keys, 128), 1)
    grad_rope = jnp.where(lane < ROPE, grad_ropes[0] + pltpu.roll(grad_ropes[1], ROPE, 1), 0.0)
    grad_comp = mm_nt(dkv_ref[...], expand_ref[...])

    @pl.when(pair == 0)
    def _():
        rope_acc[...] = grad_rope
        comp_acc[...] = grad_comp

    @pl.when(pair > 0)
    def _():
        rope_acc[...] += grad_rope
        comp_acc[...] += grad_comp

    @pl.when(pair == last)
    def _():
        dl_ref[:, :R] = comp_acc[...].astype(BF)
        dl_ref[:, R:] = rope_acc[...].astype(BF)


def attend_back(query, expanded, rope, grad, logs, seg_q, seg_k, expand, tables, scale):
    rows, keys = query.shape[0], expanded.shape[0]
    heads = query.shape[1] // (NOPE + ROPE)
    one = lambda shape: pl.BlockSpec(shape, lambda h: (0, 0))
    return pl.pallas_call(
        functools.partial(attend_back_kernel, scale),
        out_shape=(
            jax.ShapeDtypeStruct((rows, heads * NOPE), BF),
            jax.ShapeDtypeStruct((rows, heads * ROPE), BF),
            jax.ShapeDtypeStruct((keys, heads * (NOPE + V)), BF),
            jax.ShapeDtypeStruct((keys, R + 128), BF),
        ),
        grid=(heads // 2,),
        in_specs=[
            pl.BlockSpec((rows, 2 * NOPE), lambda h: (0, h)),
            pl.BlockSpec((rows, 2 * ROPE), lambda h: (0, heads + h)),
            pl.BlockSpec((keys, 2 * HEAD), lambda h: (0, h)),
            pl.BlockSpec((keys, 128), lambda h: (0, R // 128)),
            pl.BlockSpec((rows, 2 * V), lambda h: (0, h)),
            pl.BlockSpec((2, 1, rows), lambda h: (h, 0, 0)),
            one((1, rows)),
            one((keys, 1)),
            pl.BlockSpec((R, 2 * HEAD), lambda h: (0, h)),
        ]
        + [one((rows, 128))] * 3,
        out_specs=[
            pl.BlockSpec((rows, 2 * NOPE), lambda h: (0, h)),
            pl.BlockSpec((rows, 2 * ROPE), lambda h: (0, h)),
            pl.BlockSpec((keys, 2 * HEAD), lambda h: (0, h)),
            one((keys, R + 128)),
        ],
        scratch_shapes=[pltpu.VMEM((keys, R), F32), pltpu.VMEM((keys, 128), F32)],
        compiler_params=pltpu.CompilerParams(vmem_limit_bytes=60 * MIB),
        cost_estimate=pl.CostEstimate(
            flops=2 * heads * rows * keys * 1536, bytes_accessed=24 * MIB, transcendentals=heads * rows * keys
        ),
        name="attend_back",
    )(query, query, expanded, rope, grad, logs, seg_q, seg_k, expand, *tables)


def project_back_kernel(
    gn_ref, gr_ref, gl_ref, compressed_ref, kv_ref, gain, cosine, first, second, w_ref, sum_ref, grad_ref, gain_ref
):
    upstream = gl_ref[:, :R]
    compressed, inverse = compressed_ref[...], kv_ref[...]
    scaled = upstream * gain[...]
    mean = jnp.mean(scaled * compressed, -1, keepdims=True)
    grad = inverse * scaled - compressed * (inverse * inverse * inverse * mean)
    gains = jnp.sum(upstream * compressed * inverse, 0, keepdims=True)
    nope, rope = gn_ref.shape[1], gr_ref.shape[1]
    start = nope + rope
    grad_ref[:, :nope] = gn_ref[...]
    grad_ref[:, nope:start] = gr_ref[...]
    grad_ref[:, start : start + R] = grad.astype(BF)
    grad_ref[:, start + R :] = turn(gl_ref[:, R:], (cosine[...], -first[...], -second[...])).astype(BF)
    sum_ref[...] = mm_nt(grad_ref[...], w_ref[...]).astype(BF)

    @pl.when(pl.program_id(0) == 0)
    def _():
        gain_ref[...] = gains

    @pl.when(pl.program_id(0) > 0)
    def _():
        gain_ref[...] += gains


def project_back(grad_nope, grad_turned, grad_latent, compressed, inverse_kv, kv_gain, tables, weights):
    rows, columns = grad_nope.shape[0], weights.shape[1]
    width, tile = weights.shape[0], 128
    by_row = lambda n: pl.BlockSpec((tile, n), lambda i: (i, 0))
    whole = lambda a, **mode: pl.BlockSpec(a.shape, lambda i: (0, 0), **mode)
    return pl.pallas_call(
        project_back_kernel,
        out_shape=(
            jax.ShapeDtypeStruct((rows, width), BF),
            jax.ShapeDtypeStruct((rows, columns), BF),
            jax.ShapeDtypeStruct((1, R), F32),
        ),
        grid=(rows // tile,),
        in_specs=[
            by_row(grad_nope.shape[1]),
            by_row(grad_turned.shape[1]),
            by_row(R + 128),
            by_row(R),
            by_row(1),
            whole(kv_gain),
        ]
        + [by_row(128)] * 3
        + [whole(weights, pipeline_mode=pl.Buffered(1))],
        out_specs=[by_row(width), by_row(columns), pl.BlockSpec((1, R), lambda i: (0, 0))],
        compiler_params=pltpu.CompilerParams(vmem_limit_bytes=48 * MIB),
        cost_estimate=pl.CostEstimate(
            flops=2 * rows * width * columns, bytes_accessed=20 * MIB, transcendentals=0
        ),
        name="project_back",
    )(grad_nope, grad_turned, grad_latent, compressed, inverse_kv, kv_gain, *tables, weights)


TILE = 256


def pack_kernel(pair_tile, pair_block, pair_first, pair_on, rank, share, x_ref, o_ref, w_ref, *, weighted):
    i = pl.program_id(0)
    tokens = rank.shape[2]

    @pl.when(pair_on[i] == 1)
    def _():
        slot = pair_tile[i] * TILE + lax.broadcasted_iota(jnp.int32, (TILE, tokens), 0)
        chosen = rank[0] == slot
        rows = mm(chosen.astype(F32).astype(BF), x_ref[0])
        weight = jnp.sum(jnp.where(chosen, share[0], 0.0), 1, keepdims=True)
        if weighted:
            rows = rows * weight
        rows = rows.astype(BF)

        @pl.when(pair_first[i] == 1)
        def _():
            o_ref[...] = rows
            w_ref[...] = weight

        @pl.when(pair_first[i] == 0)
        def _():
            o_ref[...] += rows
            w_ref[...] += weight


def pack(pairs, rank, share, x, weighted):
    (blocks, _, tokens), width = rank.shape, x.shape[2]
    slots = blocks * tokens
    return pl.pallas_call(
        functools.partial(pack_kernel, weighted=weighted),
        out_shape=(
            jax.ShapeDtypeStruct((slots, width), BF),
            jax.ShapeDtypeStruct((slots, 1), F32),
        ),
        grid_spec=pltpu.PrefetchScalarGridSpec(
            num_scalar_prefetch=4,
            grid=(pairs["tile"].shape[0],),
            in_specs=[
                pl.BlockSpec((1, 1, tokens), lambda i, t, b, f, a: (b[i], 0, 0)),
                pl.BlockSpec((1, 1, tokens), lambda i, t, b, f, a: (b[i], 0, 0)),
                pl.BlockSpec((1, tokens, width), lambda i, t, b, f, a: (b[i], 0, 0)),
            ],
            out_specs=[
                pl.BlockSpec((TILE, width), lambda i, t, b, f, a: (t[i], 0)),
                pl.BlockSpec((TILE, 1), lambda i, t, b, f, a: (t[i], 0)),
            ],
        ),
        compiler_params=pltpu.CompilerParams(vmem_limit_bytes=40 * MIB),
        cost_estimate=pl.CostEstimate(
            flops=2 * 24 * TILE * tokens * width, bytes_accessed=28 * MIB, transcendentals=0
        ),
        name="pack",
    )(pairs["tile"], pairs["block"], pairs["first_tile"], pairs["on"], rank, share, x)


def expert_kernel(parts, tiles, x_ref, g_ref, w_ref, *refs):
    given, (out_ref, gin_ref, hid, gg, gu, gate, up, down, sem) = refs[: 3 * parts], refs[3 * parts :]
    size, room = given[0].shape[0], gate.shape[0] // parts

    @pl.when(pl.program_id(0) == 0)
    def _():
        copies = [
            pltpu.make_async_copy(given[k * parts + p], held.at[pl.ds(p * room, size)], sem.at[k, p])
            for k, held in enumerate((gate, up, down))
            for p in range(parts)
        ]
        for copy in copies:
            copy.start()
        if room > size:
            for held in (gate, up, down):
                for p in range(parts):
                    held[pl.ds(p * room + size, room - size), :] = jnp.zeros((room - size, held.shape[1]), BF)
        for copy in copies:
            copy.wait()

    @pl.when(pl.program_id(0) < tiles[0])
    def _():
        x, g = x_ref[...], g_ref[...]
        a = mm_nt(x, gate[...])
        b = mm_nt(x, up[...])
        grad_hidden = mm_nt(g, down[...])
        sig = jax.nn.sigmoid(a)
        act = a * sig
        hidden = (act * b).astype(BF)
        hid[...] = hidden
        out_ref[...] = (mm(hidden, down[...]) * w_ref[...]).astype(BF)
        grad_gate = (grad_hidden * b * (sig * (1.0 + a * (1.0 - sig)))).astype(BF)
        grad_up = (grad_hidden * act).astype(BF)
        gg[...] = grad_gate
        gu[...] = grad_up
        gin_ref[...] = (mm(grad_gate, gate[...]) + mm(grad_up, up[...])).astype(BF)


def experts(tiles, x, g, w, gates, ups, downs):
    slots, width = x.shape
    parts, hidden = len(gates), gates[0].shape[0]
    room = -(-hidden // 128) * 128
    row = lambda i, t: (jnp.minimum(i, t[0] - 1), 0)
    anywhere = pl.BlockSpec(memory_space=pl.ANY)
    return pl.pallas_call(
        functools.partial(expert_kernel, parts),
        out_shape=(jax.ShapeDtypeStruct((slots, width), BF),) * 2
        + (jax.ShapeDtypeStruct((slots, parts * room), BF),) * 3,
        grid_spec=pltpu.PrefetchScalarGridSpec(
            num_scalar_prefetch=1,
            grid=(slots // TILE,),
            in_specs=[
                pl.BlockSpec((TILE, width), row),
                pl.BlockSpec((TILE, width), row),
                pl.BlockSpec((TILE, 1), row),
            ]
            + [anywhere] * (3 * parts),
            out_specs=[pl.BlockSpec((TILE, width), row)] * 2
            + [pl.BlockSpec((TILE, parts * room), row)] * 3,
            scratch_shapes=[pltpu.VMEM((parts * room, width), BF)] * 3 + [pltpu.SemaphoreType.DMA((3, parts))],
        ),
        compiler_params=pltpu.CompilerParams(vmem_limit_bytes=60 * MIB),
        cost_estimate=pl.CostEstimate(
            flops=12 * 2560 * width * parts * hidden, bytes_accessed=100 * MIB, transcendentals=0
        ),
        name="experts",
    )(tiles, x, g, w, *gates, *ups, *downs)


def expert_sums(tiles, x_ref, g_ref, hid_ref, gg_ref, gu_ref, sums):
    @pl.when(pl.program_id(0) < tiles[0])
    def _():
        x, g = x_ref[...], g_ref[...]
        size = sums[0].shape[0]
        sums[0][...] += mm_tn(gg_ref[:, :size], x)
        sums[1][...] += mm_tn(gu_ref[:, :size], x)
        sums[2][...] += mm_tn(hid_ref[:, :size], g)


def expert_sums_kernel(tiles, x_ref, g_ref, hid_ref, gg_ref, gu_ref, *refs):
    outs, sums = refs[:3], refs[3:]

    @pl.when(pl.program_id(0) == 0)
    def _():
        for total in sums:
            total[...] = jnp.zeros_like(total)

    expert_sums(tiles, x_ref, g_ref, hid_ref, gg_ref, gu_ref, sums)

    @pl.when(pl.program_id(0) == pl.num_programs(0) - 1)
    def _():
        for out, total in zip(outs, sums):
            out[...] = total[...].astype(out.dtype)


def expert_totals_kernel(tiles, x_ref, g_ref, hid_ref, gg_ref, gu_ref, *refs):
    starts, outs = refs[:3], refs[3:]

    @pl.when(pl.program_id(0) == 0)
    def _():
        for out, start in zip(outs, starts):
            out[...] = start[...].astype(F32)

    expert_sums(tiles, x_ref, g_ref, hid_ref, gg_ref, gu_ref, outs)


def expert_grads(tiles, x, g, hid, gg, gu, part, hidden, starts=None):
    slots, width = x.shape
    room = -(-hidden // 128) * 128
    row = lambda i, t: (jnp.minimum(i, t[0] - 1), 0)
    column = lambda i, t: (jnp.minimum(i, t[0] - 1), part)
    whole = lambda i, t: (0, 0)
    once = pl.Buffered(1)
    kernel = expert_sums_kernel if starts is None else expert_totals_kernel
    held = [pl.BlockSpec((hidden, width), whole, pipeline_mode=once)] * 3
    return pl.pallas_call(
        kernel,
        out_shape=(jax.ShapeDtypeStruct((hidden, width), BF if starts is None else F32),) * 3,
        grid_spec=pltpu.PrefetchScalarGridSpec(
            num_scalar_prefetch=1,
            grid=(slots // TILE,),
            in_specs=[pl.BlockSpec((TILE, width), row)] * 2
            + [pl.BlockSpec((TILE, room), column)] * 3
            + (held if starts is not None else []),
            out_specs=held,
            scratch_shapes=[pltpu.VMEM((hidden, width), F32)] * 3 if starts is None else [],
        ),
        compiler_params=pltpu.CompilerParams(vmem_limit_bytes=60 * MIB),
        cost_estimate=pl.CostEstimate(
            flops=6 * 2560 * width * hidden, bytes_accessed=40 * MIB, transcendentals=0
        ),
        name="expert_grads",
    )(tiles, x, g, hid, gg, gu, *(starts or ()))


def dense_kernel(
    pair_tile, pair_block, pair_first, pair_last, pair_real, rank, x_ref, c_ref, out_ref, gin_ref, total_ref, grad_ref, acc, gacc
):
    i = pl.program_id(0)

    @pl.when(pair_first[i] == 1)
    def _():
        acc[...] = x_ref[0].astype(F32)
        gacc[...] = c_ref[0].astype(F32)

    @pl.when(pair_real[i] == 1)
    def _():
        tokens = rank.shape[1]
        slot = pair_tile[i] * TILE + lax.broadcasted_iota(jnp.int32, (tokens, TILE), 1)
        chosen = (rank[0] == slot).astype(F32).astype(BF)
        acc[...] += mm(chosen, out_ref[...])
        gacc[...] += mm(chosen, gin_ref[...])

    @pl.when(pair_last[i] == 1)
    def _():
        total_ref[0] = acc[...].astype(BF)
        grad_ref[0] = gacc[...].astype(BF)


def dense(pairs, rank_column, shared_out, shared_gin, out, gin):
    blocks, tokens, width = shared_out.shape
    by_block = lambda i, t, b, f, l, r: (b[i], 0, 0)
    by_tile = lambda i, t, b, f, l, r: (t[i], 0)
    return pl.pallas_call(
        dense_kernel,
        out_shape=(jax.ShapeDtypeStruct((blocks, tokens, width), BF),) * 2,
        grid_spec=pltpu.PrefetchScalarGridSpec(
            num_scalar_prefetch=5,
            grid=(pairs["tile"].shape[0],),
            in_specs=[
                pl.BlockSpec((1, tokens, 1), by_block),
                pl.BlockSpec((1, tokens, width), by_block),
                pl.BlockSpec((1, tokens, width), by_block),
                pl.BlockSpec((TILE, width), by_tile),
                pl.BlockSpec((TILE, width), by_tile),
            ],
            out_specs=[pl.BlockSpec((1, tokens, width), by_block)] * 2,
            scratch_shapes=[pltpu.VMEM((tokens, width), F32)] * 2,
        ),
        compiler_params=pltpu.CompilerParams(vmem_limit_bytes=60 * MIB),
        cost_estimate=pl.CostEstimate(
            flops=4 * 26 * TILE * tokens * width, bytes_accessed=90 * MIB, transcendentals=0
        ),
        name="dense",
    )(
        pairs["tile"], pairs["block"], pairs["first_block"], pairs["last_block"], pairs["real"],
        rank_column, shared_out, shared_gin, out, gin,
    )


def routing(share):
    blocks, tokens = share.shape
    used = (share > 0).astype(F32)
    upper = (jnp.arange(tokens)[:, None] <= jnp.arange(tokens)[None, :]).astype(BF)
    inside = mm(used.astype(BF), upper).astype(jnp.int32)
    counts = inside[:, -1]
    lower = jnp.arange(blocks)[:, None] > jnp.arange(blocks)[None, :]
    start = jnp.sum(jnp.where(lower, counts[None, :], 0), 1)
    end = start + counts
    rank = jnp.where(share > 0, start[:, None] + inside - 1, -1)
    last_tile = blocks * tokens // TILE - 1
    first = jnp.minimum(start // TILE, last_tile)
    last = jnp.where(counts > 0, (end - 1) // TILE, first)
    spans = last - first + 1
    after = jnp.sum(jnp.where(lower | jnp.eye(blocks, dtype=bool), spans[None, :], 0), 1)
    size = blocks + blocks * tokens // TILE
    turn = jnp.arange(size)
    all_pairs = after[-1]
    on = turn < all_pairs
    place = jnp.minimum(turn, all_pairs - 1)
    block = jnp.sum((after[None, :] <= place[:, None]).astype(jnp.int32), 1)
    pick = block[:, None] == jnp.arange(blocks)[None, :]
    take = lambda v: jnp.sum(jnp.where(pick, v[None, :], 0), 1)
    tile = take(first) + place - take(after - spans)
    shifted = lambda v: jnp.concatenate([jnp.full((1,), -1, v.dtype), v[:-1]])
    as_int = lambda v: v.astype(jnp.int32)
    pairs = {
        "tile": as_int(tile),
        "block": as_int(block),
        "on": as_int(on),
        "real": as_int(on & (take(counts) > 0)),
        "first_tile": as_int(on & (shifted(tile) != tile)),
        "first_block": as_int(on & (shifted(block) != block)),
        "last_block": as_int(on & (place == take(after) - 1)),
    }
    tiles = as_int(jnp.maximum((end[-1] + TILE - 1) // TILE, 1))[None]
    return rank.astype(jnp.int32), pairs, tiles


def other_half_sum(rows, product, beside):
    parts, me = lax.axis_size("tp"), lax.axis_index("tp")
    size = rows.shape[0] // parts
    if parts != 2:
        summed = lax.psum_scatter(product(rows).astype(BF), "tp", scatter_dimension=0, tiled=True)
        return summed.astype(F32), beside
    sent = product(lax.dynamic_slice_in_dim(rows, (1 - me) * size, size)).astype(BF)
    came, beside = lax.optimization_barrier((lax.ppermute(sent, "tp", [(0, 1), (1, 0)]), beside))
    return product(lax.dynamic_slice_in_dim(rows, me * size, size)) + came.astype(F32), beside


def swap_tp(v):
    return lax.ppermute(v, "tp", [(0, 1), (1, 0)])


def join_tp(v, came=None):
    if lax.axis_size("tp") != 2:
        return lax.all_gather(v, "tp", axis=0, tiled=True)
    came = swap_tp(v) if came is None else came
    return jnp.where(lax.axis_index("tp") == 0, jnp.stack([v, came]), jnp.stack([came, v])).reshape(
        (2 * v.shape[0],) + v.shape[1:]
    )


def on_device(
    inputs,
    segments,
    routes,
    gate_share,
    cotangent,
    attn_gain,
    kv_gain,
    ffn_gain,
    w_query,
    w_latent,
    w_expand,
    w_output,
    w_shared_gate,
    w_shared_up,
    w_shared_down,
    expert_gate,
    expert_up,
    expert_down,
):
    tokens, width = inputs.shape
    parts, part = lax.axis_size("tp"), lax.axis_index("tp")
    half = tokens // parts
    group = lax.axis_size(GROUP)
    me = lax.axis_index(GROUP)
    ctx = lax.axis_size("ctx")
    query_width = w_query.shape[1]
    heads = query_width // (NOPE + ROPE)
    scale = (NOPE + ROPE) ** (-0.5)
    own_half = lambda v: lax.dynamic_slice_in_dim(v, part * half, half)

    gain_row = jnp.concatenate([attn_gain, kv_gain, ffn_gain])
    n_attn, n_kv = attn_gain.shape[0], kv_gain.shape[0]
    gain_rows = jnp.zeros((16, 384), BF).at[0, : gain_row.shape[0]].set(gain_row)
    by_head = w_query.reshape(-1, heads, NOPE + ROPE)
    first_weights = jnp.concatenate(
        [
            by_head[..., :NOPE].reshape(-1, heads * NOPE),
            by_head[..., NOPE:].reshape(-1, heads * ROPE),
            w_latent,
            jnp.zeros((w_latent.shape[0], 128 - ROPE), BF),
        ],
        1,
    )
    expert_ids = jnp.arange(group, dtype=jnp.int32)
    shares = jnp.sum(
        jnp.where(own_half(routes).T[None] == expert_ids[:, None, None], own_half(gate_share).T[None], 0.0), 1
    )
    gate, up, down = (jnp.swapaxes(expert_gate[0], 0, 1), jnp.swapaxes(expert_up[0], 0, 1), expert_down[0])
    together = lax.optimization_barrier
    piece = w_shared_gate.shape[1] // group
    depth = w_shared_gate.shape[0]
    cut = lambda v: v.reshape(group, piece, depth)
    shared_sent = jnp.concatenate(
        [cut(jnp.swapaxes(w_shared_gate, 0, 1)), cut(jnp.swapaxes(w_shared_up, 0, 1)), cut(w_shared_down)], 1
    )
    first = ring_gather(
        [
            first_weights,
            jnp.swapaxes(w_output, 0, 1),
            w_expand,
            gain_rows,
            shares,
            jnp.broadcast_to(segments[None], (16, tokens)),
        ],
        1,
        swaps=[gate] if parts == 2 else [],
    )
    first_full, output_full, expand_full, gains, share, all_segments = first[:6]
    expand_full = expand_full.reshape(R, -1)
    output_full = output_full.reshape(width, -1)
    attn_scale = gains[:, 0, :n_attn].reshape(-1).astype(F32)
    kv_scale = gains[:, 0, n_attn : n_attn + n_kv].reshape(-1).astype(F32)
    ffn_scale = gains[:, 0, n_attn + n_kv : gain_row.shape[0]].reshape(-1).astype(F32)
    first_full = first_full.reshape(width, -1)
    all_segments = lax.dynamic_slice_in_dim(
        all_segments[:, 0], lax.axis_index("shard") * ctx, ctx
    ).reshape(-1)
    share = lax.dynamic_index_in_dim(share, me, 1, keepdims=False)
    rank, pairs, tiles = routing(share)

    cot_half = jnp.concatenate([own_half(cotangent), jnp.zeros((8, width), BF)], 0)
    cot_all = lax.all_gather(together((cot_half, gains))[0], GROUP, axis=0, tiled=False)
    if parts == 2:
        up_other = swap_tp(together((up, gains))[0])

    residual = inputs.astype(F32)
    start = lax.axis_index("ctx") * tokens
    tables = turn_tables(start + jnp.arange(tokens, dtype=jnp.int32))
    attn_low, query_low, latent_low, compressed, inverse_one, inverse_kv = project(
        inputs, attn_scale[None], kv_scale[None], first_full, tables, heads
    )
    all_latent, shared_own = ctx_gather(latent_low, shared_sent, 5)
    all_latent = all_latent.reshape(ctx * tokens, -1)
    shared_own = jnp.swapaxes(shared_own, 0, 1).reshape(3 * piece, width)
    expanded = mm(all_latent[:, :R], expand_full).astype(BF)
    if parts == 2:
        expanded, shared_own, up_other = together((expanded, shared_own, up_other))
        shared_parts = [shared_own, swap_tp(shared_own)]
    else:
        shared_parts = list(lax.all_gather(shared_own, "tp", axis=0, tiled=False))
    attended, logs = attend(query_low, expanded, all_latent, segments[:, None], all_segments[None, :], scale)
    attended, shared_parts = together((attended, shared_parts))
    shared = [
        jnp.concatenate([v[k * piece : (k + 1) * piece] for v in shared_parts], 0) for k in range(3)
    ]
    rank_row, share_row = rank[:, None, :], share[:, None, :]
    packed_grads = pack(pairs, rank_row, share_row, cot_all, True)
    attended_sum, (grad_rows, weights) = other_half_sum(
        attended, lambda rows: mm_nt(rows, output_full), packed_grads
    )
    middle = own_half(residual) + attended_sum
    normed_two, inverse_two = norm_forward(middle, ffn_scale)
    ffn_low = normed_two.astype(BF)

    if parts == 2:
        rows_all, shared_out, shared_gin, *shared_grads, down_other = gather_shared(
            ffn_low, cot_all, shared, 2, swaps=[down]
        )
        gates, ups, downs = [gate, first[6]], [up, up_other], [down, down_other]
    else:
        rows_all, shared_out, shared_gin, *shared_grads = gather_shared(ffn_low, cot_all, shared, 2)
        gates, ups, downs = (list(lax.all_gather(v, "tp", axis=0, tiled=False)) for v in (gate, up, down))
    rows_in, _ = pack(pairs, rank_row, share_row, rows_all, False)

    shared_back = [
        jnp.concatenate([v[k * piece : (k + 1) * piece] for v in shared_grads], 0) for k in range(parts)
    ]
    if parts == 2:
        shared_came = swap_tp(shared_back[1].astype(BF))
        rows_in, shared_came = together((rows_in, shared_came))
        shared_back = shared_back[0] + shared_came.astype(F32)
    else:
        shared_back = lax.psum_scatter(jnp.stack(shared_back).astype(BF), "tp", scatter_dimension=0, tiled=False)
    shared_back = lax.all_gather(shared_back.astype(BF), GROUP, axis=0, tiled=False)
    expert_out, expert_gin, *kept = experts(tiles, rows_in, grad_rows, weights, gates, ups, downs)

    grads_of = lambda which, *starts: expert_grads(
        tiles, rows_in, grad_rows, *kept, which, gate.shape[0], *starts
    )
    if parts == 2:
        expert_out, sent = together((expert_out, grads_of(1)))
        came = [swap_tp(v) for v in sent]
    moe_part, grad_part = dense(
        pairs, rank[:, :, None], shared_out, shared_gin, expert_out, expert_gin
    )
    grad_part, shared_back = together((grad_part, shared_back))
    shared_back = lax.dynamic_slice_in_dim(shared_back, me * depth, depth, 2)
    (grad_normed_two,) = ring_scatter([grad_part], 3)
    if parts == 2:
        grad_normed_two, came = together((grad_normed_two, came))
    if parts != 2:
        sent = [grads_of(k) for k in range(parts)]
        own_grads = [
            lax.psum_scatter(jnp.stack(v), "tp", scatter_dimension=0, tiled=False).astype(F32) for v in zip(*sent)
        ]

    grad_out = own_half(cotangent).astype(F32)
    grad_mid_norm, ffn_gain_grad = norm_backward(middle, inverse_two, ffn_scale, grad_normed_two)
    grad_middle = grad_out + grad_mid_norm
    grad_middle_low = join_tp(grad_middle.astype(BF))
    moe_part = lax.optimization_barrier((moe_part, grad_normed_two))[0]
    moe_total = lax.psum_scatter(
        moe_part, GROUP, scatter_dimension=0, tiled=False
    )

    grad_attended = mm(grad_middle_low, output_full).astype(BF)
    grad_nope, grad_turned, grad_kv, grad_latent = attend_back(
        query_low, expanded, all_latent, grad_attended, jnp.swapaxes(logs, 1, 2),
        segments[None, :], all_segments[:, None], expand_full, tables, scale,
    )
    grad_latent = ctx_scatter(grad_latent.reshape(ctx, tokens, -1), 6)
    grad_normed_one, grad_first, kv_gain_grad = project_back(
        grad_nope, grad_turned, grad_latent, compressed, inverse_kv, kv_scale[None], tables, first_full
    )
    if parts == 2:
        grad_normed_came = swap_tp(lax.dynamic_slice_in_dim(grad_normed_one, (1 - part) * half, half))
        (grad_middle_low, attended, all_latent, grad_kv, came), grad_normed_one = together(
            ((grad_middle_low, attended, all_latent, grad_kv, came), grad_normed_one)
        )
        own_grads, grad_normed_came = together((grads_of(0, tuple(came)), grad_normed_came))
        grad_normed_one = own_half(grad_normed_one).astype(F32) + grad_normed_came.astype(F32)
    else:
        grad_normed_one = lax.psum_scatter(grad_normed_one, "tp", scatter_dimension=0, tiled=True).astype(F32)
    gate_grad, up_grad, down_grad = (
        jnp.swapaxes(own_grads[0], 0, 1)[None], jnp.swapaxes(own_grads[1], 0, 1)[None], own_grads[2][None]
    )
    first_grad = mm_tn(attn_low, grad_first).astype(BF)
    output_grad = mm_tn(grad_middle_low, attended).astype(BF)
    expand_grad = mm_tn(all_latent[:, :R], grad_kv).astype(BF)
    grad_in_norm, attn_gain_grad = norm_backward(
        own_half(residual), own_half(inverse_one), attn_scale, grad_normed_one
    )
    grad_inputs = (grad_middle + grad_in_norm).astype(BF)

    gain_grads = jnp.concatenate(
        [v.reshape(group, -1) for v in (attn_gain_grad, kv_gain_grad[0], ffn_gain_grad)], 1
    ).astype(BF)
    tail = jnp.zeros((group, 16, 384), BF).at[:, 0, : gain_grads.shape[1]].set(gain_grads)
    moe_total, tail = together((moe_total, tail))
    result = (middle + moe_total.astype(F32)).astype(BF)
    first_own, output_own, expand_own, gains_own, *came = ring_scatter(
        [
            first_grad.reshape(group, -1, first_grad.shape[1]),
            output_grad.reshape(group, -1, output_grad.shape[1]),
            expand_grad.reshape(group, -1, expand_grad.shape[1]),
            tail,
        ],
        4,
        pieces=2,
        swaps=[grad_inputs, result] if parts == 2 else [],
    )
    grad_inputs, result = join_tp(grad_inputs, *came[:1]), join_tp(result, *came[1:])
    output_own = jnp.swapaxes(output_own, 0, 1)
    back = [shared_back[:, k * piece : (k + 1) * piece].reshape(-1, depth).astype(F32) for k in range(3)]
    sgate_grad, sup_grad, sdown_grad = jnp.swapaxes(back[0], 0, 1), jnp.swapaxes(back[1], 0, 1), back[2]
    nopes = first_own[:, : heads * NOPE].reshape(-1, heads, NOPE)
    query_own = jnp.concatenate([nopes, first_own[:, heads * NOPE : query_width].reshape(-1, heads, ROPE)], -1)
    query_own = query_own.reshape(-1, query_width)
    latent_own = first_own[:, query_width : query_width + R + ROPE]
    if parts == 2:
        small = jnp.concatenate([latent_own.reshape(-1, 128), gains_own[:8].reshape(-1, 128)], 0)
        small = small + swap_tp(small)
        latent_own = small[: -gains_own[:8].size // 128].reshape(latent_own.shape)
        gains_own = small[-gains_own[:8].size // 128 :].reshape(8, -1)[0]
    else:
        latent_own, gains_own = lax.psum((latent_own, gains_own[0]), "tp")
    return (
        result,
        grad_inputs.astype(F32),
        gains_own[:n_attn],
        gains_own[n_attn : n_attn + n_kv],
        gains_own[n_attn + n_kv : gain_row.shape[0]],
        query_own,
        latent_own,
        expand_own,
        output_own,
        sgate_grad,
        sup_grad,
        sdown_grad,
        gate_grad,
        up_grad,
        down_grad,
    )


def solution(mesh):
    group = P(GROUP)
    rows = P(GROUP, None)
    both = P(GROUP, "tp")
    turned = P("tp", GROUP)
    return jax.shard_map(
        on_device,
        mesh=mesh,
        in_specs=(
            rows, group, rows, rows, rows, group, group, group,
            both, rows, both, turned, both, both, turned,
            P(GROUP, None, "tp"), P(GROUP, None, "tp"), P(GROUP, "tp", None),
        ),
        out_specs=(
            rows, rows, group, group, group,
            both, rows, both, turned, both, both, turned,
            P(GROUP, None, "tp"), P(GROUP, None, "tp"), P(GROUP, "tp", None),
        ),
        check_vma=False,
    )
```
